128 devices in a mesh: cells: 8 (over x, core), tgt: 16 (over z, y).
Axes of the slice: x: 4, y: 4, z: 4, core: 2. Of those that a mesh axis runs over, the one named last changes fastest.
Arguments:
- placement_a: int32 [128], replicated, may hold values from 0 to 127, as said below
- members_b: int32 [128, 4], replicated, may hold values from 0 to 511, as said below
- source_mass: float32 [128, 256], P('cells'), may hold values from 0.5 to 2
- init_log: float32 [128, 4, 2048], P('cells', None, 'tgt'), may hold values from -4 to 4
Outputs:
- marginals: float32 [128, 4, 2048], P('cells', None, 'tgt')
The draws below stay inside these ranges and needn't reach their ends.
Inputs may be any that keep to these rules, and one draw needn't show every extreme that they name: `placement_a`: each cell number appears once. `members_b`: each basic cell appears once. Slots 16 * i to 16 * (i + 1) - 1 belong to index i of cells in both partitions; of the basic cells in the A slots of one index, at most 12 lie in the B slots of any one index, and exactly 12 for some pairs of indices.
All inputs are finite; a program needn't handle non-finite values.
Results may differ from the reference program's by a relative error of at most 0.00028.
Values sent between devices are 32-bit elements; how exact they have to be, the bound alone decides.
No kernel may reach another device: no remote copies, remote signals or barrier semaphores. Data moves between devices by JAX's collectives and lax.ppermute only.
A program may use at most 64 MiB of HBM per device.

```python
import math
import jax
import jax.numpy as jnp
from jax import lax

W = 2048
SIDE = 8
ITERS = 4
SWEEPS = 4
CELL_DEV = 16
ROWS = 256
CELLS = 128
BASIC = 512
MOST = 12
N_CELLS = 8


def route_tables(key):
    owners = N_CELLS
    per_device = 4 * CELL_DEV
    limit = MOST
    first_shift = jax.random.randint(jax.random.fold_in(key, 11), (), 0, owners).astype(jnp.int32)
    spread = jax.random.permutation(jax.random.fold_in(key, 12), per_device - limit).astype(jnp.int32)
    rest_shift = (first_shift + 1 + spread % (owners - 1)) % owners
    base_shift = jnp.concatenate([jnp.full((limit,), first_shift, jnp.int32), rest_shift.astype(jnp.int32)])
    offsets = base_shift[jax.random.permutation(jax.random.fold_in(key, 13), per_device)]
    owner_ids = jnp.arange(owners, dtype=jnp.int32)
    sender_keys = jax.vmap(lambda number: jax.random.fold_in(jax.random.fold_in(key, 14), number))(owner_ids)
    receiver_keys = jax.vmap(lambda number: jax.random.fold_in(jax.random.fold_in(key, 15), number))(owner_ids)
    labels = jax.vmap(lambda owner_key: jax.random.permutation(owner_key, per_device))(sender_keys).astype(jnp.int32)
    receiver_perm = jax.vmap(lambda owner_key: jax.random.permutation(owner_key, per_device))(receiver_keys).astype(jnp.int32)
    dest_owner = (owner_ids[:, None] + offsets[labels]) % owners
    dest_slot = receiver_perm[dest_owner, labels]
    destination = (dest_owner * per_device + dest_slot).reshape(-1).astype(jnp.int32)
    order_a = jax.random.permutation(jax.random.fold_in(key, 16), CELLS).astype(jnp.int32)
    positions = jnp.arange(BASIC, dtype=jnp.int32)
    ids_a = 4 * order_a[positions // 4] + positions % 4
    members = jnp.zeros((BASIC,), jnp.int32).at[destination].set(ids_a)
    return (order_a, members.reshape(CELLS, 4))


def draw_placement_a(key, part):
    return route_tables(key)[0]


def draw_members_b(key, part):
    return route_tables(key)[1]


def levels(key, extent, cuts, smallest, largest):
    def one(dim, shards_of):
        heights = jax.random.uniform(jax.random.fold_in(jax.random.fold_in(key, 6), dim), (shards_of,), jnp.float32, smallest / len(cuts), largest / len(cuts))
        return jnp.repeat(jnp.exp(heights), extent[dim] // shards_of).reshape((-1,) + (1,) * (len(extent) - dim - 1))

    factor_of = one(*cuts[0])
    for cut in cuts[1:]:
        factor_of = factor_of * one(*cut)
    return factor_of


def centred(rng, dims, deviation, most, split=(), kind=jnp.bfloat16):
    array = jax.random.normal(rng, dims, jnp.float32) * deviation
    if len(split) > 0:
        array = levels(rng, dims, split, -0.22, 0.18) * array
    return jnp.clip(array, min=-most, max=most).astype(kind)


def setup_inputs(seed: int = 0) -> dict:
    splits = jax.random.split(jax.random.key(seed), 5)
    return {
        "placement_a": draw_placement_a(jax.random.fold_in(splits[4], 71), 0),
        "members_b": draw_members_b(jax.random.fold_in(splits[4], 71), 0),
        "source_mass": jnp.clip(jnp.exp(math.log(2.0) - 1.3862944 * jax.random.uniform(splits[2], (CELLS, ROWS), jnp.float32) ** levels(splits[2], (CELLS, ROWS), ((0, 8),), -0.2, 0.2)), 0.5, 2.0),
        "init_log": centred(splits[3], (CELLS, 4, W), 1.0, 4.0, ((0, 8), (2, 16)), jnp.float32),
    }


inverse_eps = 200.0
block_cols = 32
grid_cols = 64


def log_sum(values, axis_number):
    top_score = jnp.max(values, axis=axis_number, keepdims=True)
    exp_sum = jnp.sum(jnp.exp(values - top_score), axis=axis_number, keepdims=True)
    return jnp.squeeze(top_score + jnp.log(exp_sum), axis=axis_number)


def basic_coords(basic_ids, side_px, block_rows):
    pixels = jnp.arange(side_px * side_px, dtype=jnp.int32)
    height = ((basic_ids[:, None] // block_cols) * side_px + pixels[None, :] // side_px).astype(jnp.float32) + 0.5
    across = ((basic_ids[:, None] % block_cols) * side_px + pixels[None, :] % side_px).astype(jnp.float32) + 0.5
    return height / float(block_rows * side_px), across / float(block_cols * side_px)


def target_coords(start, count, width):
    column = start + jnp.arange(count, dtype=jnp.int32)
    height = (column // grid_cols).astype(jnp.float32) + 0.5
    across = (column % grid_cols).astype(jnp.float32) + 0.5
    return height / float(width // grid_cols), across / float(grid_cols)


def kernel_cost(row_height, row_across, col_height, col_across):
    return ((row_height[:, None] - col_height[None, :]) ** 2 + (row_across[:, None] - col_across[None, :]) ** 2) * inverse_eps


def sweep_cells(basic_ids, log_mass, log_marg, block_rows, col_height, col_across):
    row_count = 4 * SIDE * SIDE
    height, across = basic_coords(basic_ids, SIDE, block_rows)
    height = height.reshape(CELLS // 8, 8, row_count)
    across = across.reshape(CELLS // 8, 8, row_count)
    log_source = log_mass.reshape(CELLS // 8, 8, row_count)
    log_target = log_sum(log_marg.reshape(CELLS, 4, W), 1).reshape(CELLS // 8, 8, W)

    def one_cell(cell_height, cell_across, cell_source, cell_target):
        kernel = kernel_cost(cell_height, cell_across, col_height, col_across)
        dual_col = jnp.zeros((W,), jnp.float32)
        dual_row = cell_source
        for iteration in range(ITERS):
            dual_row = cell_source - log_sum(dual_col[None, :] - kernel, 1)
            dual_col = cell_target - log_sum(dual_row[:, None] - kernel, 0)
        joined = (dual_row[:, None] + dual_col[None, :] - kernel).reshape(4, SIDE * SIDE, W)
        return log_sum(joined, 1)

    def one_group(group_data):
        return jax.vmap(one_cell)(group_data[0], group_data[1], group_data[2], group_data[3])

    result = lax.map(one_group, (height, across, log_source, log_target))
    return result.reshape(4 * CELLS, W)


def reference(placement_a, members_b, source_mass, init_log):
    basic_count = 4 * CELLS
    block_rows = basic_count // block_cols
    positions = jnp.arange(basic_count, dtype=jnp.int32)
    ids_a = (4 * placement_a[:, None] + jnp.arange(4, dtype=jnp.int32)[None, :]).reshape(-1).astype(jnp.int32)
    ids_b = members_b.reshape(-1).astype(jnp.int32)
    where_a = jnp.zeros((basic_count,), jnp.int32).at[ids_a].set(positions)
    where_b = jnp.zeros((basic_count,), jnp.int32).at[ids_b].set(positions)
    a_to_b = where_b[ids_a]
    b_to_a = where_a[ids_b]
    mass_a = jnp.log(source_mass.reshape(basic_count, SIDE * SIDE))
    mass_b = mass_a[b_to_a]
    col_height, col_across = target_coords(0, W, W)
    log_marg = init_log.reshape(basic_count, W) + math.log(SIDE * SIDE / W)
    for sweep_index in range(SWEEPS):
        if sweep_index % 2 == 0:
            log_marg = sweep_cells(ids_a, mass_a, log_marg, block_rows, col_height, col_across)
            log_marg = log_marg[b_to_a]
        else:
            log_marg = sweep_cells(ids_b, mass_b, log_marg, block_rows, col_height, col_across)
            log_marg = log_marg[a_to_b]
    return jnp.exp(log_marg).reshape(CELLS, 4, W)
```

```python
import numpy as np
import ml_dtypes

import jax
import jax.numpy as jnp
from jax import lax
from jax.experimental import pallas as pl
from jax.experimental.pallas import tpu as pltpu
from jax.sharding import Mesh, PartitionSpec as P

F32 = jnp.float32
BF16 = jnp.bfloat16
W = 2048
NT = (((1,), (1,)), ((), ()))
CENTRE = 95


def _halves(matrix):
    high = matrix.astype(ml_dtypes.bfloat16)
    low = (matrix - high.astype(np.float64)).astype(ml_dtypes.bfloat16)
    return np.concatenate([high, low], axis=1)


def _tables():
    j = np.arange(W)
    yh = (j // 64 + 0.5) / 32 - 0.5
    ya = (j % 64 + 0.5) / 64 - 0.5
    r = np.arange(64)
    dh = (r // 8 - 3.5) / 128
    da = (r % 8 - 3.5) / 256
    basic = np.exp(400.0 * (yh[:, None] * dh[None] + ya[:, None] * da[None]))
    cell_da = np.concatenate([da + (k - 1.5) / 32 for k in range(4)])
    cell_dh = np.concatenate([dh] * 4)
    cell = np.exp(400.0 * (yh[:, None] * cell_dh[None] + ya[:, None] * cell_da[None]))
    return _halves(cell), _halves(basic)


def dot(a, b):
    return jnp.dot(a, b, preferred_element_type=F32)


def dot_nt(a, b):
    return lax.dot_general(a, b, NT, preferred_element_type=F32)


def split2(x):
    high = x.astype(BF16)
    return high, (x - high.astype(F32)).astype(BF16)


def split3(x):
    high = x.astype(BF16)
    rest = x - high.astype(F32)
    mid = rest.astype(BF16)
    return high, mid, (rest - mid.astype(F32)).astype(BF16)


def pick(onehot, x):
    o = onehot.astype(BF16)
    high, mid, low = split3(x)
    return (dot(o, high) + dot(o, mid)) + dot(o, low)


def pick2(onehot, x):
    o = onehot.astype(BF16)
    high, low = split2(x)
    return dot(o, high) + dot(o, low)


def targets(first, count):
    j = first + lax.broadcasted_iota(jnp.int32, (1, count), 1)
    yh = (lax.shift_right_logical(j, 6).astype(F32) + 0.5) / 32.0 - 0.5
    ya = (lax.bitwise_and(j, 63).astype(F32) + 0.5) / 64.0 - 0.5
    return yh, ya


def basic_centre(ids):
    row = jnp.floor(ids / 32.0)
    return (row * 8.0 + 4.0) / 128.0 - 0.5, ((ids - row * 32.0) * 8.0 + 4.0) / 256.0 - 0.5


def cell_centre(cells):
    row = jnp.floor(cells / 8.0)
    return (row * 8.0 + 4.0) / 128.0 - 0.5, ((cells - row * 8.0) * 32.0 + 16.0) / 256.0 - 0.5


def tilt(centre, y):
    return (400.0 * centre[0]) * y[0] + (400.0 * centre[1]) * y[1]


def eye_mask():
    return lax.broadcasted_iota(jnp.int32, (128, 128), 0) == lax.broadcasted_iota(jnp.int32, (128, 128), 1)


def to_col(row):
    return jnp.sum(jnp.where(eye_mask(), jnp.broadcast_to(row, (128, 128)), 0.0), axis=1, keepdims=True)


def to_row(col):
    return jnp.sum(jnp.where(eye_mask(), jnp.broadcast_to(col, (128, 128)), 0.0), axis=0, keepdims=True)


def local_cells(placement_row, core):
    dst = lax.broadcasted_iota(jnp.int32, (128, 128), 0)
    src = lax.broadcasted_iota(jnp.int32, (128, 128), 1)
    side = lax.bitwise_xor(lax.shift_right_logical(dst, 6), core)
    slot = lax.bitwise_and(lax.shift_right_logical(dst, 4), 3) * 32 + side * 16 + lax.bitwise_and(dst, 15)
    col = jnp.sum(jnp.where(slot == src, jnp.broadcast_to(placement_row, (128, 128)), 0.0), axis=1, keepdims=True)
    return col, to_row(col)


def own_ids(member_rows, group):
    lane = lax.broadcasted_iota(jnp.int32, (16, 128), 1)
    sub = lax.broadcasted_iota(jnp.int32, (16, 128), 0)
    k = lax.shift_right_logical(sub, 2)
    rows = jnp.zeros((16, 128), F32)
    for i in range(4):
        rows = jnp.where(k == i, jnp.broadcast_to(member_rows[i], (16, 128)), rows)
    return jnp.sum(jnp.where(lane == 4 * group + lax.bitwise_and(sub, 3), rows, 0.0), axis=1, keepdims=True)


def low_half(shape):
    return lax.broadcasted_iota(jnp.int32, shape, 1) < 64


def swap(x):
    return pltpu.roll(x, 64, 1)


def doubled(x, upper):
    mask = low_half(x.shape)
    return jnp.where(mask, swap(x), x) if upper else jnp.where(mask, x, swap(x))


def segment(x, k):
    y = jnp.where(k >= 2.0, x[:, 128:], x[:, :128])
    odd = (k == 1.0) | (k == 3.0)
    z = jnp.where(odd, swap(y), y)
    return jnp.where(low_half(z.shape), z, swap(z))


def cell_sums(u, cell_ref):
    n = u.shape[0]
    x = jnp.concatenate(split2(u), axis=0)
    p = dot(x, cell_ref[...])
    p = p[:n] + p[n:]
    return p[:, :256] + p[:, 256:]


def cell_cols(e, high, low):
    n = e.shape[0]
    eh, el = split2(e)
    p = dot_nt(jnp.concatenate([eh, el], axis=0), high)
    return p[:n] + p[n:] + dot_nt(eh, low)


def basic_sums(t, basic_ref):
    n = t.shape[0]
    p = dot(jnp.concatenate(split2(t), axis=0), basic_ref[...])
    p = p[:n] + p[n:]
    return p + swap(p)


def basic_cols(e, basic):
    n = e.shape[0]
    p = dot_nt(jnp.concatenate(split2(e), axis=0), basic)
    return p[:n] + p[n:]


def sweep_a(log_b, mass, centre, y, cell_ref):
    b = jnp.exp(log_b - jnp.max(log_b, axis=1, keepdims=True))
    high, low = cell_ref[:, :256], cell_ref[:, 256:]
    u = jnp.exp(-200.0 * ((centre[0] - y[0]) ** 2 + (centre[1] - y[1]) ** 2))
    for i in range(4):
        s = cell_sums(u, cell_ref)
        e = mass * (s[:, CENTRE : CENTRE + 1] / s)
        d = cell_cols(e, high, low)
        if i < 3:
            u = b / d
    return e, d


def over_k(x, op):
    y = op(x[:8], x[8:])
    return op(y, pltpu.roll(y, 4, 0))


def twice(x):
    return jnp.concatenate([x, x], axis=0)


def sweep_b(log_b, mass, centre, y, basic_ref):
    r = tilt(centre, y)
    top = 200.0 * (centre[0] * centre[0] + centre[1] * centre[1])
    t = jnp.exp(-200.0 * ((centre[0] - y[0]) ** 2 + (centre[1] - y[1]) ** 2))
    for i in range(4):
        e = mass / basic_sums(t, basic_ref)
        if i == 3:
            break
        d = basic_cols(e, basic_ref[...])
        q = r - top
        peak = over_k(q, jnp.maximum)
        z = over_k(jnp.exp(q - twice(peak)) * d, jnp.add)
        v = r + twice(log_b - peak - jnp.log(z))
        top = jnp.max(v, axis=1, keepdims=True)
        t = jnp.exp(v - top)
    return e, top


def solve_pair(log_b_a, mass_a, mass_b, ids, y, cell_ref, basic_ref, send_ref):
    k = ids - 4.0 * jnp.floor(ids / 4.0)
    at_cell = cell_centre(jnp.floor(ids / 4.0))
    at_basic = basic_centre(ids)
    e_a, d_a = sweep_a(log_b_a, mass_a, at_cell, y, cell_ref)
    e_first = segment(e_a, k)
    d_first = basic_cols(e_first, basic_ref[...])
    v = log_b_a - jnp.log(d_a) + (400.0 * (at_basic[1] - at_cell[1])) * y[1]
    peak = over_k(v, jnp.maximum)
    log_b_b = peak + jnp.log(over_k(jnp.exp(v - twice(peak)) * d_first, jnp.add))
    e_second, top = sweep_b(log_b_b, mass_b, at_basic, y, basic_ref)
    send_ref[0:16, :] = jnp.where(low_half((16, 128)), e_first, e_second)
    send_ref[16:32, :] = jnp.broadcast_to(top, (16, 128))


def member_rows_of(members_ref):
    members = members_ref[...].astype(F32)
    return [to_row(members[:, k : k + 1]) for k in range(4)]


def first_kernel(place_ref, placement_ref, members_ref, own_ref, other_ref, cell_ref, basic_ref,
                 send_ref, mass_a_ref, mass_b_ref):
    cell_col, cell_row = local_cells(placement_ref[...].astype(F32), place_ref[0])
    ids = own_ids(member_rows_of(members_ref), place_ref[1])
    onehot = jnp.where(cell_row == jnp.floor(ids / 4.0), 1.0, 0.0)
    log_b = []
    for t in range(16):
        rows = [ref[x * 16 + t, 0:16, :] for ref in (own_ref, other_ref) for x in range(4)]
        log_b.append(pick(onehot, jnp.concatenate(rows, axis=0)))
    log_b = jnp.concatenate(log_b, axis=1)
    mass = []
    for part in (16, 17):
        rows = jnp.concatenate([own_ref[:, part, :], other_ref[:, part, :]], axis=0)
        mass.append(pick(onehot, rows))
    mass_a = jnp.concatenate(mass, axis=1)
    mass_b = segment(mass_a, ids - 4.0 * jnp.floor(ids / 4.0))
    mass_a_ref[...] = mass_a
    mass_b_ref[...] = mass_b
    solve_pair(log_b, mass_a, mass_b, ids, targets(0, W), cell_ref, basic_ref, send_ref)


def received(recv_ref):
    factors, tops = [], []
    for k in range(4):
        factors.append(jnp.concatenate([recv_ref[g, 4 * k : 4 * k + 4, :] for g in range(32)], axis=0))
        tops.append(jnp.concatenate([recv_ref[g, 16 + 4 * k : 20 + 4 * k, :] for g in range(32)], axis=0))
    return factors, tops


def a_rows(member_rows, cell_col, k):
    want = 4.0 * cell_col + float(k)
    return [jnp.where(row == want, 1.0, 0.0) for row in member_rows]


def pick_parts(onehots, parts, exact):
    get = pick if exact else pick2
    total = get(onehots[0], parts[0])
    for o, p in zip(onehots[1:], parts[1:]):
        total = total + get(o, p)
    return total


def cell_factors(by_k, upper):
    mask = low_half(by_k[0].shape)
    if upper:
        return jnp.concatenate([jnp.where(mask, swap(by_k[i]), by_k[i + 1]) for i in (0, 2)], axis=1)
    return jnp.concatenate([jnp.where(mask, by_k[i], swap(by_k[i + 1])) for i in (0, 2)], axis=1)


def mix(v, d):
    peak = jnp.maximum(jnp.maximum(v[0], v[1]), jnp.maximum(v[2], v[3]))
    z = [jnp.exp(a - peak) * b for a, b in zip(v, d)]
    return peak + jnp.log((z[0] + z[1]) + (z[2] + z[3]))


def second_kernel(place_ref, placement_ref, members_ref, own_ref, other_ref, recv_ref, mass_a_ref, mass_b_ref,
                  cell_ref, basic_ref, send_ref, log_b_ref):
    cell_col, cell_row = local_cells(placement_ref[...].astype(F32), place_ref[0])
    member_rows = member_rows_of(members_ref)
    ids = own_ids(member_rows, place_ref[1])
    own_cells = jnp.floor(ids / 4.0)
    factors, tops = received(recv_ref)
    by_k = [pick_parts(a_rows(member_rows, cell_col, k), factors, False) for k in range(4)]
    e_cell = cell_factors(by_k, False)
    want = jnp.concatenate([4.0 * own_cells + float(k) for k in range(4)], axis=0)
    hits = [jnp.where(row == want, 1.0, 0.0) for row in member_rows]
    slot = (hits[0] + hits[1]) + (hits[2] + hits[3])
    near = [pick2(slot, f) for f in factors]
    near_top = [pick(slot, t)[:, :1] for t in tops]
    near_ids = [jnp.sum(slot * row, axis=1, keepdims=True) for row in member_rows]
    near_cell = [jnp.where(cell_row == jnp.floor(i / 4.0), 1.0, 0.0) for i in near_ids]
    at_near = [basic_centre(i) for i in near_ids]
    own_first = near_ids[0] == want
    own_factor, own_top = near[3], near_top[3]
    for k in range(3):
        same = near_ids[k] == want
        own_factor = jnp.where(same, near[k], own_factor)
        own_top = jnp.where(same, near_top[k], own_top)
    del own_first
    e0 = jnp.concatenate([doubled(f, False) for f in near], axis=0)
    e1 = jnp.concatenate([doubled(f, True) for f in near] + [doubled(own_factor, True)], axis=0)
    at_cell = cell_centre(cell_col)
    at_want = basic_centre(want)
    near_all = jnp.concatenate(near_cell, axis=0)
    for block in range(8):
        y = targets(block * 256, 256)
        lanes = []
        for t in (2 * block, 2 * block + 1):
            rows = [ref[x * 16 + t, 0:16, :] for ref in (own_ref, other_ref) for x in range(4)]
            lanes.append(jnp.concatenate(rows, axis=0))
        log_b0 = jnp.concatenate(lanes, axis=1)
        here = pl.ds(block * 256, 256)
        d_cell = cell_cols(e_cell, cell_ref[here, :256], cell_ref[here, 256:])
        gamma = log_b0 - jnp.log(d_cell) - tilt(at_cell, y)
        gamma = pick(near_all, gamma)
        basic = basic_ref[here, :]
        d0 = basic_cols(e0, basic)
        d1 = basic_cols(e1, basic)
        tilts = [tilt(c, y) for c in at_near]
        rows = [slice(64 * k, 64 * k + 64) for k in range(4)]
        log_b1 = mix([gamma[rows[k]] + tilts[k] for k in range(4)], [d0[rows[k]] for k in range(4)])
        gamma1 = log_b1 - mix([tilts[k] - near_top[k] for k in range(4)], [d1[rows[k]] for k in range(4)])
        v = gamma1 + tilt(at_want, y) - own_top
        d_own = d1[256:]
        log_b_ref[:, here] = mix([v[16 * k : 16 * k + 16] for k in range(4)],
                                 [d_own[16 * k : 16 * k + 16] for k in range(4)])
    solve_pair(log_b_ref[...], mass_a_ref[...], mass_b_ref[...], ids, targets(0, W), cell_ref, basic_ref, send_ref)


def third_kernel(place_ref, placement_ref, members_ref, own_ref, other_ref, first_ref, second_ref, cell_ref,
                 basic_ref, out_ref, keep_ref):
    cell_col, cell_row = local_cells(placement_ref[...].astype(F32), place_ref[0])
    member_rows = member_rows_of(members_ref)
    members = members_ref[...].astype(F32)
    share = place_ref[2]
    y = targets(share * 128, 128)
    here = pl.ds(pl.multiple_of(share * 128, 128), 128)
    high, low, basic = cell_ref[here, :256], cell_ref[here, 256:], basic_ref[here, :]
    rows = [ref[x * 16 + share, 0:16, :] for ref in (own_ref, other_ref) for x in range(4)]
    log_b = jnp.concatenate(rows, axis=0)
    at_cell = cell_centre(cell_col)
    tilt_cell = tilt(at_cell, y)
    b_ids = [members[:, k : k + 1] for k in range(4)]
    b_cell = jnp.concatenate([jnp.where(cell_row == jnp.floor(i / 4.0), 1.0, 0.0) for i in b_ids], axis=0)
    b_tilt = [tilt(basic_centre(i), y) for i in b_ids]
    a_hits = [a_rows(member_rows, cell_col, k) for k in range(4)]
    a_slot = [(h[0] + h[1]) + (h[2] + h[3]) for h in a_hits]
    a_tilt = [tilt(basic_centre(4.0 * cell_col + float(k)), y) for k in range(4)]
    parts = [slice(128 * k, 128 * k + 128) for k in range(4)]
    for turn, ref in enumerate((first_ref, second_ref)):
        factors, tops = received(ref)
        by_k = [pick_parts(a_hits[k], factors, False) for k in range(4)]
        d_cell = cell_cols(cell_factors(by_k, False), high, low)
        gamma = pick(b_cell, log_b - jnp.log(d_cell) - tilt_cell)
        d0 = basic_cols(jnp.concatenate([doubled(f, False) for f in factors], axis=0), basic)
        d1 = basic_cols(jnp.concatenate([doubled(f, True) for f in factors], axis=0), basic)
        log_b1 = mix([gamma[parts[k]] + b_tilt[k] for k in range(4)], [d0[parts[k]] for k in range(4)])
        gamma1 = log_b1 - mix([b_tilt[k] - tops[k] for k in range(4)], [d1[parts[k]] for k in range(4)])
        back = pick(jnp.concatenate(a_slot, axis=0), gamma1)
        da = basic_cols(jnp.concatenate([doubled(f, True) for f in by_k], axis=0), basic)
        a_top = [pick_parts(a_hits[k], tops, True) for k in range(4)]
        v = [back[parts[k]] + a_tilt[k] - a_top[k] for k in range(4)]
        if turn == 0:
            log_b = mix(v, [da[parts[k]] for k in range(4)])
        else:
            for k in range(4):
                keep_ref[k, :, :] = jnp.exp(v[k] + jnp.log(da[parts[k]]))
    mine = pl.ds(pl.multiple_of(place_ref[3] * 16, 16), 16)
    for k in range(4):
        out_ref[:, k, :] = keep_ref[k, mine, :]


def call(body, inputs, outs, scratch=()):
    spec = pl.BlockSpec(memory_space=pltpu.VMEM)
    return pl.pallas_call(
        body,
        out_shape=[jax.ShapeDtypeStruct(s, F32) for s in outs],
        in_specs=[pl.BlockSpec(memory_space=pltpu.SMEM)] + [spec] * (len(inputs) - 1),
        out_specs=[spec] * len(outs),
        scratch_shapes=list(scratch),
        compiler_params=pltpu.CompilerParams(vmem_limit_bytes=48 * 2**20),
    )(*inputs)


def on_device(placement_a, members_b, source_mass, init_log, cell, basic):
    x, c, z, y = (lax.axis_index(name) for name in ("x", "c", "z", "y"))
    share = z * 4 + y
    place = jnp.stack([c, x * 8 + c * 4 + y, share, x]).astype(jnp.int32)
    log_b = jax.nn.logsumexp(init_log, axis=1) + float(np.log(64.0 / W))
    mass = lax.dynamic_slice_in_dim(source_mass, share, 1, 0).reshape(2, 128)
    block = jnp.concatenate([log_b, mass], axis=0)
    own = lax.all_to_all(jnp.broadcast_to(block[None], (64, 18, 128)), ("x", "z", "y"), 0, 0, tiled=True)
    other = lax.ppermute(own, "c", [(0, 1), (1, 0)])
    placement = placement_a.reshape(1, 128)

    def exchange(rows):
        return lax.all_to_all(jnp.broadcast_to(rows[None], (32, 32, 128)), ("x", "c", "y"), 0, 0, tiled=True)

    common = (place, placement, members_b, own, other)
    send, mass_a, mass_b = call(first_kernel, common + (cell, basic), [(32, 128), (16, 256), (16, 128)])
    first = exchange(send)
    (send,) = call(second_kernel, common + (first, mass_a, mass_b, cell, basic), [(32, 128)],
                   [pltpu.VMEM((16, W), F32)])
    second = exchange(send)
    (out,) = call(third_kernel, common + (first, second, cell, basic), [(16, 4, 128)],
                  [pltpu.VMEM((4, 128, 128), F32)])
    return out


def solution(mesh):
    split = Mesh(mesh.devices.reshape(4, 2, 4, 4), ("x", "c", "z", "y"))
    cell, basic = _tables()
    placed = (P(), P(), P(("x", "c"), None), P(("x", "c"), None, ("z", "y")), P(), P())
    body = jax.shard_map(
        on_device, mesh=split, in_specs=placed, out_specs=P(("x", "c"), None, ("z", "y")), check_vma=False
    )

    def run(placement_a, members_b, source_mass, init_log):
        return body(placement_a, members_b, source_mass, init_log, jnp.asarray(cell), jnp.asarray(basic))

    return run
```

```python
import numpy as np
import ml_dtypes

import jax
import jax.numpy as jnp
from jax import lax
from jax.experimental import pallas as pl
from jax.experimental.pallas import tpu as pltpu
from jax.sharding import Mesh, PartitionSpec as P

F32 = jnp.float32
BF16 = jnp.bfloat16
W = 2048
CENTRE = 128 + 31


def _halves(matrix):
    high = matrix.astype(ml_dtypes.bfloat16)
    low = (matrix - high.astype(np.float64)).astype(ml_dtypes.bfloat16)
    return high, low


def _thrice(matrix):
    high, low = _halves(matrix)
    return np.concatenate([high, high, low], axis=0)


def _tables():
    yh = (np.arange(32) + 0.5) / 32 - 0.5
    ya = (np.arange(64) + 0.5) / 64 - 0.5
    dh = (np.arange(8) - 3.5) / 128
    da = (np.arange(8) - 3.5) / 256
    shifts = [(k - 1.5) / 32 for k in range(4)]

    def whole(shift):
        up = np.exp(400.0 * dh[:, None] * yh[None])
        along = np.exp(400.0 * (da + shift)[:, None] * ya[None])
        return (up[:, None, :, None] * along[None, :, None, :]).reshape(64, W)

    def along(shift):
        part = np.zeros((2, 64, 2, 8, 8))
        for h in range(2):
            part[h, :, h] = np.exp(400.0 * ya[:, None] * (da + shift)[None])[:, None, :]
        return part.reshape(128, 128)

    cells = [along(s) for s in shifts]
    factors = [_thrice(m) for m in cells] + [_thrice(np.concatenate([m.T for m in cells], axis=0))]
    factors += [_thrice(along(0.0)), _thrice(along(0.0).T)]
    wholes = _halves(np.concatenate([whole(s) for s in shifts], axis=0)) + _halves(whole(0.0))
    return np.concatenate(factors, axis=0), np.concatenate(wholes, axis=0)


CELL, BACK, BASIC, BASIC_BACK = 0, 1536, 3072, 3456


def dot(a, b):
    return jnp.dot(a, b, preferred_element_type=F32)


def split2(x):
    high = x.astype(BF16)
    return high, (x - high.astype(F32)).astype(BF16)


def split3(x):
    high = x.astype(BF16)
    rest = x - high.astype(F32)
    mid = rest.astype(BF16)
    return high, mid, (rest - mid.astype(F32)).astype(BF16)


def pick(onehot, x):
    o = onehot.astype(BF16)
    high, mid, low = split3(x)
    return (dot(o, high) + dot(o, mid)) + dot(o, low)


def targets(first, count):
    j = first + lax.broadcasted_iota(jnp.int32, (1, count), 1)
    yh = (lax.shift_right_logical(j, 6).astype(F32) + 0.5) / 32.0 - 0.5
    ya = (lax.bitwise_and(j, 63).astype(F32) + 0.5) / 64.0 - 0.5
    return yh, ya


def basic_centre(ids):
    row = jnp.floor(ids / 32.0)
    return (row * 8.0 + 4.0) / 128.0 - 0.5, ((ids - row * 32.0) * 8.0 + 4.0) / 256.0 - 0.5


def cell_centre(cells):
    row = jnp.floor(cells / 8.0)
    return (row * 8.0 + 4.0) / 128.0 - 0.5, ((cells - row * 8.0) * 32.0 + 16.0) / 256.0 - 0.5


def tilt(centre, y):
    return (400.0 * centre[0]) * y[0] + (400.0 * centre[1]) * y[1]


def eye_mask():
    return lax.broadcasted_iota(jnp.int32, (128, 128), 0) == lax.broadcasted_iota(jnp.int32, (128, 128), 1)


def to_col(row):
    return jnp.sum(jnp.where(eye_mask(), jnp.broadcast_to(row, (128, 128)), 0.0), axis=1, keepdims=True)


def to_row(col):
    return jnp.sum(jnp.where(eye_mask(), jnp.broadcast_to(col, (128, 128)), 0.0), axis=0, keepdims=True)


def local_cells(placement_row, core):
    dst = lax.broadcasted_iota(jnp.int32, (128, 128), 0)
    src = lax.broadcasted_iota(jnp.int32, (128, 128), 1)
    side = lax.bitwise_xor(lax.shift_right_logical(dst, 6), core)
    slot = lax.bitwise_and(lax.shift_right_logical(dst, 4), 3) * 32 + side * 16 + lax.bitwise_and(dst, 15)
    col = jnp.sum(jnp.where(slot == src, jnp.broadcast_to(placement_row, (128, 128)), 0.0), axis=1, keepdims=True)
    return col, to_row(col)


def own_ids(member_rows, group):
    lane = lax.broadcasted_iota(jnp.int32, (16, 128), 1)
    sub = lax.broadcasted_iota(jnp.int32, (16, 128), 0)
    k = lax.shift_right_logical(sub, 2)
    rows = jnp.zeros((16, 128), F32)
    for i in range(4):
        rows = jnp.where(k == i, jnp.broadcast_to(member_rows[i], (16, 128)), rows)
    return jnp.sum(jnp.where(lane == 4 * group + lax.bitwise_and(sub, 3), rows, 0.0), axis=1, keepdims=True)


def low_half(shape):
    return lax.broadcasted_iota(jnp.int32, shape, 1) < 64


def swap(x):
    return pltpu.roll(x, 64, 1)


def doubled(x, upper):
    mask = low_half(x.shape)
    return jnp.where(mask, swap(x), x) if upper else jnp.where(mask, x, swap(x))


def segment(x, k):
    y = jnp.where(k >= 2.0, x[:, 256:], x[:, :256])
    return jnp.where((k == 1.0) | (k == 3.0), y[:, 128:], y[:, :128])


def quadrupled(x):
    return jnp.concatenate([doubled(x[:, :128], False), doubled(x[:, :128], True),
                            doubled(x[:, 128:], False), doubled(x[:, 128:], True)], axis=1)


def thrice(x):
    high, low = split2(x)
    return jnp.concatenate([high, low, high], axis=1)


def up_rows():
    lane = lax.broadcasted_iota(jnp.int32, (16, 128), 1)
    row = 2 * lax.broadcasted_iota(jnp.int32, (16, 128), 0) + lax.shift_right_logical(lane, 6)
    yh = (row.astype(F32) + 0.5) / 32.0 - 0.5
    dh = (lax.bitwise_and(lax.shift_right_logical(lane, 3), 7).astype(F32) - 3.5) / 128.0
    up = jnp.exp(400.0 * yh * dh)
    return [up[t : t + 1, :] for t in range(16)]


def sums(u, factor_ref, up, cells):
    n = u.shape[0]
    x = thrice(jnp.concatenate([u[:, 128 * t : 128 * t + 128] for t in range(16)], axis=0))
    out = []
    for first in [CELL + 384 * k for k in range(4)] if cells else [BASIC]:
        p = dot(x, factor_ref[first : first + 384, :])
        parts = [p[n * t : n * t + n] * h for t, h in enumerate(up)]
        while len(parts) > 1:
            parts = [parts[i] + parts[i + 1] for i in range(0, len(parts), 2)]
        out.append(parts[0] + swap(parts[0]))
    return jnp.concatenate(out, axis=1)


def cols(e, factor_ref, up):
    n, groups = e.shape[0], e.shape[1] // 128
    x = jnp.concatenate([e * jnp.concatenate([h] * groups, axis=1) for h in up], axis=0)
    d = dot(thrice(x), factor_ref[BACK : BACK + 1536, :] if groups == 4 else factor_ref[BASIC_BACK : BASIC_BACK + 384, :])
    return jnp.concatenate([d[n * t : n * t + n] for t in range(16)], axis=1)


def cell_cols(e, whole):
    n = e.shape[0]
    eh, el = split2(e)
    p = dot(jnp.concatenate([eh, el], axis=0), whole[:256])
    return p[:n] + p[n:] + dot(eh, whole[256:512])


def basic_cols(e, whole):
    n = e.shape[0]
    p = dot(jnp.concatenate(split2(e), axis=0), whole[512:])
    return p[:n] + p[n:]


def nearness(centre, y):
    return jnp.exp(-200.0 * ((centre[0] - y[0]) ** 2 + (centre[1] - y[1]) ** 2))


def balanced(mass, s):
    return mass * (s[:, CENTRE : CENTRE + 1] / s)


def sweep_a(log_b, mass, d, factor_ref, up):
    b = jnp.exp(log_b - jnp.max(log_b, axis=1, keepdims=True))
    for _ in range(3):
        e = balanced(mass, sums(b / d, factor_ref, up, True))
        d = cols(e, factor_ref, up)
    return e, d


def over_k(x, op):
    y = op(x[:8], x[8:])
    return op(y, pltpu.roll(y, 4, 0))


def twice(x):
    return jnp.concatenate([x, x], axis=0)


def column_part(r, top, d):
    q = r - top
    peak = over_k(q, jnp.maximum)
    return peak + jnp.log(over_k(jnp.exp(q - twice(peak)) * d, jnp.add))


def sweep_b(log_b, mass, r, part, factor_ref, up):
    for i in range(3):
        v = r + twice(log_b - part)
        top = jnp.max(v, axis=1, keepdims=True)
        e = mass / sums(jnp.exp(v - top), factor_ref, up, False)
        if i < 2:
            part = column_part(r, top, cols(e, factor_ref, up))
    return e, top


def solve_pair(log_b_a, mass_a, mass_b, ids, d, part, factor_ref, up, send_ref):
    y = targets(0, W)
    k = ids - 4.0 * jnp.floor(ids / 4.0)
    at_cell = cell_centre(jnp.floor(ids / 4.0))
    at_basic = basic_centre(ids)
    e_a, d_a = sweep_a(log_b_a, mass_a, d, factor_ref, up)
    e_first = segment(e_a, k)
    d_first = cols(e_first, factor_ref, up)
    v = log_b_a - jnp.log(d_a) + (400.0 * (at_basic[1] - at_cell[1])) * y[1]
    peak = over_k(v, jnp.maximum)
    log_b_b = peak + jnp.log(over_k(jnp.exp(v - twice(peak)) * d_first, jnp.add))
    e_second, top = sweep_b(log_b_b, mass_b, tilt(at_basic, y), part, factor_ref, up)
    rows = jnp.where(low_half((16, 128)), e_first, jnp.log(e_second) - top)
    for i in range(32):
        send_ref[i, :, :] = rows


def member_rows_of(members_ref):
    members = members_ref[...].astype(F32)
    return [to_row(members[:, k : k + 1]) for k in range(4)]


def block_kernel(place_ref, init_hbm, mass_hbm, block_ref, init_ref, mass_ref, sems):
    copies = [pltpu.make_async_copy(init_hbm, init_ref, sems.at[0]), pltpu.make_async_copy(mass_hbm, mass_ref, sems.at[1])]
    for copy in copies:
        copy.start()
    for copy in copies:
        copy.wait()
    x = [init_ref[:, k, :] for k in range(4)]
    peak = jnp.maximum(jnp.maximum(x[0], x[1]), jnp.maximum(x[2], x[3]))
    z = [jnp.exp(a - peak) for a in x]
    log_b = peak + jnp.log((z[0] + z[1]) + (z[2] + z[3])) + float(np.log(64.0 / W))
    row = mass_ref[pl.ds(place_ref[2], 1), :]
    mass = jnp.concatenate([row[:, :128], row[:, 128:]] + [jnp.zeros((6, 128), F32)], axis=0)
    block = jnp.concatenate([log_b, mass], axis=0)
    for i in range(64):
        block_ref[i, :, :] = block


def start_kernel(place_ref, placement_ref, members_ref, factor_ref, sum_a_ref, sum_b_ref, keep_ref):
    ids = own_ids(member_rows_of(members_ref), place_ref[1])
    y = targets(0, W)
    up = up_rows()
    sum_a_ref[...] = sums(nearness(cell_centre(jnp.floor(ids / 4.0)), y), factor_ref, up, True)
    sum_b_ref[...] = sums(nearness(basic_centre(ids), y), factor_ref, up, False)
    keep_ref[...] = factor_ref[...]


def first_kernel(place_ref, placement_ref, members_ref, own_ref, other_ref, sum_a_ref, sum_b_ref, factor_ref,
                 send_ref, table_ref, mass_a_ref, mass_b_ref, d_ref, part_ref):
    cell_col, cell_row = local_cells(placement_ref[...].astype(F32), place_ref[0])
    ids = own_ids(member_rows_of(members_ref), place_ref[1])
    up = up_rows()
    onehot = jnp.where(cell_row == jnp.floor(ids / 4.0), 1.0, 0.0)
    mass = []
    for part in (16, 17):
        rows = jnp.concatenate([own_ref[:, part, :], other_ref[:, part, :]], axis=0)
        mass.append(pick(onehot, rows))
    mass_a = quadrupled(jnp.concatenate(mass, axis=1))
    mass_b = segment(mass_a, ids - 4.0 * jnp.floor(ids / 4.0))
    d = cols(balanced(mass_a, sum_a_ref[...]), factor_ref, up)
    log_b = []
    for t in range(16):
        rows = [ref[x * 16 + t, 0:16, :] for ref in (own_ref, other_ref) for x in range(4)]
        rows = jnp.concatenate(rows, axis=0)
        table_ref[:, 128 * t : 128 * t + 128] = rows
        log_b.append(pick(onehot, rows))
    log_b = jnp.concatenate(log_b, axis=1)
    at_basic = basic_centre(ids)
    top = 200.0 * (at_basic[0] * at_basic[0] + at_basic[1] * at_basic[1])
    part = column_part(tilt(at_basic, targets(0, W)), top, cols(mass_b / sum_b_ref[...], factor_ref, up))
    mass_a_ref[...] = mass_a
    mass_b_ref[...] = mass_b
    d_ref[...] = d
    part_ref[...] = part
    solve_pair(log_b, mass_a, mass_b, ids, d, part, factor_ref, up, send_ref)


def received(recv_ref):
    return [jnp.concatenate([recv_ref[g, 4 * k : 4 * k + 4, :] for g in range(32)], axis=0) for k in range(4)]


def high_top(x):
    return jnp.max(jnp.where(low_half(x.shape), -jnp.inf, x), axis=1, keepdims=True)


def unpack(factors):
    tops = [-high_top(f) for f in factors]
    return ([doubled(f, False) for f in factors],
            [jnp.exp(doubled(f, True) + t) for f, t in zip(factors, tops)], tops)


def a_rows(member_rows, cell_col, k):
    want = 4.0 * cell_col + float(k)
    return [jnp.where(row == want, 1.0, 0.0) for row in member_rows]


def pick_parts(onehots, parts):
    total = pick(onehots[0], parts[0])
    for o, p in zip(onehots[1:], parts[1:]):
        total = total + pick(o, p)
    return total


def cell_factors(by_k):
    mask = low_half(by_k[0].shape)
    return jnp.concatenate([jnp.where(mask, by_k[i], swap(by_k[i + 1])) for i in (0, 2)], axis=1)


def mix(v, d):
    peak = jnp.maximum(jnp.maximum(v[0], v[1]), jnp.maximum(v[2], v[3]))
    z = [jnp.exp(a - peak) * b for a, b in zip(v, d)]
    return peak + jnp.log((z[0] + z[1]) + (z[2] + z[3]))


def second_kernel(place_ref, placement_ref, members_ref, recv_ref, table_ref, mass_a_ref, mass_b_ref, d_ref, part_ref,
                  factor_ref, whole_ref, send_ref, here_ref, log_b_ref):
    here_ref[...] = table_ref[:, pl.ds(pl.multiple_of(place_ref[2] * 128, 128), 128)]
    cell_col, cell_row = local_cells(placement_ref[...].astype(F32), place_ref[0])
    member_rows = member_rows_of(members_ref)
    ids = own_ids(member_rows, place_ref[1])
    own_cells = jnp.floor(ids / 4.0)
    factors = received(recv_ref)
    e_cell = cell_factors([pick_parts(a_rows(member_rows, cell_col, k), factors) for k in range(4)])
    want = jnp.concatenate([4.0 * own_cells + float(k) for k in range(4)], axis=0)
    hits = [jnp.where(row == want, 1.0, 0.0) for row in member_rows]
    slot = (hits[0] + hits[1]) + (hits[2] + hits[3])
    near = [pick(slot, f) for f in factors]
    near_ids = [jnp.sum(slot * row, axis=1, keepdims=True) for row in member_rows]
    near_cell = [jnp.where(cell_row == jnp.floor(i / 4.0), 1.0, 0.0) for i in near_ids]
    at_near = [basic_centre(i) for i in near_ids]
    e0, e1, tops = unpack(near)
    own_factor, own_top = e1[3], tops[3]
    for k in range(3):
        same = near_ids[k] == want
        own_factor = jnp.where(same, e1[k], own_factor)
        own_top = jnp.where(same, tops[k], own_top)
    e0 = jnp.concatenate(e0, axis=0)
    e1 = jnp.concatenate(e1 + [own_factor], axis=0)
    at_cell = cell_centre(cell_col)
    at_want = basic_centre(want)
    near_all = jnp.concatenate(near_cell, axis=0)
    for block in range(8):
        y = targets(block * 256, 256)
        here = pl.ds(block * 256, 256)
        whole = whole_ref[:, here]
        d_cell = cell_cols(e_cell, whole)
        gamma = pick(near_all, table_ref[:, here] - jnp.log(d_cell) - tilt(at_cell, y))
        d0 = basic_cols(e0, whole)
        d1 = basic_cols(e1, whole)
        tilts = [tilt(c, y) for c in at_near]
        rows = [slice(64 * k, 64 * k + 64) for k in range(4)]
        log_b1 = mix([gamma[rows[k]] + tilts[k] for k in range(4)], [d0[rows[k]] for k in range(4)])
        gamma1 = log_b1 - mix([tilts[k] - tops[k] for k in range(4)], [d1[rows[k]] for k in range(4)])
        v = gamma1 + tilt(at_want, y) - own_top
        d_own = d1[256:]
        log_b_ref[:, here] = mix([v[16 * k : 16 * k + 16] for k in range(4)],
                                 [d_own[16 * k : 16 * k + 16] for k in range(4)])
    solve_pair(log_b_ref[...], mass_a_ref[...], mass_b_ref[...], ids, d_ref[...], part_ref[...],
               factor_ref, up_rows(), send_ref)


def local_turn(place_ref, placement_ref, members_ref, recv_ref, whole_ref, log_b):
    cell_col, cell_row = local_cells(placement_ref[...].astype(F32), place_ref[0])
    member_rows = member_rows_of(members_ref)
    members = members_ref[...].astype(F32)
    share = place_ref[2]
    y = targets(share * 128, 128)
    here = pl.ds(pl.multiple_of(share * 128, 128), 128)
    whole = whole_ref[:, here]
    b_ids = [members[:, k : k + 1] for k in range(4)]
    b_cell = jnp.concatenate([jnp.where(cell_row == jnp.floor(i / 4.0), 1.0, 0.0) for i in b_ids], axis=0)
    b_tilt = [tilt(basic_centre(i), y) for i in b_ids]
    a_hits = [a_rows(member_rows, cell_col, k) for k in range(4)]
    a_slot = jnp.concatenate([(h[0] + h[1]) + (h[2] + h[3]) for h in a_hits], axis=0)
    a_tilt = [tilt(basic_centre(4.0 * cell_col + float(k)), y) for k in range(4)]
    parts = [slice(128 * k, 128 * k + 128) for k in range(4)]
    factors = received(recv_ref)
    by_k = [pick_parts(a_hits[k], factors) for k in range(4)]
    d_cell = cell_cols(cell_factors(by_k), whole)
    gamma = pick(b_cell, log_b - jnp.log(d_cell) - tilt(cell_centre(cell_col), y))
    e0, e1, tops = unpack(factors)
    _, ea, a_tops = unpack(by_k)
    d0 = basic_cols(jnp.concatenate(e0, axis=0), whole)
    d1 = basic_cols(jnp.concatenate(e1, axis=0), whole)
    da = basic_cols(jnp.concatenate(ea, axis=0), whole)
    log_b1 = mix([gamma[parts[k]] + b_tilt[k] for k in range(4)], [d0[parts[k]] for k in range(4)])
    gamma1 = log_b1 - mix([b_tilt[k] - tops[k] for k in range(4)], [d1[parts[k]] for k in range(4)])
    back = pick(a_slot, gamma1)
    return [back[parts[k]] + a_tilt[k] - a_tops[k] for k in range(4)], [da[parts[k]] for k in range(4)]


def middle_kernel(place_ref, placement_ref, members_ref, here_ref, recv_ref, whole_ref, log_b_ref):
    log_b_ref[...] = mix(*local_turn(place_ref, placement_ref, members_ref, recv_ref, whole_ref, here_ref[...]))


def last_kernel(place_ref, placement_ref, members_ref, log_b_ref, recv_ref, whole_ref, out_ref, keep_ref):
    v, d = local_turn(place_ref, placement_ref, members_ref, recv_ref, whole_ref, log_b_ref[...])
    for k in range(4):
        keep_ref[k, :, :] = jnp.exp(v[k] + jnp.log(d[k]))
    mine = pl.ds(pl.multiple_of(place_ref[3] * 16, 16), 16)
    for k in range(4):
        out_ref[:, k, :] = keep_ref[k, mine, :]


def call(body, inputs, outs, scratch=(), work=1, space=pltpu.VMEM):
    return pl.pallas_call(
        body,
        out_shape=[jax.ShapeDtypeStruct(s[:2], s[2]) if BF16 in s else jax.ShapeDtypeStruct(s, F32) for s in outs],
        in_specs=[pl.BlockSpec(memory_space=pltpu.SMEM)] + [pl.BlockSpec(memory_space=space)] * (len(inputs) - 1),
        out_specs=[pl.BlockSpec(memory_space=pltpu.VMEM)] * len(outs),
        scratch_shapes=list(scratch),
        compiler_params=pltpu.CompilerParams(vmem_limit_bytes=20 * 2**20),
        cost_estimate=pl.CostEstimate(flops=work * 10**9, bytes_accessed=10**6, transcendentals=0),
    )(*inputs)


def on_device(placement_a, members_b, source_mass, init_log, factors, wholes):
    x, c, z, y = (lax.axis_index(name) for name in ("x", "c", "z", "y"))
    share = z * 4 + y
    place = jnp.stack([c, x * 8 + c * 4 + y, share, x]).astype(jnp.int32)
    index = (place, placement_a.reshape(1, 128), members_b)
    (block,) = call(block_kernel, (place, init_log, source_mass), [(64, 24, 128)],
                    [pltpu.VMEM((16, 4, 128), F32), pltpu.VMEM((16, 256), F32), pltpu.SemaphoreType.DMA((2,))],
                    space=pltpu.HBM)
    own = lax.all_to_all(block, ("x", "z", "y"), 0, 0, tiled=True)
    sum_a, sum_b, factors = call(start_kernel, index + (factors,), [(16, 512), (16, 128), (3840, 128, BF16)])
    other = lax.ppermute(own, "c", [(0, 1), (1, 0)])

    def exchange(rows):
        return lax.all_to_all(rows, ("x", "c", "y"), 0, 0, tiled=True)

    send, table, *rest = call(first_kernel, index + (own, other, sum_a, sum_b, factors),
                              [(32, 16, 128), (128, W), (16, 512), (16, 128), (16, W), (8, W)])
    first = exchange(send)
    send, here = call(second_kernel, index + (first, table, *rest, factors, wholes), [(32, 16, 128), (128, 128)],
                   [pltpu.VMEM((16, W), F32)])
    second = exchange(send)
    (log_b,) = call(middle_kernel, index + (here, first, wholes), [(128, 128)])
    (out,) = call(last_kernel, index + (log_b, second, wholes), [(16, 4, 128)], [pltpu.VMEM((4, 128, 128), F32)])
    return out


def solution(mesh):
    split = Mesh(mesh.devices.reshape(4, 2, 4, 4), ("x", "c", "z", "y"))
    tables = _tables()
    placed = (P(), P(), P(("x", "c"), None), P(("x", "c"), None, ("z", "y"))) + (P(),) * len(tables)
    body = jax.shard_map(
        on_device, mesh=split, in_specs=placed, out_specs=P(("x", "c"), None, ("z", "y")), check_vma=False
    )

    def run(placement_a, members_b, source_mass, init_log):
        return body(placement_a, members_b, source_mass, init_log, *(jnp.asarray(t) for t in tables))

    return run
```

```python
import numpy as np
import ml_dtypes

import jax
import jax.numpy as jnp
from jax import lax
from jax.experimental import pallas as pl
from jax.experimental.pallas import tpu as pltpu
from jax.sharding import Mesh, PartitionSpec as P

F32 = jnp.float32
BF16 = jnp.bfloat16
W = 2048
CENTRE = 128 + 31


def _halves(matrix):
    high = matrix.astype(ml_dtypes.bfloat16)
    low = (matrix - high.astype(np.float64)).astype(ml_dtypes.bfloat16)
    return high, low


def _thrice(matrix):
    high, low = _halves(matrix)
    return np.concatenate([high, high, low], axis=0)


def _tables():
    yh = (np.arange(32) + 0.5) / 32 - 0.5
    ya = (np.arange(64) + 0.5) / 64 - 0.5
    dh = (np.arange(8) - 3.5) / 128
    da = (np.arange(8) - 3.5) / 256
    shifts = [(k - 1.5) / 32 for k in range(4)]

    def whole(shift):
        up = np.exp(400.0 * dh[:, None] * yh[None])
        along = np.exp(400.0 * (da + shift)[:, None] * ya[None])
        return (up[:, None, :, None] * along[None, :, None, :]).reshape(64, W)

    def along(shift):
        part = np.zeros((2, 64, 2, 8, 8))
        for h in range(2):
            part[h, :, h] = np.exp(400.0 * ya[:, None] * (da + shift)[None])[:, None, :]
        return part.reshape(128, 128)

    cells = [along(s) for s in shifts]
    factors = [_thrice(m) for m in cells] + [_thrice(np.concatenate([m.T for m in cells], axis=0))]
    factors += [_thrice(along(0.0)), _thrice(along(0.0).T)]
    wholes = _halves(np.concatenate([whole(s) for s in shifts], axis=0)) + _halves(whole(0.0))
    return np.concatenate(factors, axis=0), np.concatenate(wholes, axis=0)


CELL, BACK, BASIC, BASIC_BACK = 0, 1536, 3072, 3456


def dot(a, b):
    return jnp.dot(a, b, preferred_element_type=F32)


def split2(x):
    high = x.astype(BF16)
    return high, (x - high.astype(F32)).astype(BF16)


def split3(x):
    high = x.astype(BF16)
    rest = x - high.astype(F32)
    mid = rest.astype(BF16)
    return high, mid, (rest - mid.astype(F32)).astype(BF16)


def pick(onehot, x):
    o = onehot.astype(BF16)
    return dot(jnp.concatenate([o, o, o], axis=1), jnp.concatenate(split3(x), axis=0))


def targets(first, count):
    j = first + lax.broadcasted_iota(jnp.int32, (1, count), 1)
    yh = (lax.shift_right_logical(j, 6).astype(F32) + 0.5) / 32.0 - 0.5
    ya = (lax.bitwise_and(j, 63).astype(F32) + 0.5) / 64.0 - 0.5
    return yh, ya


def basic_centre(ids):
    row = jnp.floor(ids / 32.0)
    return (row * 8.0 + 4.0) / 128.0 - 0.5, ((ids - row * 32.0) * 8.0 + 4.0) / 256.0 - 0.5


def cell_centre(cells):
    row = jnp.floor(cells / 8.0)
    return (row * 8.0 + 4.0) / 128.0 - 0.5, ((cells - row * 8.0) * 32.0 + 16.0) / 256.0 - 0.5


def tilt(centre, y):
    return (400.0 * centre[0]) * y[0] + (400.0 * centre[1]) * y[1]


def eye_mask():
    return lax.broadcasted_iota(jnp.int32, (128, 128), 0) == lax.broadcasted_iota(jnp.int32, (128, 128), 1)


def to_col(row):
    return jnp.sum(jnp.where(eye_mask(), jnp.broadcast_to(row, (128, 128)), 0.0), axis=1, keepdims=True)


def to_row(col):
    return jnp.sum(jnp.where(eye_mask(), jnp.broadcast_to(col, (128, 128)), 0.0), axis=0, keepdims=True)


def local_cells(placement_row, core):
    dst = lax.broadcasted_iota(jnp.int32, (128, 128), 0)
    src = lax.broadcasted_iota(jnp.int32, (128, 128), 1)
    side = lax.bitwise_xor(lax.shift_right_logical(dst, 6), core)
    slot = lax.bitwise_and(lax.shift_right_logical(dst, 4), 3) * 32 + side * 16 + lax.bitwise_and(dst, 15)
    col = jnp.sum(jnp.where(slot == src, jnp.broadcast_to(placement_row, (128, 128)), 0.0), axis=1, keepdims=True)
    return col, to_row(col)


def own_ids(member_rows, group):
    lane = lax.broadcasted_iota(jnp.int32, (16, 128), 1)
    sub = lax.broadcasted_iota(jnp.int32, (16, 128), 0)
    k = lax.shift_right_logical(sub, 2)
    rows = jnp.zeros((16, 128), F32)
    for i in range(4):
        rows = jnp.where(k == i, jnp.broadcast_to(member_rows[i], (16, 128)), rows)
    return jnp.sum(jnp.where(lane == 4 * group + lax.bitwise_and(sub, 3), rows, 0.0), axis=1, keepdims=True)


def low_half(shape):
    return lax.broadcasted_iota(jnp.int32, shape, 1) < 64


def swap(x):
    return pltpu.roll(x, 64, 1)


def doubled(x, upper):
    mask = low_half(x.shape)
    return jnp.where(mask, swap(x), x) if upper else jnp.where(mask, x, swap(x))


def segment(x, k):
    y = jnp.where(k >= 2.0, x[:, 256:], x[:, :256])
    return jnp.where((k == 1.0) | (k == 3.0), y[:, 128:], y[:, :128])


def quadrupled(x):
    return jnp.concatenate([doubled(x[:, :128], False), doubled(x[:, :128], True),
                            doubled(x[:, 128:], False), doubled(x[:, 128:], True)], axis=1)


def thrice(x):
    high, low = split2(x)
    return jnp.concatenate([high, low, high], axis=1)


def up_rows():
    lane = lax.broadcasted_iota(jnp.int32, (16, 128), 1)
    row = 2 * lax.broadcasted_iota(jnp.int32, (16, 128), 0) + lax.shift_right_logical(lane, 6)
    yh = (row.astype(F32) + 0.5) / 32.0 - 0.5
    dh = (lax.bitwise_and(lax.shift_right_logical(lane, 3), 7).astype(F32) - 3.5) / 128.0
    up = jnp.exp(400.0 * yh * dh)
    return [up[t : t + 1, :] for t in range(16)]


def sums(u, factor_ref, up, cells):
    n = u.shape[0]
    x = thrice(jnp.concatenate([u[:, 128 * t : 128 * t + 128] for t in range(16)], axis=0))
    out = []
    for first in [CELL + 384 * k for k in range(4)] if cells else [BASIC]:
        p = dot(x, factor_ref[first : first + 384, :])
        parts = [p[n * t : n * t + n] * h for t, h in enumerate(up)]
        while len(parts) > 1:
            parts = [parts[i] + parts[i + 1] for i in range(0, len(parts), 2)]
        out.append(parts[0] + swap(parts[0]))
    return jnp.concatenate(out, axis=1)


def cols(e, factor_ref, up):
    n, groups = e.shape[0], e.shape[1] // 128
    x = jnp.concatenate([e * jnp.concatenate([h] * groups, axis=1) for h in up], axis=0)
    d = dot(thrice(x), factor_ref[BACK : BACK + 1536, :] if groups == 4 else factor_ref[BASIC_BACK : BASIC_BACK + 384, :])
    return jnp.concatenate([d[n * t : n * t + n] for t in range(16)], axis=1)


def halves(e):
    return jnp.concatenate(split2(e), axis=0)


def cell_cols(e, whole):
    n = e.shape[0] // 2
    p = dot(e, whole[:256])
    return p[:n] + p[n:] + dot(e[:n], whole[256:512])


def basic_cols(e, whole):
    n = e.shape[0] // 2
    p = dot(e, whole[512:])
    return p[:n] + p[n:]


def nearness(centre, y):
    return jnp.exp(-200.0 * ((centre[0] - y[0]) ** 2 + (centre[1] - y[1]) ** 2))


def balanced(mass, s):
    return mass * (s[:, CENTRE : CENTRE + 1] / s)


def sweep_a(log_b, mass, d, factor_ref, up, beside):
    b = jnp.exp(log_b - jnp.max(log_b, axis=1, keepdims=True))
    for i in range(3):
        beside(i)
        e = balanced(mass, sums(b / d, factor_ref, up, True))
        d = cols(e, factor_ref, up)
    return e, d


def over_k(x, op):
    y = op(x[:8], x[8:])
    return op(y, pltpu.roll(y, 4, 0))


def twice(x):
    return jnp.concatenate([x, x], axis=0)


def column_part(r, top, d):
    q = r - top
    peak = over_k(q, jnp.maximum)
    return peak + jnp.log(over_k(jnp.exp(q - twice(peak)) * d, jnp.add))


def sweep_b(log_b, mass, r, part, factor_ref, up, beside):
    for i in range(3):
        beside(5 + i)
        v = r + twice(log_b - part)
        top = jnp.max(v, axis=1, keepdims=True)
        e = mass / sums(jnp.exp(v - top), factor_ref, up, False)
        if i < 2:
            part = column_part(r, top, cols(e, factor_ref, up))
    return e, top


def solve_pair(log_b_a, mass_a, mass_b, ids, d, part, factor_ref, up, send_ref, beside=lambda i: None):
    y = targets(0, W)
    k = ids - 4.0 * jnp.floor(ids / 4.0)
    at_cell = cell_centre(jnp.floor(ids / 4.0))
    at_basic = basic_centre(ids)
    e_a, d_a = sweep_a(log_b_a, mass_a, d, factor_ref, up, beside)
    e_first = segment(e_a, k)
    beside(3)
    d_first = cols(e_first, factor_ref, up)
    v = log_b_a - jnp.log(d_a) + (400.0 * (at_basic[1] - at_cell[1])) * y[1]
    peak = over_k(v, jnp.maximum)
    beside(4)
    log_b_b = peak + jnp.log(over_k(jnp.exp(v - twice(peak)) * d_first, jnp.add))
    e_second, top = sweep_b(log_b_b, mass_b, tilt(at_basic, y), part, factor_ref, up, beside)
    rows = jnp.where(low_half((16, 128)), e_first, jnp.log(e_second) - top)
    for i in range(32):
        send_ref[i, :, :] = rows


def member_rows_of(members_ref):
    members = members_ref[...].astype(F32)
    return [to_row(members[:, k : k + 1]) for k in range(4)]


def exchange_ids(members_ref):
    members = members_ref[...].astype(F32)
    slot = lax.broadcasted_iota(jnp.int32, (128, 128), 0)
    lane = lax.broadcasted_iota(jnp.int32, (128, 128), 1)
    k = lax.bitwise_and(lax.shift_right_logical(lane, 2), 3)
    value = jnp.broadcast_to(members[:, 0:1], (128, 128))
    for i in range(1, 4):
        value = jnp.where(k == i, jnp.broadcast_to(members[:, i : i + 1], (128, 128)), value)
    of_lane = 4 * lax.shift_right_logical(lane, 4) + lax.bitwise_and(lane, 3)
    return jnp.concatenate(
        [jnp.sum(jnp.where(slot == of_lane + 32 * t, value, 0.0), axis=0, keepdims=True) for t in range(4)], axis=1)


def near_cells(want, member_rows, cell_row, exchanged, cells_ref, groups_ref, rows_ref, ids_ref):
    hits = [jnp.where(row == want, 1.0, 0.0) for row in member_rows]
    slot = (hits[0] + hits[1]) + (hits[2] + hits[3])
    ids = jnp.concatenate([jnp.sum(slot * row, axis=1, keepdims=True) for row in member_rows], axis=0)
    cell = jnp.floor(ids / 4.0)
    cells = jnp.where(cell_row == cell, 1.0, 0.0)
    cells_ref[...] = cells.astype(BF16)
    for k in range(4):
        groups_ref[256 * k : 256 * k + 256, :] = jnp.where(exchanged == 4.0 * cell + float(k), 1.0, 0.0).astype(BF16)
    ids = jnp.concatenate([ids, want], axis=0)
    rows_ref[...] = jnp.where(exchanged == ids, 1.0, 0.0).astype(BF16)
    ids_ref[...] = jnp.broadcast_to(ids, (320, 128))
    return ids, cells


def start_kernel(place_ref, placement_ref, members_ref, factor_ref, sum_a_ref, sum_b_ref, keep_ref, own_ids_ref, onehot_ref,
                 cell_ref, cells_ref, groups_ref, rows_ref, ids_ref):
    cell_col, cell_row = local_cells(placement_ref[...].astype(F32), place_ref[0])
    member_rows = member_rows_of(members_ref)
    ids = own_ids(member_rows, place_ref[1])
    y = targets(0, W)
    up = up_rows()
    sum_a_ref[...] = sums(nearness(cell_centre(jnp.floor(ids / 4.0)), y), factor_ref, up, True)
    sum_b_ref[...] = sums(nearness(basic_centre(ids), y), factor_ref, up, False)
    keep_ref[...] = factor_ref[...]
    own_ids_ref[...] = jnp.broadcast_to(ids, (16, 128))
    cells = jnp.floor(ids / 4.0)
    onehot_ref[...] = jnp.where(cell_row == cells, 1.0, 0.0)
    cell_ref[...] = jnp.broadcast_to(cell_col, (128, 128))
    want = jnp.concatenate([4.0 * cells + float(k) for k in range(4)], axis=0)
    near_cells(want, member_rows, cell_row, exchange_ids(members_ref), cells_ref, groups_ref, rows_ref, ids_ref)


def first_kernel(place_ref, own_ref, other_ref, sum_a_ref, sum_b_ref, ids_ref, onehot_ref, cell_ref, cells_ref, near_ref,
                 factor_ref, send_ref, here_ref, level_ref, mass_a_ref, mass_b_ref, d_ref, part_ref, table_ref):
    ids, onehot, up = ids_ref[:, :1], onehot_ref[...], up_rows()
    mass = []
    for part in (16, 17):
        rows = jnp.concatenate([own_ref[:, part, :], other_ref[:, part, :]], axis=0)
        mass.append(pick(onehot, rows))
    mass_a = quadrupled(jnp.concatenate(mass, axis=1))
    mass_b = segment(mass_a, ids - 4.0 * jnp.floor(ids / 4.0))
    d = cols(balanced(mass_a, sum_a_ref[...]), factor_ref, up)
    log_b = []
    for t in range(16):
        rows = [ref[x * 16 + t, 0:16, :] for ref in (own_ref, other_ref) for x in range(4)]
        rows = jnp.concatenate(rows, axis=0)
        table_ref[:, 128 * t : 128 * t + 128] = rows
        log_b.append(pick(onehot, rows))
    here_ref[...] = table_ref[:, pl.ds(pl.multiple_of(place_ref[2] * 128, 128), 128)]
    log_b = jnp.concatenate(log_b, axis=1)
    at_basic = basic_centre(ids)
    top = 200.0 * (at_basic[0] * at_basic[0] + at_basic[1] * at_basic[1])
    part = column_part(tilt(at_basic, targets(0, W)), top, cols(mass_b / sum_b_ref[...], factor_ref, up))
    mass_a_ref[...] = mass_a
    mass_b_ref[...] = mass_b
    d_ref[...] = d
    part_ref[...] = part
    near, cell_col = near_ref[0:256, :1], cell_ref[:, :1]

    def level(block):
        at = slice(256 * block, 256 * block + 256)
        level_ref[:, at] = near_level(near, cells_ref[...], table_ref[:, at], cell_col, targets(256 * block, 256))

    solve_pair(log_b, mass_a, mass_b, ids, d, part, factor_ref, up, send_ref, level)


def received(recv_ref):
    return [jnp.concatenate([recv_ref[g, 4 * k : 4 * k + 4, :] for g in range(32)], axis=0) for k in range(4)]


def high_top(x):
    return jnp.max(jnp.where(low_half(x.shape), -jnp.inf, x), axis=1, keepdims=True)


def unpack(f):
    top = -high_top(f)
    return doubled(f, False), jnp.exp(doubled(f, True) + top), top


def a_rows(member_rows, cell_col, k):
    want = 4.0 * cell_col + float(k)
    return jnp.concatenate([jnp.where(row == want, 1.0, 0.0) for row in member_rows], axis=1).astype(BF16)


def packed(f):
    high, low = split2(f)
    return jnp.where(low_half(f.shape), high.astype(F32), swap(low.astype(F32))).astype(BF16)


def cell_halves(by_k):
    mask = low_half(by_k[0].shape)
    high = [jnp.where(mask, by_k[i], swap(by_k[i + 1])) for i in (0, 2)]
    low = [jnp.where(mask, swap(by_k[i]), by_k[i + 1]) for i in (0, 2)]
    return jnp.concatenate([jnp.concatenate(high, axis=1), jnp.concatenate(low, axis=1)], axis=0).astype(BF16)


def mix(v, d):
    peak = jnp.maximum(jnp.maximum(v[0], v[1]), jnp.maximum(v[2], v[3]))
    z = [jnp.exp(a - peak) * b for a, b in zip(v, d)]
    return peak + jnp.log((z[0] + z[1]) + (z[2] + z[3]))


def near_level(ids, cells, log_b, cell_col, y):
    return pick(cells, log_b - tilt(cell_centre(cell_col), y)) + tilt(basic_centre(ids), y)


def gathered(recv_ref, groups_ref, rows_ref):
    f = recv_ref[...].reshape(512, 128)
    by_k = dot(groups_ref[...], packed(f))
    o = rows_ref[...]
    high, mid, low = split3(f)
    e0, e1, top = unpack((dot(o, high) + dot(o, mid)) + dot(o, low))
    by_k = [by_k[256 * k : 256 * k + 256] for k in range(4)]
    return cell_halves(by_k), halves(e0[:256]), halves(e1), top


def near_margins(gather, level, centre, y, whole):
    e_cell, e0, e1, top = gather
    parts = [slice(64 * k, 64 * k + 64) for k in range(4)]
    v = level - jnp.log(cell_cols(e_cell, whole))
    d0 = basic_cols(e0, whole)
    d1 = basic_cols(e1, whole)
    q = tilt(centre, y) - top
    log_b = mix([v[a] for a in parts], [d0[a] for a in parts])
    gamma = log_b - mix([q[a] for a in parts], [d1[a] for a in parts])
    return gamma + q[256:], d1[256:]


def second_kernel(place_ref, own_ids_ref, recv_ref, level_ref, groups_ref, rows_ref, ids_ref, mass_a_ref, mass_b_ref, d_ref,
                  part_ref, factor_ref, whole_ref, send_ref, here_ref):
    here_ref[...] = whole_ref[:, pl.ds(pl.multiple_of(place_ref[2] * 128, 128), 128)]
    gather = gathered(recv_ref, groups_ref, rows_ref)
    centre = basic_centre(ids_ref[:, :1])
    log_b = []
    for block in range(8):
        at = slice(block * 256, block * 256 + 256)
        v, d = near_margins(gather, level_ref[:, at], centre, targets(256 * block, 256), whole_ref[:, at])
        log_b.append(mix([v[16 * k : 16 * k + 16] for k in range(4)], [d[16 * k : 16 * k + 16] for k in range(4)]))
    solve_pair(jnp.concatenate(log_b, axis=1), mass_a_ref[...], mass_b_ref[...], own_ids_ref[:, :1], d_ref[...], part_ref[...],
               factor_ref, up_rows(), send_ref)


def middle_kernel(place_ref, placement_ref, members_ref, log_b_ref, recv_ref, whole_ref, level_ref, cells_ref, groups_ref,
                  rows_ref, ids_ref):
    cell_col, cell_row = local_cells(placement_ref[...].astype(F32), place_ref[0])
    member_rows = member_rows_of(members_ref)
    members = members_ref[...].astype(F32)
    share = place_ref[2]
    y = targets(share * 128, 128)
    whole = whole_ref[...]
    b_ids = [members[:, k : k + 1] for k in range(4)]
    b_cell = jnp.concatenate([jnp.where(cell_row == jnp.floor(i / 4.0), 1.0, 0.0) for i in b_ids], axis=0)
    b_tilt = [tilt(basic_centre(i), y) for i in b_ids]
    a_tilt = [tilt(basic_centre(4.0 * cell_col + float(k)), y) for k in range(4)]
    parts = [slice(128 * k, 128 * k + 128) for k in range(4)]
    every = jnp.concatenate(received(recv_ref), axis=0)
    hits = [a_rows(member_rows, cell_col, k) for k in range(4)]
    rows = packed(every)
    e_cell = cell_halves([dot(h, rows) for h in hits])
    by_k = jnp.concatenate([pick(h, every) for h in hits], axis=0)
    gamma = pick(b_cell, log_b_ref[...] - jnp.log(cell_cols(e_cell, whole)) - tilt(cell_centre(cell_col), y))
    e0, e1, top = unpack(every)
    _, ea, a_top = unpack(by_k)
    d0, d1, da = [basic_cols(halves(e), whole) for e in (e0, e1, ea)]
    log_b1 = mix([gamma[a] + t for a, t in zip(parts, b_tilt)], [d0[a] for a in parts])
    gamma1 = log_b1 - mix([t - top[a] for a, t in zip(parts, b_tilt)], [d1[a] for a in parts])
    log_b = []
    for k in range(4):
        hit = hits[k].astype(F32)
        slot = (hit[:, :128] + hit[:, 128:256]) + (hit[:, 256:384] + hit[:, 384:])
        log_b.append(pick(slot, gamma1) + a_tilt[k] - a_top[parts[k]])
    log_b = mix(log_b, [da[a] for a in parts])
    lane = lax.broadcasted_iota(jnp.int32, (16, 128), 1)
    first = place_ref[3] * 16 + lax.broadcasted_iota(jnp.int32, (16, 128), 0)
    own_cells = jnp.sum(jnp.where(lane == first, jnp.broadcast_to(cell_row, (16, 128)), 0.0), axis=1, keepdims=True)
    want = jnp.concatenate([4.0 * own_cells + float(k) for k in range(4)], axis=0)
    ids, cells = near_cells(want, member_rows, cell_row, exchange_ids(members_ref), cells_ref, groups_ref, rows_ref, ids_ref)
    level_ref[...] = near_level(ids[:256], cells, log_b, cell_col, y)


def last_kernel(place_ref, recv_ref, level_ref, groups_ref, rows_ref, ids_ref, whole_ref, out_ref):
    centre = basic_centre(ids_ref[:, :1])
    v, d = near_margins(gathered(recv_ref, groups_ref, rows_ref), level_ref[...], centre,
                        targets(place_ref[2] * 128, 128), whole_ref[...])
    out = jnp.exp(v + jnp.log(d))
    for k in range(4):
        out_ref[:, k, :] = out[16 * k : 16 * k + 16]


def call(body, inputs, outs, scratch=(), work=1):
    def spec(value):
        return pl.BlockSpec(memory_space=pltpu.SMEM if value.shape == (4,) else pltpu.VMEM)

    return pl.pallas_call(
        body,
        out_shape=[jax.ShapeDtypeStruct(s[:-1], BF16) if s[-1] is BF16 else jax.ShapeDtypeStruct(s, F32) for s in outs],
        in_specs=[spec(value) for value in inputs],
        out_specs=[pl.BlockSpec(memory_space=pltpu.VMEM)] * len(outs),
        scratch_shapes=list(scratch),
        compiler_params=pltpu.CompilerParams(vmem_limit_bytes=24 * 2**20),
        cost_estimate=pl.CostEstimate(flops=work * 10**9, bytes_accessed=10**6, transcendentals=0),
    )(*inputs)


FACTORS = (3840, 128, BF16)
NEAR = [(256, 128, BF16), (1024, 512, BF16), (320, 512, BF16), (320, 128)]


def on_device(placement_a, members_b, source_mass, init_log, factors, wholes):
    x, c, z, y = (lax.axis_index(name) for name in ("x", "c", "z", "y"))
    share = z * 4 + y
    place = jnp.stack([c, x * 8 + c * 4 + y, share, x]).astype(jnp.int32)
    index = (place, placement_a.reshape(1, 128), members_b)
    v = [init_log[:, k, :] for k in range(4)]
    peak = jnp.maximum(jnp.maximum(v[0], v[1]), jnp.maximum(v[2], v[3]))
    e = [jnp.exp(a - peak) for a in v]
    log_b = peak + jnp.log((e[0] + e[1]) + (e[2] + e[3])) + float(np.log(64.0 / W))
    mass = lax.dynamic_slice_in_dim(source_mass, share, 1, 0).reshape(2, 128)
    block = jnp.concatenate([log_b, mass, jnp.zeros((6, 128), F32)], axis=0)
    own = lax.all_to_all(jnp.broadcast_to(block[None], (64, 24, 128)), ("x", "z", "y"), 0, 0, tiled=True)
    sum_a, sum_b, factors, own_ids_, onehot, cell, cells, groups, rows, ids = call(
        start_kernel, index + (factors,), [(16, 512), (16, 128), FACTORS, (16, 128), (16, 128), (128, 128)] + NEAR)
    other = lax.ppermute(own, "c", [(0, 1), (1, 0)])

    def exchange(rows):
        return lax.all_to_all(rows, ("x", "c", "y"), 0, 0, tiled=True)

    send, here, level, *rest = call(
        first_kernel, (place, own, other, sum_a, sum_b, own_ids_, onehot, cell, cells, ids, factors),
        [(32, 16, 128), (128, 128), (256, W), (16, 512), (16, 128), (16, W), (8, W)], [pltpu.VMEM((128, W), F32)])
    first = exchange(send)
    send, whole = call(second_kernel, (place, own_ids_, first, level, groups, rows, ids, *rest, factors, wholes),
                       [(32, 16, 128), (640, 128, BF16)])
    second = exchange(send)
    level, _, groups, rows, ids = call(middle_kernel, index + (here, first, whole), [(256, 128)] + NEAR)
    (out,) = call(last_kernel, (place, second, level, groups, rows, ids, whole), [(16, 4, 128)])
    return out


def solution(mesh):
    split = Mesh(mesh.devices.reshape(4, 2, 4, 4), ("x", "c", "z", "y"))
    tables = _tables()
    placed = (P(), P(), P(("x", "c"), None), P(("x", "c"), None, ("z", "y"))) + (P(),) * len(tables)
    body = jax.shard_map(
        on_device, mesh=split, in_specs=placed, out_specs=P(("x", "c"), None, ("z", "y")), check_vma=False
    )

    def run(placement_a, members_b, source_mass, init_log):
        return body(placement_a, members_b, source_mass, init_log, *(jnp.asarray(t) for t in tables))

    return run
```

```python
import numpy as np
import ml_dtypes

import jax
import jax.numpy as jnp
from jax import lax
from jax.experimental import pallas as pl
from jax.experimental.pallas import tpu as pltpu
from jax.sharding import Mesh, PartitionSpec as P

F32 = jnp.float32
BF16 = jnp.bfloat16
W = 2048
CENTRE = (slice(48, 64), slice(15, 16))


def _halves(matrix):
    high = matrix.astype(ml_dtypes.bfloat16)
    low = (matrix - high.astype(np.float64)).astype(ml_dtypes.bfloat16)
    return high, low


def _thrice(matrix):
    high, low = _halves(matrix)
    return np.concatenate([high, high, low], axis=0)


def _tables():
    yh = (np.arange(32) + 0.5) / 32 - 0.5
    ya = (np.arange(64) + 0.5) / 64 - 0.5
    dh = (np.arange(8) - 3.5) / 128
    da = (np.arange(8) - 3.5) / 256
    shifts = [(k - 1.5) / 32 for k in range(4)]

    def whole(shift):
        up = np.exp(400.0 * dh[:, None] * yh[None])
        along = np.exp(400.0 * (da + shift)[:, None] * ya[None])
        return (up[:, None, :, None] * along[None, :, None, :]).reshape(64, W)

    def along(shift):
        part = np.zeros((2, 64, 2, 8, 8))
        for h in range(2):
            part[h, :, h] = np.exp(400.0 * ya[:, None] * (da + shift)[None])[:, None, :]
        return part.reshape(128, 128)

    cell = np.concatenate([np.exp(400.0 * ya[:, None] * (da + s)[None]) for s in shifts], axis=1)
    high, low = _halves(np.concatenate([cell.T, cell.T], axis=1))
    order = np.zeros((8, 4, 8, 8, 4, 4, 8), ml_dtypes.bfloat16)
    for i, k, r in np.ndindex(8, 4, 8):
        order[i, k, i, r, :, k, r] = 1
    factors = [
        _thrice(np.tile(cell, (2, 4))),
        np.concatenate([high, high, low, np.zeros_like(low)], axis=0),
        _thrice(along(0.0)),
        _thrice(along(0.0).T),
        order.reshape(2048, 128),
    ]
    wholes = _halves(np.concatenate([whole(s) for s in shifts], axis=0)) + _halves(whole(0.0))
    up = np.exp(400.0 * yh.reshape(16, 2, 1) * dh[None, None])
    of_row = np.repeat(up.transpose(0, 2, 1).reshape(128, 1, 2), 64, axis=2)
    of_pixel = np.repeat(up.reshape(16, 1, 16), 8, axis=2)
    ups = np.repeat(np.concatenate([of_row, of_pixel], axis=0), 8, axis=1).reshape(1152, 128)
    return np.concatenate(factors, axis=0), np.concatenate(wholes, axis=0), ups.astype(np.float32)


CELL, BACK, BASIC, BASIC_BACK, ORDER = 0, 384, 512, 896, 1280


def dot(a, b):
    return jnp.dot(a, b, preferred_element_type=F32)


def split2(x):
    high = x.astype(BF16)
    return high, (x - high.astype(F32)).astype(BF16)


def split3(x):
    high = x.astype(BF16)
    rest = x - high.astype(F32)
    mid = rest.astype(BF16)
    return high, mid, (rest - mid.astype(F32)).astype(BF16)


def pick(onehot, x):
    o = onehot.astype(BF16)
    return dot(jnp.concatenate([o, o, o], axis=1), jnp.concatenate(split3(x), axis=0))


def targets(first, count):
    j = first + lax.broadcasted_iota(jnp.int32, (1, count), 1)
    yh = (lax.shift_right_logical(j, 6).astype(F32) + 0.5) / 32.0 - 0.5
    ya = (lax.bitwise_and(j, 63).astype(F32) + 0.5) / 64.0 - 0.5
    return yh, ya


def basic_centre(ids):
    row = jnp.floor(ids / 32.0)
    return (row * 8.0 + 4.0) / 128.0 - 0.5, ((ids - row * 32.0) * 8.0 + 4.0) / 256.0 - 0.5


def cell_centre(cells):
    row = jnp.floor(cells / 8.0)
    return (row * 8.0 + 4.0) / 128.0 - 0.5, ((cells - row * 8.0) * 32.0 + 16.0) / 256.0 - 0.5


def tilt(centre, y):
    return (400.0 * centre[0]) * y[0] + (400.0 * centre[1]) * y[1]


def eye_mask():
    return lax.broadcasted_iota(jnp.int32, (128, 128), 0) == lax.broadcasted_iota(jnp.int32, (128, 128), 1)


def to_col(row):
    return jnp.sum(jnp.where(eye_mask(), jnp.broadcast_to(row, (128, 128)), 0.0), axis=1, keepdims=True)


def to_row(col):
    return jnp.sum(jnp.where(eye_mask(), jnp.broadcast_to(col, (128, 128)), 0.0), axis=0, keepdims=True)


def local_cells(placement_row, core):
    dst = lax.broadcasted_iota(jnp.int32, (128, 128), 0)
    src = lax.broadcasted_iota(jnp.int32, (128, 128), 1)
    side = lax.bitwise_xor(lax.shift_right_logical(dst, 6), core)
    slot = lax.bitwise_and(lax.shift_right_logical(dst, 4), 3) * 32 + side * 16 + lax.bitwise_and(dst, 15)
    col = jnp.sum(jnp.where(slot == src, jnp.broadcast_to(placement_row, (128, 128)), 0.0), axis=1, keepdims=True)
    return col, to_row(col)


def own_ids(member_rows, group):
    lane = lax.broadcasted_iota(jnp.int32, (16, 128), 1)
    sub = lax.broadcasted_iota(jnp.int32, (16, 128), 0)
    k = lax.shift_right_logical(sub, 2)
    rows = jnp.zeros((16, 128), F32)
    for i in range(4):
        rows = jnp.where(k == i, jnp.broadcast_to(member_rows[i], (16, 128)), rows)
    return jnp.sum(jnp.where(lane == 4 * group + lax.bitwise_and(sub, 3), rows, 0.0), axis=1, keepdims=True)


def low_half(shape):
    return lax.broadcasted_iota(jnp.int32, shape, 1) < 64


def swap(x):
    return pltpu.roll(x, 64, 1)


def doubled(x, upper):
    mask = low_half(x.shape)
    return jnp.where(mask, swap(x), x) if upper else jnp.where(mask, x, swap(x))


def segment(x, k):
    y = jnp.where(k >= 2.0, x[:, 256:], x[:, :256])
    return jnp.where((k == 1.0) | (k == 3.0), y[:, 128:], y[:, :128])


def quadrupled(x):
    return jnp.concatenate([doubled(x[:, :128], False), doubled(x[:, :128], True),
                            doubled(x[:, 128:], False), doubled(x[:, 128:], True)], axis=1)


def thrice(x):
    high, low = split2(x)
    return jnp.concatenate([high, low, high], axis=1)


def up_of(up_ref, i):
    h = up_ref[8 * i : 8 * i + 8, :]
    return jnp.concatenate([h, h], axis=0)


def total(parts):
    while len(parts) > 1:
        parts = [parts[i] + parts[i + 1] for i in range(0, len(parts), 2)]
    return parts[0]


def cell_sums(u, factor_ref, up_ref):
    v = [None] * 8
    for t in range(16):
        part = u[:, 128 * t : 128 * t + 128]
        for i in range(8):
            term = part * up_of(up_ref, 8 * t + i)
            v[i] = term if t == 0 else v[i] + term
    return dot(thrice(jnp.concatenate(v, axis=0)), factor_ref[CELL : CELL + 384, :])


def cell_back(e, factor_ref, up_ref):
    high = e.astype(BF16).astype(F32)
    lane = lax.broadcasted_iota(jnp.int32, e.shape, 1)
    x = jnp.where(lax.shift_right_logical(lane, 5) == 1, e - high, high).astype(BF16)
    z = dot(x, factor_ref[BACK : BACK + 128, :])
    z = [z[16 * i : 16 * i + 16] for i in range(8)]
    return jnp.concatenate(
        [total([z[i] * up_of(up_ref, 8 * t + i) for i in range(8)]) for t in range(16)], axis=1)


def ordered(mass, factor_ref):
    x = jnp.concatenate(split3(mass), axis=0)
    out = []
    for i in range(8):
        p = dot(x, factor_ref[ORDER + 256 * i : ORDER + 256 * i + 256, :])
        out.append((p[:16] + p[16:32]) + p[32:])
    return jnp.concatenate(out, axis=0)


def sums(u, factor_ref, up_ref):
    x = thrice(jnp.concatenate([u[:, 128 * t : 128 * t + 128] for t in range(16)], axis=0))
    p = dot(x, factor_ref[BASIC : BASIC + 384, :])
    s = total([p[16 * t : 16 * t + 16] * up_of(up_ref, 128 + t) for t in range(16)])
    return s + swap(s)


def cols(e, factor_ref, up_ref):
    x = jnp.concatenate([e * up_of(up_ref, 128 + t) for t in range(16)], axis=0)
    d = dot(thrice(x), factor_ref[BASIC_BACK : BASIC_BACK + 384, :])
    return jnp.concatenate([d[16 * t : 16 * t + 16] for t in range(16)], axis=1)


def halves(e):
    return jnp.concatenate(split2(e), axis=0)


def cell_cols(e, whole):
    n = e.shape[0] // 2
    p = dot(e, whole[:256])
    return p[:n] + p[n:] + dot(e[:n], whole[256:512])


def basic_cols(e, whole):
    n = e.shape[0] // 2
    p = dot(e, whole[512:])
    return p[:n] + p[n:]


def nearness(centre, y):
    return jnp.exp(-200.0 * ((centre[0] - y[0]) ** 2 + (centre[1] - y[1]) ** 2))


def balanced(mass, s):
    return mass * (jnp.concatenate([s[CENTRE]] * 8, axis=0) / s)


def sweep_a(log_b, mass, d, factor_ref, up_ref, beside):
    b = jnp.exp(log_b - jnp.max(log_b, axis=1, keepdims=True))
    for i in range(3):
        beside(i)
        u = b / d
        s = cell_sums(u, factor_ref, up_ref)
        d = cell_back(balanced(mass, s), factor_ref, up_ref)
    return u, s[CENTRE], d


def over_k(x, op):
    y = op(x[:8], x[8:])
    return op(y, pltpu.roll(y, 4, 0))


def twice(x):
    return jnp.concatenate([x, x], axis=0)


def column_part(r, top, d):
    q = r - top
    peak = over_k(q, jnp.maximum)
    return peak + jnp.log(over_k(jnp.exp(q - twice(peak)) * d, jnp.add))


def sweep_b(log_b, mass, r, part, factor_ref, up_ref, beside):
    for i in range(3):
        beside(5 + i)
        v = r + twice(log_b - part)
        top = jnp.max(v, axis=1, keepdims=True)
        e = mass / sums(jnp.exp(v - top), factor_ref, up_ref)
        if i < 2:
            part = column_part(r, top, cols(e, factor_ref, up_ref))
    return e, top


def solve_pair(log_b_a, mass_a, mass_b, ids, d, part, factor_ref, up_ref, send_ref, beside=lambda i: None):
    y = targets(0, W)
    at_cell = cell_centre(jnp.floor(ids / 4.0))
    at_basic = basic_centre(ids)
    shift = (400.0 * (at_basic[1] - at_cell[1])) * y[1]
    u, centre, d_a = sweep_a(log_b_a, mass_a, d, factor_ref, up_ref, beside)
    e_first = mass_b * (centre / sums(u * jnp.exp(shift), factor_ref, up_ref))
    beside(3)
    d_first = cols(e_first, factor_ref, up_ref)
    v = log_b_a - jnp.log(d_a) + shift
    peak = over_k(v, jnp.maximum)
    beside(4)
    log_b_b = peak + jnp.log(over_k(jnp.exp(v - twice(peak)) * d_first, jnp.add))
    e_second, top = sweep_b(log_b_b, mass_b, tilt(at_basic, y), part, factor_ref, up_ref, beside)
    rows = jnp.where(low_half((16, 128)), e_first, jnp.log(e_second) - top)
    for i in range(32):
        send_ref[i, :, :] = rows


def member_rows_of(members_ref):
    members = members_ref[...].astype(F32)
    return [to_row(members[:, k : k + 1]) for k in range(4)]


def exchange_ids(members_ref):
    members = members_ref[...].astype(F32)
    slot = lax.broadcasted_iota(jnp.int32, (128, 128), 0)
    lane = lax.broadcasted_iota(jnp.int32, (128, 128), 1)
    k = lax.bitwise_and(lax.shift_right_logical(lane, 2), 3)
    value = jnp.broadcast_to(members[:, 0:1], (128, 128))
    for i in range(1, 4):
        value = jnp.where(k == i, jnp.broadcast_to(members[:, i : i + 1], (128, 128)), value)
    of_lane = 4 * lax.shift_right_logical(lane, 4) + lax.bitwise_and(lane, 3)
    return jnp.concatenate(
        [jnp.sum(jnp.where(slot == of_lane + 32 * t, value, 0.0), axis=0, keepdims=True) for t in range(4)], axis=1)


def near_cells(want, member_rows, cell_row, exchanged, cells_ref, groups_ref, rows_ref, ids_ref):
    hits = [jnp.where(row == want, 1.0, 0.0) for row in member_rows]
    slot = (hits[0] + hits[1]) + (hits[2] + hits[3])
    ids = jnp.concatenate([jnp.sum(slot * row, axis=1, keepdims=True) for row in member_rows], axis=0)
    cell = jnp.floor(ids / 4.0)
    cells = jnp.where(cell_row == cell, 1.0, 0.0)
    cells_ref[...] = cells.astype(BF16)
    for k in range(4):
        groups_ref[256 * k : 256 * k + 256, :] = jnp.where(exchanged == 4.0 * cell + float(k), 1.0, 0.0).astype(BF16)
    ids = jnp.concatenate([ids, want], axis=0)
    rows_ref[...] = jnp.where(exchanged == ids, 1.0, 0.0).astype(BF16)
    ids_ref[...] = jnp.broadcast_to(ids, (320, 128))
    return ids, cells


def start_kernel(place_ref, placement_ref, members_ref, factor_ref, up_ref, sum_a_ref, sum_b_ref, keep_ref, keep_up_ref, own_ids_ref, onehot_ref,
                 cell_ref, cells_ref, groups_ref, rows_ref, ids_ref):
    cell_col, cell_row = local_cells(placement_ref[...].astype(F32), place_ref[0])
    member_rows = member_rows_of(members_ref)
    ids = own_ids(member_rows, place_ref[1])
    y = targets(0, W)
    sum_a_ref[...] = cell_sums(nearness(cell_centre(jnp.floor(ids / 4.0)), y), factor_ref, up_ref)
    sum_b_ref[...] = sums(nearness(basic_centre(ids), y), factor_ref, up_ref)
    keep_ref[...] = factor_ref[...]
    keep_up_ref[...] = up_ref[...]
    own_ids_ref[...] = jnp.broadcast_to(ids, (16, 128))
    cells = jnp.floor(ids / 4.0)
    onehot_ref[...] = jnp.where(cell_row == cells, 1.0, 0.0)
    cell_ref[...] = jnp.broadcast_to(cell_col, (128, 128))
    want = jnp.concatenate([4.0 * cells + float(k) for k in range(4)], axis=0)
    near_cells(want, member_rows, cell_row, exchange_ids(members_ref), cells_ref, groups_ref, rows_ref, ids_ref)


def first_kernel(place_ref, own_ref, other_ref, sum_a_ref, sum_b_ref, ids_ref, onehot_ref, cell_ref, cells_ref, near_ref,
                 factor_ref, up_ref, send_ref, here_ref, level_ref, mass_a_ref, mass_b_ref, d_ref, part_ref, table_ref):
    ids, onehot = ids_ref[:, :1], onehot_ref[...]
    mass = []
    for part in (16, 17):
        rows = jnp.concatenate([own_ref[:, part, :], other_ref[:, part, :]], axis=0)
        mass.append(pick(onehot, rows))
    mass = jnp.concatenate(mass, axis=1)
    mass_a = ordered(mass, factor_ref)
    mass_b = segment(quadrupled(mass), ids - 4.0 * jnp.floor(ids / 4.0))
    d = cell_back(balanced(mass_a, sum_a_ref[...]), factor_ref, up_ref)
    log_b = []
    for t in range(16):
        rows = [ref[x * 16 + t, 0:16, :] for ref in (own_ref, other_ref) for x in range(4)]
        rows = jnp.concatenate(rows, axis=0)
        table_ref[:, 128 * t : 128 * t + 128] = rows
        log_b.append(pick(onehot, rows))
    here_ref[...] = table_ref[:, pl.ds(pl.multiple_of(place_ref[2] * 128, 128), 128)]
    log_b = jnp.concatenate(log_b, axis=1)
    at_basic = basic_centre(ids)
    top = 200.0 * (at_basic[0] * at_basic[0] + at_basic[1] * at_basic[1])
    part = column_part(tilt(at_basic, targets(0, W)), top, cols(mass_b / sum_b_ref[...], factor_ref, up_ref))
    mass_a_ref[...] = mass_a
    mass_b_ref[...] = mass_b
    d_ref[...] = d
    part_ref[...] = part
    near, cell_col = near_ref[0:256, :1], cell_ref[:, :1]

    def level(block):
        at = slice(256 * block, 256 * block + 256)
        level_ref[:, at] = near_level(near, cells_ref[...], table_ref[:, at], cell_col, targets(256 * block, 256))

    solve_pair(log_b, mass_a, mass_b, ids, d, part, factor_ref, up_ref, send_ref, level)


def received(recv_ref):
    return [jnp.concatenate([recv_ref[g, 4 * k : 4 * k + 4, :] for g in range(32)], axis=0) for k in range(4)]


def high_top(x):
    return jnp.max(jnp.where(low_half(x.shape), -jnp.inf, x), axis=1, keepdims=True)


def unpack(f):
    top = -high_top(f)
    return doubled(f, False), jnp.exp(doubled(f, True) + top), top


def a_rows(member_rows, cell_col, k):
    want = 4.0 * cell_col + float(k)
    return jnp.concatenate([jnp.where(row == want, 1.0, 0.0) for row in member_rows], axis=1).astype(BF16)


def packed(f):
    high, low = split2(f)
    return jnp.where(low_half(f.shape), high.astype(F32), swap(low.astype(F32))).astype(BF16)


def cell_halves(by_k):
    mask = low_half(by_k[0].shape)
    high = [jnp.where(mask, by_k[i], swap(by_k[i + 1])) for i in (0, 2)]
    low = [jnp.where(mask, swap(by_k[i]), by_k[i + 1]) for i in (0, 2)]
    return jnp.concatenate([jnp.concatenate(high, axis=1), jnp.concatenate(low, axis=1)], axis=0).astype(BF16)


def mix(v, d):
    peak = jnp.maximum(jnp.maximum(v[0], v[1]), jnp.maximum(v[2], v[3]))
    z = [jnp.exp(a - peak) * b for a, b in zip(v, d)]
    return peak + jnp.log((z[0] + z[1]) + (z[2] + z[3]))


def near_level(ids, cells, log_b, cell_col, y):
    return pick(cells, log_b - tilt(cell_centre(cell_col), y)) + tilt(basic_centre(ids), y)


def gathered(recv_ref, groups_ref, rows_ref):
    f = recv_ref[...].reshape(512, 128)
    by_k = dot(groups_ref[...], packed(f))
    o = rows_ref[...]
    high, mid, low = split3(f)
    e0, e1, top = unpack((dot(o, high) + dot(o, mid)) + dot(o, low))
    by_k = [by_k[256 * k : 256 * k + 256] for k in range(4)]
    return cell_halves(by_k), halves(e0[:256]), halves(e1), top


def near_margins(gather, level, centre, y, whole):
    e_cell, e0, e1, top = gather
    parts = [slice(64 * k, 64 * k + 64) for k in range(4)]
    v = level - jnp.log(cell_cols(e_cell, whole))
    d0 = basic_cols(e0, whole)
    d1 = basic_cols(e1, whole)
    q = tilt(centre, y) - top
    log_b = mix([v[a] for a in parts], [d0[a] for a in parts])
    gamma = log_b - mix([q[a] for a in parts], [d1[a] for a in parts])
    return gamma + q[256:], d1[256:]


def second_kernel(place_ref, own_ids_ref, recv_ref, level_ref, groups_ref, rows_ref, ids_ref, mass_a_ref, mass_b_ref, d_ref,
                  part_ref, factor_ref, up_ref, whole_ref, send_ref, here_ref):
    here_ref[...] = whole_ref[:, pl.ds(pl.multiple_of(place_ref[2] * 128, 128), 128)]
    gather = gathered(recv_ref, groups_ref, rows_ref)
    centre = basic_centre(ids_ref[:, :1])
    log_b = []
    for block in range(8):
        at = slice(block * 256, block * 256 + 256)
        v, d = near_margins(gather, level_ref[:, at], centre, targets(256 * block, 256), whole_ref[:, at])
        log_b.append(mix([v[16 * k : 16 * k + 16] for k in range(4)], [d[16 * k : 16 * k + 16] for k in range(4)]))
    solve_pair(jnp.concatenate(log_b, axis=1), mass_a_ref[...], mass_b_ref[...], own_ids_ref[:, :1], d_ref[...], part_ref[...],
               factor_ref, up_ref, send_ref)


def middle_kernel(place_ref, placement_ref, members_ref, log_b_ref, recv_ref, whole_ref, level_ref, cells_ref, groups_ref,
                  rows_ref, ids_ref):
    cell_col, cell_row = local_cells(placement_ref[...].astype(F32), place_ref[0])
    member_rows = member_rows_of(members_ref)
    members = members_ref[...].astype(F32)
    share = place_ref[2]
    y = targets(share * 128, 128)
    whole = whole_ref[...]
    b_ids = [members[:, k : k + 1] for k in range(4)]
    b_cell = jnp.concatenate([jnp.where(cell_row == jnp.floor(i / 4.0), 1.0, 0.0) for i in b_ids], axis=0)
    b_tilt = [tilt(basic_centre(i), y) for i in b_ids]
    a_tilt = [tilt(basic_centre(4.0 * cell_col + float(k)), y) for k in range(4)]
    parts = [slice(128 * k, 128 * k + 128) for k in range(4)]
    every = jnp.concatenate(received(recv_ref), axis=0)
    hits = [a_rows(member_rows, cell_col, k) for k in range(4)]
    rows = packed(every)
    e_cell = cell_halves([dot(h, rows) for h in hits])
    by_k = jnp.concatenate([pick(h, every) for h in hits], axis=0)
    gamma = pick(b_cell, log_b_ref[...] - jnp.log(cell_cols(e_cell, whole)) - tilt(cell_centre(cell_col), y))
    e0, e1, top = unpack(every)
    _, ea, a_top = unpack(by_k)
    d0, d1, da = [basic_cols(halves(e), whole) for e in (e0, e1, ea)]
    log_b1 = mix([gamma[a] + t for a, t in zip(parts, b_tilt)], [d0[a] for a in parts])
    gamma1 = log_b1 - mix([t - top[a] for a, t in zip(parts, b_tilt)], [d1[a] for a in parts])
    log_b = []
    for k in range(4):
        hit = hits[k].astype(F32)
        slot = (hit[:, :128] + hit[:, 128:256]) + (hit[:, 256:384] + hit[:, 384:])
        log_b.append(pick(slot, gamma1) + a_tilt[k] - a_top[parts[k]])
    log_b = mix(log_b, [da[a] for a in parts])
    lane = lax.broadcasted_iota(jnp.int32, (16, 128), 1)
    first = place_ref[3] * 16 + lax.broadcasted_iota(jnp.int32, (16, 128), 0)
    own_cells = jnp.sum(jnp.where(lane == first, jnp.broadcast_to(cell_row, (16, 128)), 0.0), axis=1, keepdims=True)
    want = jnp.concatenate([4.0 * own_cells + float(k) for k in range(4)], axis=0)
    ids, cells = near_cells(want, member_rows, cell_row, exchange_ids(members_ref), cells_ref, groups_ref, rows_ref, ids_ref)
    level_ref[...] = near_level(ids[:256], cells, log_b, cell_col, y)


def last_kernel(place_ref, recv_ref, level_ref, groups_ref, rows_ref, ids_ref, whole_ref, out_ref):
    centre = basic_centre(ids_ref[:, :1])
    v, d = near_margins(gathered(recv_ref, groups_ref, rows_ref), level_ref[...], centre,
                        targets(place_ref[2] * 128, 128), whole_ref[...])
    out = jnp.exp(v + jnp.log(d))
    for k in range(4):
        out_ref[:, k, :] = out[16 * k : 16 * k + 16]


def call(body, inputs, outs, scratch=(), work=1):
    def spec(value):
        return pl.BlockSpec(memory_space=pltpu.SMEM if value.shape == (4,) else pltpu.VMEM)

    return pl.pallas_call(
        body,
        out_shape=[jax.ShapeDtypeStruct(s[:-1], BF16) if s[-1] is BF16 else jax.ShapeDtypeStruct(s, F32) for s in outs],
        in_specs=[spec(value) for value in inputs],
        out_specs=[pl.BlockSpec(memory_space=pltpu.VMEM)] * len(outs),
        scratch_shapes=list(scratch),
        compiler_params=pltpu.CompilerParams(vmem_limit_bytes=24 * 2**20),
        cost_estimate=pl.CostEstimate(flops=work * 10**9, bytes_accessed=10**6, transcendentals=0),
    )(*inputs)


FACTORS = [(3328, 128, BF16), (1152, 128)]
NEAR = [(256, 128, BF16), (1024, 512, BF16), (320, 512, BF16), (320, 128)]


def on_device(placement_a, members_b, source_mass, init_log, factors, wholes, ups):
    x, c, z, y = (lax.axis_index(name) for name in ("x", "c", "z", "y"))
    share = z * 4 + y
    place = jnp.stack([c, x * 8 + c * 4 + y, share, x]).astype(jnp.int32)
    index = (place, placement_a.reshape(1, 128), members_b)
    v = [init_log[:, k, :] for k in range(4)]
    peak = jnp.maximum(jnp.maximum(v[0], v[1]), jnp.maximum(v[2], v[3]))
    e = [jnp.exp(a - peak) for a in v]
    log_b = peak + jnp.log((e[0] + e[1]) + (e[2] + e[3])) + float(np.log(64.0 / W))
    mass = lax.dynamic_slice_in_dim(source_mass, share, 1, 0).reshape(2, 128)
    block = jnp.concatenate([log_b, mass, jnp.zeros((6, 128), F32)], axis=0)
    own = lax.all_to_all(jnp.broadcast_to(block[None], (64, 24, 128)), ("x", "z", "y"), 0, 0, tiled=True)
    sum_a, sum_b, factors, ups, held, onehot, cell, cells, groups, rows, ids = call(
        start_kernel, index + (factors, ups), [(128, 128), (16, 128)] + FACTORS + [(16, 128), (16, 128), (128, 128)] + NEAR)
    other = lax.ppermute(own, "c", [(0, 1), (1, 0)])

    def exchange(rows):
        return lax.all_to_all(rows, ("x", "c", "y"), 0, 0, tiled=True)

    send, here, level, *rest = call(
        first_kernel, (place, own, other, sum_a, sum_b, held, onehot, cell, cells, ids, factors, ups),
        [(32, 16, 128), (128, 128), (256, W), (128, 128), (16, 128), (16, W), (8, W)], [pltpu.VMEM((128, W), F32)])
    first = exchange(send)
    send, whole = call(second_kernel, (place, held, first, level, groups, rows, ids, *rest, factors, ups, wholes),
                       [(32, 16, 128), (640, 128, BF16)])
    second = exchange(send)
    level, _, groups, rows, ids = call(middle_kernel, index + (here, first, whole), [(256, 128)] + NEAR)
    (out,) = call(last_kernel, (place, second, level, groups, rows, ids, whole), [(16, 4, 128)])
    return out


def solution(mesh):
    split = Mesh(mesh.devices.reshape(4, 2, 4, 4), ("x", "c", "z", "y"))
    tables = _tables()
    placed = (P(), P(), P(("x", "c"), None), P(("x", "c"), None, ("z", "y"))) + (P(),) * len(tables)
    body = jax.shard_map(
        on_device, mesh=split, in_specs=placed, out_specs=P(("x", "c"), None, ("z", "y")), check_vma=False
    )

    def run(placement_a, members_b, source_mass, init_log):
        return body(placement_a, members_b, source_mass, init_log, *(jnp.asarray(t) for t in tables))

    return run
```

```python
import numpy as np
import ml_dtypes

import jax
import jax.numpy as jnp
from jax import lax
from jax.experimental import pallas as pl
from jax.experimental.pallas import tpu as pltpu
from jax.sharding import Mesh, PartitionSpec as P

F32 = jnp.float32
BF16 = jnp.bfloat16
W = 2048
CENTRE = (slice(48, 64), slice(15, 16))


def _halves(matrix):
    high = matrix.astype(ml_dtypes.bfloat16)
    low = (matrix - high.astype(np.float64)).astype(ml_dtypes.bfloat16)
    return high, low


def _thrice(matrix):
    high, low = _halves(matrix)
    return np.concatenate([high, high, low], axis=0)


def _tables():
    yh = (np.arange(32) + 0.5) / 32 - 0.5
    ya = (np.arange(64) + 0.5) / 64 - 0.5
    dh = (np.arange(8) - 3.5) / 128
    da = (np.arange(8) - 3.5) / 256
    shifts = [(k - 1.5) / 32 for k in range(4)]

    def whole(shift):
        up = np.exp(400.0 * dh[:, None] * yh[None])
        along = np.exp(400.0 * (da + shift)[:, None] * ya[None])
        return (up[:, None, :, None] * along[None, :, None, :]).reshape(64, W)

    def along(shift):
        part = np.zeros((2, 64, 2, 8, 8))
        for h in range(2):
            part[h, :, h] = np.exp(400.0 * ya[:, None] * (da + shift)[None])[:, None, :]
        return part.reshape(128, 128)

    cell = np.concatenate([np.exp(400.0 * ya[:, None] * (da + s)[None]) for s in shifts], axis=1)
    high, low = _halves(np.concatenate([cell.T, cell.T], axis=1))
    order = np.zeros((8, 4, 8, 8, 4, 4, 8), ml_dtypes.bfloat16)
    for i, k, r in np.ndindex(8, 4, 8):
        order[i, k, i, r, :, k, r] = 1
    factors = [
        _thrice(np.tile(cell, (2, 4))),
        np.concatenate([high, high, low, np.zeros_like(low)], axis=0),
        _thrice(along(0.0)),
        _thrice(along(0.0).T),
        order.reshape(2048, 128),
    ]
    high, low = _halves(whole(0.0))
    wholes = _halves(np.concatenate([whole(s) for s in shifts], axis=0)) + (high, high, low, np.zeros_like(low))
    up = np.exp(400.0 * yh.reshape(16, 2, 1) * dh[None, None])
    of_row = np.repeat(up.transpose(0, 2, 1).reshape(128, 1, 2), 64, axis=2)
    of_pixel = np.repeat(up.reshape(16, 1, 16), 8, axis=2)
    ups = np.repeat(np.concatenate([of_row, of_pixel], axis=0), 8, axis=1).reshape(1152, 128)
    return np.concatenate(factors, axis=0), np.concatenate(wholes, axis=0), ups.astype(np.float32)


CELL, BACK, BASIC, BASIC_BACK, ORDER = 0, 384, 512, 896, 1280


def dot(a, b):
    return jnp.dot(a, b, preferred_element_type=F32)


def split2(x):
    high = x.astype(BF16)
    return high, (x - high.astype(F32)).astype(BF16)


def split3(x):
    high = x.astype(BF16)
    rest = x - high.astype(F32)
    mid = rest.astype(BF16)
    return high, mid, (rest - mid.astype(F32)).astype(BF16)


def pick(onehot, x):
    o = onehot.astype(BF16)
    return dot(jnp.concatenate([o, o, o], axis=1), jnp.concatenate(split3(x), axis=0))


def targets(first, count):
    j = first + lax.broadcasted_iota(jnp.int32, (1, count), 1)
    yh = (lax.shift_right_logical(j, 6).astype(F32) + 0.5) / 32.0 - 0.5
    ya = (lax.bitwise_and(j, 63).astype(F32) + 0.5) / 64.0 - 0.5
    return yh, ya


def basic_centre(ids):
    row = jnp.floor(ids / 32.0)
    return (row * 8.0 + 4.0) / 128.0 - 0.5, ((ids - row * 32.0) * 8.0 + 4.0) / 256.0 - 0.5


def cell_centre(cells):
    row = jnp.floor(cells / 8.0)
    return (row * 8.0 + 4.0) / 128.0 - 0.5, ((cells - row * 8.0) * 32.0 + 16.0) / 256.0 - 0.5


def tilt(centre, y):
    return (400.0 * centre[0]) * y[0] + (400.0 * centre[1]) * y[1]


def eye_mask():
    return lax.broadcasted_iota(jnp.int32, (128, 128), 0) == lax.broadcasted_iota(jnp.int32, (128, 128), 1)


def to_col(row):
    return jnp.sum(jnp.where(eye_mask(), jnp.broadcast_to(row, (128, 128)), 0.0), axis=1, keepdims=True)


def to_row(col):
    return jnp.sum(jnp.where(eye_mask(), jnp.broadcast_to(col, (128, 128)), 0.0), axis=0, keepdims=True)


def local_cells(placement_row, core):
    dst = lax.broadcasted_iota(jnp.int32, (128, 128), 0)
    src = lax.broadcasted_iota(jnp.int32, (128, 128), 1)
    side = lax.bitwise_xor(lax.shift_right_logical(dst, 6), core)
    slot = lax.bitwise_and(lax.shift_right_logical(dst, 4), 3) * 32 + side * 16 + lax.bitwise_and(dst, 15)
    col = jnp.sum(jnp.where(slot == src, jnp.broadcast_to(placement_row, (128, 128)), 0.0), axis=1, keepdims=True)
    return col, to_row(col)


def own_ids(member_rows, group):
    lane = lax.broadcasted_iota(jnp.int32, (16, 128), 1)
    sub = lax.broadcasted_iota(jnp.int32, (16, 128), 0)
    k = lax.shift_right_logical(sub, 2)
    rows = jnp.zeros((16, 128), F32)
    for i in range(4):
        rows = jnp.where(k == i, jnp.broadcast_to(member_rows[i], (16, 128)), rows)
    return jnp.sum(jnp.where(lane == 4 * group + lax.bitwise_and(sub, 3), rows, 0.0), axis=1, keepdims=True)


def low_half(shape):
    return lax.broadcasted_iota(jnp.int32, shape, 1) < 64


def swap(x):
    return pltpu.roll(x, 64, 1)


def doubled(x, upper):
    mask = low_half(x.shape)
    return jnp.where(mask, swap(x), x) if upper else jnp.where(mask, x, swap(x))


def segment(x, k):
    y = jnp.where(k >= 2.0, x[:, 256:], x[:, :256])
    return jnp.where((k == 1.0) | (k == 3.0), y[:, 128:], y[:, :128])


def quadrupled(x):
    return jnp.concatenate([doubled(x[:, :128], False), doubled(x[:, :128], True),
                            doubled(x[:, 128:], False), doubled(x[:, 128:], True)], axis=1)


def thrice(x):
    high, low = split2(x)
    return jnp.concatenate([high, low, high], axis=1)


def up_of(up_ref, i):
    h = up_ref[8 * i : 8 * i + 8, :]
    return jnp.concatenate([h, h], axis=0)


def total(parts):
    while len(parts) > 1:
        parts = [parts[i] + parts[i + 1] for i in range(0, len(parts), 2)]
    return parts[0]


def cell_sums(u, factor_ref, up_ref):
    v = [None] * 8
    for t in range(16):
        part = u[:, 128 * t : 128 * t + 128]
        for i in range(8):
            term = part * up_of(up_ref, 8 * t + i)
            v[i] = term if t == 0 else v[i] + term
    return dot(thrice(jnp.concatenate(v, axis=0)), factor_ref[CELL : CELL + 384, :])


def cell_back(e, factor_ref, up_ref):
    high = e.astype(BF16).astype(F32)
    lane = lax.broadcasted_iota(jnp.int32, e.shape, 1)
    x = jnp.where(lax.shift_right_logical(lane, 5) == 1, e - high, high).astype(BF16)
    z = dot(x, factor_ref[BACK : BACK + 128, :])
    z = [z[16 * i : 16 * i + 16] for i in range(8)]
    return jnp.concatenate(
        [total([z[i] * up_of(up_ref, 8 * t + i) for i in range(8)]) for t in range(16)], axis=1)


def ordered(mass, factor_ref):
    x = jnp.concatenate(split3(mass), axis=0)
    out = []
    for i in range(8):
        p = dot(x, factor_ref[ORDER + 256 * i : ORDER + 256 * i + 256, :])
        out.append((p[:16] + p[16:32]) + p[32:])
    return jnp.concatenate(out, axis=0)


def sums(u, factor_ref, up_ref):
    x = thrice(jnp.concatenate([u[:, 128 * t : 128 * t + 128] for t in range(16)], axis=0))
    p = dot(x, factor_ref[BASIC : BASIC + 384, :])
    s = total([p[16 * t : 16 * t + 16] * up_of(up_ref, 128 + t) for t in range(16)])
    return s + swap(s)


def cols(e, factor_ref, up_ref):
    x = jnp.concatenate([e * up_of(up_ref, 128 + t) for t in range(16)], axis=0)
    d = dot(thrice(x), factor_ref[BASIC_BACK : BASIC_BACK + 384, :])
    return jnp.concatenate([d[16 * t : 16 * t + 16] for t in range(16)], axis=1)


def wide(e):
    high = e.astype(BF16).astype(F32)
    return jnp.concatenate([jnp.where(low_half(e.shape), high, e - high), high], axis=1).astype(BF16)


def cell_cols(e, whole):
    n = e.shape[0] // 2
    p = dot(e, whole[:256])
    return p[:n] + p[n:] + dot(e[:n], whole[256:512])


def basic_cols(e, whole):
    return dot(e, whole[512:])


def nearness(centre, y):
    return jnp.exp(-200.0 * ((centre[0] - y[0]) ** 2 + (centre[1] - y[1]) ** 2))


def balanced(mass, s):
    return mass * (jnp.concatenate([s[CENTRE]] * 8, axis=0) / s)


def sweep_a(log_b, mass, d, factor_ref, up_ref, beside):
    b = jnp.exp(log_b - jnp.max(log_b, axis=1, keepdims=True))
    for i in range(3):
        beside(i)
        u = b / d
        s = cell_sums(u, factor_ref, up_ref)
        d = cell_back(balanced(mass, s), factor_ref, up_ref)
    return u, s[CENTRE], d


def over_k(x, op):
    y = op(x[:8], x[8:])
    return op(y, pltpu.roll(y, 4, 0))


def twice(x):
    return jnp.concatenate([x, x], axis=0)


def column_part(r, top, d):
    q = r - top
    peak = over_k(q, jnp.maximum)
    return peak + jnp.log(over_k(jnp.exp(q - twice(peak)) * d, jnp.add))


def sweep_b(log_b, mass, r, part, factor_ref, up_ref, beside):
    for i in range(3):
        beside(5 + i)
        v = r + twice(log_b - part)
        top = jnp.max(v, axis=1, keepdims=True)
        e = mass / sums(jnp.exp(v - top), factor_ref, up_ref)
        if i < 2:
            part = column_part(r, top, cols(e, factor_ref, up_ref))
    return e, top


def solve_pair(log_b_a, mass_a, mass_b, ids, d, part, factor_ref, up_ref, send_ref, beside=lambda i: None):
    y = targets(0, W)
    at_cell = cell_centre(jnp.floor(ids / 4.0))
    at_basic = basic_centre(ids)
    shift = (400.0 * (at_basic[1] - at_cell[1])) * y[1]
    u, centre, d_a = sweep_a(log_b_a, mass_a, d, factor_ref, up_ref, beside)
    e_first = mass_b * (centre / sums(u * jnp.exp(shift), factor_ref, up_ref))
    beside(3)
    d_first = cols(e_first, factor_ref, up_ref)
    v = log_b_a - jnp.log(d_a) + shift
    peak = over_k(v, jnp.maximum)
    beside(4)
    log_b_b = peak + jnp.log(over_k(jnp.exp(v - twice(peak)) * d_first, jnp.add))
    e_second, top = sweep_b(log_b_b, mass_b, tilt(at_basic, y), part, factor_ref, up_ref, beside)
    rows = jnp.where(low_half((16, 128)), e_first, jnp.log(e_second) - top)
    for i in range(32):
        send_ref[i, :, :] = rows


def member_rows_of(members_ref):
    members = members_ref[...].astype(F32)
    return [members[k : k + 1, :] for k in range(4)]


def exchange_ids(member_rows):
    members = [to_col(row) for row in member_rows]
    slot = lax.broadcasted_iota(jnp.int32, (128, 128), 0)
    lane = lax.broadcasted_iota(jnp.int32, (128, 128), 1)
    k = lax.bitwise_and(lax.shift_right_logical(lane, 2), 3)
    value = jnp.broadcast_to(members[0], (128, 128))
    for i in range(1, 4):
        value = jnp.where(k == i, jnp.broadcast_to(members[i], (128, 128)), value)
    of_lane = 4 * lax.shift_right_logical(lane, 4) + lax.bitwise_and(lane, 3)
    return jnp.concatenate(
        [jnp.sum(jnp.where(slot == of_lane + 32 * t, value, 0.0), axis=0, keepdims=True) for t in range(4)], axis=1)


def near_cells(want, member_rows, cell_row, exchanged, cells_ref, groups_ref, rows_ref, ids_ref):
    hits = [jnp.where(row == want, 1.0, 0.0) for row in member_rows]
    slot = (hits[0] + hits[1]) + (hits[2] + hits[3])
    ids = jnp.concatenate([jnp.sum(slot * row, axis=1, keepdims=True) for row in member_rows], axis=0)
    cell = jnp.floor(ids / 4.0)
    cells = jnp.where(cell_row == cell, 1.0, 0.0)
    cells_ref[...] = cells.astype(BF16)
    for k in range(4):
        groups_ref[256 * k : 256 * k + 256, :] = jnp.where(exchanged == 4.0 * cell + float(k), 1.0, 0.0).astype(BF16)
    ids = jnp.concatenate([ids, want], axis=0)
    rows_ref[...] = jnp.where(exchanged == ids, 1.0, 0.0).astype(BF16)
    ids_ref[...] = jnp.broadcast_to(ids, (320, 128))
    return ids, cells


def start_kernel(place_ref, placement_hbm, members_hbm, factor_hbm, up_hbm, sum_a_ref, sum_b_ref, factor_ref, up_ref, own_ids_ref, onehot_ref,
                 cell_ref, cells_ref, groups_ref, rows_ref, ids_ref, placement_ref, members_ref, sems):
    pairs = ((placement_hbm, placement_ref), (members_hbm, members_ref), (factor_hbm, factor_ref), (up_hbm, up_ref))
    copies = [pltpu.make_async_copy(*pair, sems.at[i]) for i, pair in enumerate(pairs)]
    for copy in copies:
        copy.start()
    for copy in copies[:2]:
        copy.wait()
    cell_col, cell_row = local_cells(placement_ref[...].astype(F32), place_ref[0])
    member_rows = member_rows_of(members_ref)
    ids = own_ids(member_rows, place_ref[1])
    own_ids_ref[...] = jnp.broadcast_to(ids, (16, 128))
    cells = jnp.floor(ids / 4.0)
    onehot_ref[...] = jnp.where(cell_row == cells, 1.0, 0.0)
    cell_ref[...] = jnp.broadcast_to(cell_col, (128, 128))
    want = jnp.concatenate([4.0 * cells + float(k) for k in range(4)], axis=0)
    near_cells(want, member_rows, cell_row, exchange_ids(member_rows), cells_ref, groups_ref, rows_ref, ids_ref)
    for copy in copies[2:]:
        copy.wait()
    y = targets(0, W)
    sum_a_ref[...] = cell_sums(nearness(cell_centre(jnp.floor(ids / 4.0)), y), factor_ref, up_ref)
    sum_b_ref[...] = sums(nearness(basic_centre(ids), y), factor_ref, up_ref)


def first_kernel(place_ref, own_ref, other_ref, sum_a_ref, sum_b_ref, ids_ref, onehot_ref, cell_ref, cells_ref, near_ref,
                 factor_ref, up_ref, send_ref, here_ref, level_ref, mass_a_ref, mass_b_ref, d_ref, part_ref, table_ref):
    ids, onehot = ids_ref[:, :1], onehot_ref[...]
    mass = []
    for part in (16, 17):
        at = pl.ds(part, 64, stride=18)
        rows = jnp.concatenate([own_ref[at, :], other_ref[at, :]], axis=0)
        mass.append(pick(onehot, rows))
    mass = jnp.concatenate(mass, axis=1)
    mass_a = ordered(mass, factor_ref)
    mass_b = segment(quadrupled(mass), ids - 4.0 * jnp.floor(ids / 4.0))
    d = cell_back(balanced(mass_a, sum_a_ref[...]), factor_ref, up_ref)
    log_b = []
    for t in range(16):
        starts = [18 * (16 * x + t) for x in range(4)]
        rows = [ref[i : i + 16, :] for ref in (own_ref, other_ref) for i in starts]
        rows = jnp.concatenate(rows, axis=0)
        table_ref[:, 128 * t : 128 * t + 128] = rows
        log_b.append(pick(onehot, rows))
    here_ref[...] = table_ref[:, pl.ds(pl.multiple_of(place_ref[2] * 128, 128), 128)]
    log_b = jnp.concatenate(log_b, axis=1)
    at_basic = basic_centre(ids)
    top = 200.0 * (at_basic[0] * at_basic[0] + at_basic[1] * at_basic[1])
    part = column_part(tilt(at_basic, targets(0, W)), top, cols(mass_b / sum_b_ref[...], factor_ref, up_ref))
    mass_a_ref[...] = mass_a
    mass_b_ref[...] = mass_b
    d_ref[...] = d
    part_ref[...] = part
    near, cell_col = near_ref[0:256, :1], cell_ref[:, :1]

    def level(block):
        at = slice(256 * block, 256 * block + 256)
        level_ref[:, at] = near_level(near, cells_ref[...], table_ref[:, at], cell_col, targets(256 * block, 256))

    solve_pair(log_b, mass_a, mass_b, ids, d, part, factor_ref, up_ref, send_ref, level)


def received(recv_ref):
    return [jnp.concatenate([recv_ref[g, 4 * k : 4 * k + 4, :] for g in range(32)], axis=0) for k in range(4)]


def high_top(x):
    return jnp.max(jnp.where(low_half(x.shape), -jnp.inf, x), axis=1, keepdims=True)


def unpack(f):
    top = -high_top(f)
    return doubled(f, False), jnp.exp(doubled(f, True) + top), top


def a_rows(member_rows, cell_col, k):
    want = 4.0 * cell_col + float(k)
    return jnp.concatenate([jnp.where(row == want, 1.0, 0.0) for row in member_rows], axis=1).astype(BF16)


def packed(f):
    high, low = split2(f)
    return jnp.where(low_half(f.shape), high.astype(F32), swap(low.astype(F32))).astype(BF16)


def cell_halves(by_k):
    mask = low_half(by_k[0].shape)
    high = [jnp.where(mask, by_k[i], swap(by_k[i + 1])) for i in (0, 2)]
    low = [jnp.where(mask, swap(by_k[i]), by_k[i + 1]) for i in (0, 2)]
    return jnp.concatenate([jnp.concatenate(high, axis=1), jnp.concatenate(low, axis=1)], axis=0).astype(BF16)


def mix(v, d):
    peak = jnp.maximum(jnp.maximum(v[0], v[1]), jnp.maximum(v[2], v[3]))
    z = [jnp.exp(a - peak) * b for a, b in zip(v, d)]
    return peak + jnp.log((z[0] + z[1]) + (z[2] + z[3]))


def near_level(ids, cells, log_b, cell_col, y):
    return pick(cells, log_b - tilt(cell_centre(cell_col), y)) + tilt(basic_centre(ids), y)


def gathered(recv_ref, groups_ref, rows_ref):
    f = recv_ref[...].reshape(512, 128)
    by_k = dot(groups_ref[...], packed(f))
    o = rows_ref[...]
    high, mid, low = split3(f)
    two = dot(o, jnp.concatenate([high, mid], axis=1))
    e0, e1, top = unpack((two[:, :128] + two[:, 128:]) + dot(o, low))
    by_k = [by_k[256 * k : 256 * k + 256] for k in range(4)]
    return cell_halves(by_k), wide(e0[:256]), wide(e1), top


def near_margins(gather, level, centre, y, whole):
    e_cell, e0, e1, top = gather
    parts = [slice(64 * k, 64 * k + 64) for k in range(4)]
    v = level - jnp.log(cell_cols(e_cell, whole))
    d0 = basic_cols(e0, whole)
    d1 = basic_cols(e1, whole)
    q = tilt(centre, y) - top
    log_b = mix([v[a] for a in parts], [d0[a] for a in parts])
    gamma = log_b - mix([q[a] for a in parts], [d1[a] for a in parts])
    return gamma + q[256:], d1[256:]


def second_kernel(place_ref, own_ids_ref, recv_ref, level_ref, groups_ref, rows_ref, ids_ref, mass_a_ref, mass_b_ref, d_ref,
                  part_ref, factor_ref, up_ref, whole_ref, send_ref, here_ref):
    here_ref[...] = whole_ref[:, pl.ds(pl.multiple_of(place_ref[2] * 128, 128), 128)]
    gather = gathered(recv_ref, groups_ref, rows_ref)
    centre = basic_centre(ids_ref[:, :1])
    log_b = []
    for block in range(8):
        at = slice(block * 256, block * 256 + 256)
        v, d = near_margins(gather, level_ref[:, at], centre, targets(256 * block, 256), whole_ref[:, at])
        log_b.append(mix([v[16 * k : 16 * k + 16] for k in range(4)], [d[16 * k : 16 * k + 16] for k in range(4)]))
    solve_pair(jnp.concatenate(log_b, axis=1), mass_a_ref[...], mass_b_ref[...], own_ids_ref[:, :1], d_ref[...], part_ref[...],
               factor_ref, up_ref, send_ref)


def middle_kernel(place_ref, placement_ref, members_ref, log_b_ref, recv_ref, whole_ref, level_ref, cells_ref, groups_ref,
                  rows_ref, ids_ref):
    cell_col, cell_row = local_cells(placement_ref[...].astype(F32), place_ref[0])
    member_rows = member_rows_of(members_ref)
    share = place_ref[2]
    y = targets(share * 128, 128)
    whole = whole_ref[...]
    b_ids = [to_col(row) for row in member_rows]
    b_cell = jnp.concatenate([jnp.where(cell_row == jnp.floor(i / 4.0), 1.0, 0.0) for i in b_ids], axis=0)
    b_tilt = [tilt(basic_centre(i), y) for i in b_ids]
    a_tilt = [tilt(basic_centre(4.0 * cell_col + float(k)), y) for k in range(4)]
    parts = [slice(128 * k, 128 * k + 128) for k in range(4)]
    every = jnp.concatenate(received(recv_ref), axis=0)
    hits = [a_rows(member_rows, cell_col, k) for k in range(4)]
    rows = packed(every)
    e_cell = cell_halves([dot(h, rows) for h in hits])
    by_k = jnp.concatenate([pick(h, every) for h in hits], axis=0)
    gamma = pick(b_cell, log_b_ref[...] - jnp.log(cell_cols(e_cell, whole)) - tilt(cell_centre(cell_col), y))
    e0, e1, top = unpack(every)
    _, ea, a_top = unpack(by_k)
    d0, d1, da = [basic_cols(wide(e), whole) for e in (e0, e1, ea)]
    log_b1 = mix([gamma[a] + t for a, t in zip(parts, b_tilt)], [d0[a] for a in parts])
    gamma1 = log_b1 - mix([t - top[a] for a, t in zip(parts, b_tilt)], [d1[a] for a in parts])
    log_b = []
    for k in range(4):
        hit = hits[k].astype(F32)
        slot = (hit[:, :128] + hit[:, 128:256]) + (hit[:, 256:384] + hit[:, 384:])
        log_b.append(pick(slot, gamma1) + a_tilt[k] - a_top[parts[k]])
    log_b = mix(log_b, [da[a] for a in parts])
    lane = lax.broadcasted_iota(jnp.int32, (16, 128), 1)
    first = place_ref[3] * 16 + lax.broadcasted_iota(jnp.int32, (16, 128), 0)
    own_cells = jnp.sum(jnp.where(lane == first, jnp.broadcast_to(cell_row, (16, 128)), 0.0), axis=1, keepdims=True)
    want = jnp.concatenate([4.0 * own_cells + float(k) for k in range(4)], axis=0)
    ids, cells = near_cells(want, member_rows, cell_row, exchange_ids(member_rows), cells_ref, groups_ref, rows_ref, ids_ref)
    level_ref[...] = near_level(ids[:256], cells, log_b, cell_col, y)


def last_kernel(place_ref, recv_ref, level_ref, groups_ref, rows_ref, ids_ref, whole_ref, out_ref):
    centre = basic_centre(ids_ref[:, :1])
    v, d = near_margins(gathered(recv_ref, groups_ref, rows_ref), level_ref[...], centre,
                        targets(place_ref[2] * 128, 128), whole_ref[...])
    out = jnp.exp(v + jnp.log(d))
    for k in range(4):
        out_ref[:, k, :] = out[16 * k : 16 * k + 16]


def call(body, inputs, outs, scratch=(), work=1, far=0):
    near = len(inputs) - far
    inputs = inputs[:near] + tuple(pltpu.with_memory_space_constraint(v, pltpu.HBM) for v in inputs[near:])

    def spec(value):
        return pl.BlockSpec(memory_space=pltpu.SMEM if value.shape == (4,) else pltpu.VMEM)

    return pl.pallas_call(
        body,
        out_shape=[jax.ShapeDtypeStruct(s[:-1], BF16) if s[-1] is BF16 else jax.ShapeDtypeStruct(s, F32) for s in outs],
        in_specs=[spec(value) for value in inputs[:near]] + [pl.BlockSpec(memory_space=pltpu.HBM)] * far,
        out_specs=[pl.BlockSpec(memory_space=pltpu.VMEM)] * len(outs),
        scratch_shapes=list(scratch),
        compiler_params=pltpu.CompilerParams(vmem_limit_bytes=24 * 2**20),
        cost_estimate=pl.CostEstimate(flops=work * 10**9, bytes_accessed=10**6, transcendentals=0),
    )(*inputs)


FACTORS = [(3328, 128, BF16), (1152, 128)]
NEAR = [(256, 128, BF16), (1024, 512, BF16), (320, 512, BF16), (320, 128)]


def on_device(placement_a, members_b, source_mass, init_log, factors, wholes, ups):
    x, c, z, y = (lax.axis_index(name) for name in ("x", "c", "z", "y"))
    share = z * 4 + y
    place = jnp.stack([c, x * 8 + c * 4 + y, share, x]).astype(jnp.int32)
    index = (place, placement_a.reshape(1, 128), members_b.T)
    v = [init_log[:, k, :] for k in range(4)]
    peak = jnp.maximum(jnp.maximum(v[0], v[1]), jnp.maximum(v[2], v[3]))
    e = [jnp.exp(a - peak) for a in v]
    log_b = peak + jnp.log((e[0] + e[1]) + (e[2] + e[3])) + float(np.log(64.0 / W))
    mass = lax.dynamic_slice_in_dim(source_mass, share, 1, 0).reshape(2, 128)
    block = jnp.concatenate([log_b, mass], axis=0).reshape(9, 2, 128)
    own = lax.all_to_all(jnp.broadcast_to(block[None], (64, 9, 2, 128)), ("x", "z", "y"), 0, 0, tiled=True)
    sum_a, sum_b, factors, ups, held, onehot, cell, cells, groups, rows, ids = call(
        start_kernel, index + (factors, ups), [(128, 128), (16, 128)] + FACTORS + [(16, 128), (16, 128), (128, 128)] + NEAR,
        [pltpu.VMEM((1, 128), jnp.int32), pltpu.VMEM((4, 128), jnp.int32), pltpu.SemaphoreType.DMA((4,))], far=4)
    other = lax.ppermute(own, "c", [(0, 1), (1, 0)]).reshape(1152, 128)
    own = own.reshape(1152, 128)

    def exchange(rows):
        return lax.all_to_all(rows, ("x", "c", "y"), 0, 0, tiled=True)

    send, here, level, *rest = call(
        first_kernel, (place, own, other, sum_a, sum_b, held, onehot, cell, cells, ids, factors, ups),
        [(32, 16, 128), (128, 128), (256, W), (128, 128), (16, 128), (16, W), (8, W)], [pltpu.VMEM((128, W), F32)])
    first = exchange(send)
    send, whole = call(second_kernel, (place, held, first, level, groups, rows, ids, *rest, factors, ups, wholes),
                       [(32, 16, 128), (768, 128, BF16)])
    second = exchange(send)
    level, _, groups, rows, ids = call(middle_kernel, index + (here, first, whole), [(256, 128)] + NEAR)
    (out,) = call(last_kernel, (place, second, level, groups, rows, ids, whole), [(16, 4, 128)])
    return out


def solution(mesh):
    split = Mesh(mesh.devices.reshape(4, 2, 4, 4), ("x", "c", "z", "y"))
    tables = _tables()
    placed = (P(), P(), P(("x", "c"), None), P(("x", "c"), None, ("z", "y"))) + (P(),) * len(tables)
    body = jax.shard_map(
        on_device, mesh=split, in_specs=placed, out_specs=P(("x", "c"), None, ("z", "y")), check_vma=False
    )

    def run(placement_a, members_b, source_mass, init_log):
        return body(placement_a, members_b, source_mass, init_log, *(jnp.asarray(t) for t in tables))

    return run
```

```python
import numpy as np
import ml_dtypes

import jax
import jax.numpy as jnp
from jax import lax
from jax.experimental import pallas as pl
from jax.experimental.pallas import tpu as pltpu
from jax.sharding import Mesh, PartitionSpec as P

F32 = jnp.float32
BF16 = jnp.bfloat16
W = 2048
CENTRE = (slice(48, 64), slice(15, 16))


def _halves(matrix):
    high = matrix.astype(ml_dtypes.bfloat16)
    low = (matrix - high.astype(np.float64)).astype(ml_dtypes.bfloat16)
    return high, low


def _thrice(matrix):
    high, low = _halves(matrix)
    return np.concatenate([high, high, low], axis=0)


def _tables():
    yh = (np.arange(32) + 0.5) / 32 - 0.5
    ya = (np.arange(64) + 0.5) / 64 - 0.5
    dh = (np.arange(8) - 3.5) / 128
    da = (np.arange(8) - 3.5) / 256
    shifts = [(k - 1.5) / 32 for k in range(4)]

    def whole(shift):
        up = np.exp(400.0 * dh[:, None] * yh[None])
        along = np.exp(400.0 * (da + shift)[:, None] * ya[None])
        return (up[:, None, :, None] * along[None, :, None, :]).reshape(64, W)

    def along(shift):
        part = np.zeros((2, 64, 2, 8, 8))
        for h in range(2):
            part[h, :, h] = np.exp(400.0 * ya[:, None] * (da + shift)[None])[:, None, :]
        return part.reshape(128, 128)

    cell = np.concatenate([np.exp(400.0 * ya[:, None] * (da + s)[None]) for s in shifts], axis=1)
    high, low = _halves(np.concatenate([cell.T, cell.T], axis=1))
    one = np.exp(400.0 * ya[:, None] * da[None])
    turned = _halves(np.concatenate([one.T, one.T], axis=1))
    turned = (turned[0],) + turned + (np.zeros_like(turned[0]),)
    order = np.zeros((8, 4, 8, 8, 4, 4, 8), ml_dtypes.bfloat16)
    for i, k, r in np.ndindex(8, 4, 8):
        order[i, k, i, r, :, k, r] = 1
    factors = [
        _thrice(np.tile(cell, (2, 4))),
        np.concatenate([high, high, low, np.zeros_like(low)], axis=0),
        _thrice(along(0.0)),
        _thrice(along(0.0).T),
        order.reshape(2048, 128),
        _thrice(np.tile(one, (2, 16))),
        np.concatenate([np.concatenate([m, np.zeros((24, 128), m.dtype)], axis=0) for m in turned], axis=0),
    ]
    high, low = _halves(whole(0.0))
    wholes = _halves(np.concatenate([whole(s) for s in shifts], axis=0)) + (high, high, low, np.zeros_like(low))
    up = np.exp(400.0 * yh.reshape(16, 2, 1) * dh[None, None])
    of_row = np.repeat(up.transpose(0, 2, 1).reshape(128, 1, 2), 64, axis=2)
    of_pixel = np.repeat(up.reshape(16, 1, 16), 8, axis=2)
    ups = np.repeat(np.concatenate([of_row, of_pixel], axis=0), 8, axis=1).reshape(1152, 128)
    return np.concatenate(factors, axis=0), np.concatenate(wholes, axis=0), ups.astype(np.float32)


CELL, BACK, BASIC, BASIC_BACK, ORDER, ONE, ONE_BACK = 0, 384, 512, 896, 1280, 3328, 3712


def dot(a, b):
    return jnp.dot(a, b, preferred_element_type=F32)


def split2(x):
    high = x.astype(BF16)
    return high, (x - high.astype(F32)).astype(BF16)


def split3(x):
    high = x.astype(BF16)
    rest = x - high.astype(F32)
    mid = rest.astype(BF16)
    return high, mid, (rest - mid.astype(F32)).astype(BF16)


def pick(onehot, x):
    o = onehot.astype(BF16)
    return dot(jnp.concatenate([o, o, o], axis=1), jnp.concatenate(split3(x), axis=0))


def targets(first, count):
    j = first + lax.broadcasted_iota(jnp.int32, (1, count), 1)
    yh = (lax.shift_right_logical(j, 6).astype(F32) + 0.5) / 32.0 - 0.5
    ya = (lax.bitwise_and(j, 63).astype(F32) + 0.5) / 64.0 - 0.5
    return yh, ya


def basic_centre(ids):
    row = jnp.floor(ids / 32.0)
    return (row * 8.0 + 4.0) / 128.0 - 0.5, ((ids - row * 32.0) * 8.0 + 4.0) / 256.0 - 0.5


def cell_centre(cells):
    row = jnp.floor(cells / 8.0)
    return (row * 8.0 + 4.0) / 128.0 - 0.5, ((cells - row * 8.0) * 32.0 + 16.0) / 256.0 - 0.5


def tilt(centre, y):
    return (400.0 * centre[0]) * y[0] + (400.0 * centre[1]) * y[1]


def eye_mask():
    return lax.broadcasted_iota(jnp.int32, (128, 128), 0) == lax.broadcasted_iota(jnp.int32, (128, 128), 1)


def to_col(row):
    return jnp.sum(jnp.where(eye_mask(), jnp.broadcast_to(row, (128, 128)), 0.0), axis=1, keepdims=True)


def to_row(col):
    return jnp.sum(jnp.where(eye_mask(), jnp.broadcast_to(col, (128, 128)), 0.0), axis=0, keepdims=True)


def local_cells(placement_row, core):
    dst = lax.broadcasted_iota(jnp.int32, (128, 128), 0)
    src = lax.broadcasted_iota(jnp.int32, (128, 128), 1)
    side = lax.bitwise_xor(lax.shift_right_logical(dst, 6), core)
    slot = lax.bitwise_and(lax.shift_right_logical(dst, 4), 3) * 32 + side * 16 + lax.bitwise_and(dst, 15)
    col = jnp.sum(jnp.where(slot == src, jnp.broadcast_to(placement_row, (128, 128)), 0.0), axis=1, keepdims=True)
    return col, to_row(col)


def own_ids(member_rows, group):
    lane = lax.broadcasted_iota(jnp.int32, (16, 128), 1)
    sub = lax.broadcasted_iota(jnp.int32, (16, 128), 0)
    k = lax.shift_right_logical(sub, 2)
    rows = jnp.zeros((16, 128), F32)
    for i in range(4):
        rows = jnp.where(k == i, jnp.broadcast_to(member_rows[i], (16, 128)), rows)
    return jnp.sum(jnp.where(lane == 4 * group + lax.bitwise_and(sub, 3), rows, 0.0), axis=1, keepdims=True)


def low_half(shape):
    return lax.broadcasted_iota(jnp.int32, shape, 1) < 64


def swap(x):
    return pltpu.roll(x, 64, 1)


def doubled(x, upper):
    mask = low_half(x.shape)
    return jnp.where(mask, swap(x), x) if upper else jnp.where(mask, x, swap(x))


def segment(x, k):
    y = jnp.where(k >= 2.0, x[:, 256:], x[:, :256])
    return jnp.where((k == 1.0) | (k == 3.0), y[:, 128:], y[:, :128])


def quadrupled(x):
    return jnp.concatenate([doubled(x[:, :128], False), doubled(x[:, :128], True),
                            doubled(x[:, 128:], False), doubled(x[:, 128:], True)], axis=1)


def thrice(x):
    high, low = split2(x)
    return jnp.concatenate([high, low, high], axis=1)


def up_of(up_ref, i):
    h = up_ref[8 * i : 8 * i + 8, :]
    return jnp.concatenate([h, h], axis=0)


def total(parts):
    while len(parts) > 1:
        parts = [parts[i] + parts[i + 1] for i in range(0, len(parts), 2)]
    return parts[0]


def cell_sums(u, factor_ref, up_ref, first=CELL):
    v = [None] * 8
    for t in range(16):
        part = u[:, 128 * t : 128 * t + 128]
        for i in range(8):
            term = part * up_of(up_ref, 8 * t + i)
            v[i] = term if t == 0 else v[i] + term
    return dot(thrice(jnp.concatenate(v, axis=0)), factor_ref[first : first + 384, :])


def cell_back(e, factor_ref, up_ref, first=BACK):
    high = e.astype(BF16).astype(F32)
    lane = lax.broadcasted_iota(jnp.int32, e.shape, 1)
    x = jnp.where(lax.shift_right_logical(lane, 5) == 1, e - high, high).astype(BF16)
    z = dot(x, factor_ref[first : first + 128, :])
    z = [z[16 * i : 16 * i + 16] for i in range(8)]
    return jnp.concatenate(
        [total([z[i] * up_of(up_ref, 8 * t + i) for i in range(8)]) for t in range(16)], axis=1)


def ordered(mass, factor_ref):
    x = jnp.concatenate(split3(mass), axis=0)
    out = []
    for i in range(8):
        p = dot(x, factor_ref[ORDER + 256 * i : ORDER + 256 * i + 256, :])
        out.append((p[:16] + p[16:32]) + p[32:])
    return jnp.concatenate(out, axis=0)


def sums(u, factor_ref, up_ref):
    x = thrice(jnp.concatenate([u[:, 128 * t : 128 * t + 128] for t in range(16)], axis=0))
    p = dot(x, factor_ref[BASIC : BASIC + 384, :])
    s = total([p[16 * t : 16 * t + 16] * up_of(up_ref, 128 + t) for t in range(16)])
    return s + swap(s)


def cols(e, factor_ref, up_ref):
    x = jnp.concatenate([e * up_of(up_ref, 128 + t) for t in range(16)], axis=0)
    d = dot(thrice(x), factor_ref[BASIC_BACK : BASIC_BACK + 384, :])
    return jnp.concatenate([d[16 * t : 16 * t + 16] for t in range(16)], axis=1)


def wide(e):
    high = e.astype(BF16).astype(F32)
    return jnp.concatenate([jnp.where(low_half(e.shape), high, e - high), high], axis=1).astype(BF16)


def cell_cols(e, whole):
    n = e.shape[0] // 2
    p = dot(e, whole[:256])
    return p[:n] + p[n:] + dot(e[:n], whole[256:512])


def basic_cols(e, whole):
    return dot(e, whole[512:])


def nearness(centre, y):
    return jnp.exp(-200.0 * ((centre[0] - y[0]) ** 2 + (centre[1] - y[1]) ** 2))


def balanced(mass, s):
    return mass * (jnp.concatenate([s[CENTRE]] * 8, axis=0) / s)


def sweep_a(log_b, mass, d, factor_ref, up_ref, beside):
    b = jnp.exp(log_b - jnp.max(log_b, axis=1, keepdims=True))
    for i in range(3):
        beside(i)
        u = b / d
        s = cell_sums(u, factor_ref, up_ref)
        d = cell_back(balanced(mass, s), factor_ref, up_ref)
    return u, s[CENTRE], d


def over_k(x, op):
    y = op(x[:8], x[8:])
    return op(y, pltpu.roll(y, 4, 0))


def twice(x):
    return jnp.concatenate([x, x], axis=0)


def column_part(r, top, d):
    q = r - top
    peak = over_k(q, jnp.maximum)
    return peak + jnp.log(over_k(jnp.exp(q - twice(peak)) * d, jnp.add))


def sweep_b(log_b, masses, r, part, factor_ref, up_ref, beside):
    for i in range(3):
        beside(5 + i)
        v = r + twice(log_b - part)
        top = jnp.max(v, axis=1, keepdims=True)
        t = jnp.exp(v - top)
        if i < 2:
            e = masses[0] / cell_sums(t, factor_ref, up_ref, ONE)
            part = column_part(r, top, cell_back(e, factor_ref, up_ref, ONE_BACK))
    e = masses[1] / sums(t, factor_ref, up_ref)
    return e, top


def solve_pair(log_b_a, mass_a, masses_b, ids, d, part, factor_ref, up_ref, send_ref, beside=lambda i: None):
    y = targets(0, W)
    at_cell = cell_centre(jnp.floor(ids / 4.0))
    at_basic = basic_centre(ids)
    shift = (400.0 * (at_basic[1] - at_cell[1])) * y[1]
    u, centre, d_a = sweep_a(log_b_a, mass_a, d, factor_ref, up_ref, beside)
    e_first = masses_b[1] * (centre / sums(u * jnp.exp(shift), factor_ref, up_ref))
    beside(3)
    d_first = cols(e_first, factor_ref, up_ref)
    v = log_b_a - jnp.log(d_a) + shift
    peak = over_k(v, jnp.maximum)
    beside(4)
    log_b_b = peak + jnp.log(over_k(jnp.exp(v - twice(peak)) * d_first, jnp.add))
    e_second, top = sweep_b(log_b_b, masses_b, tilt(at_basic, y), part, factor_ref, up_ref, beside)
    rows = jnp.where(low_half((16, 128)), e_first, jnp.log(e_second) - top)
    for i in range(32):
        send_ref[i, :, :] = rows


def member_rows_of(members_ref):
    members = members_ref[...].astype(F32)
    return [members[k : k + 1, :] for k in range(4)]


def exchange_ids(member_rows):
    members = [to_col(row) for row in member_rows]
    slot = lax.broadcasted_iota(jnp.int32, (128, 128), 0)
    lane = lax.broadcasted_iota(jnp.int32, (128, 128), 1)
    k = lax.bitwise_and(lax.shift_right_logical(lane, 2), 3)
    value = jnp.broadcast_to(members[0], (128, 128))
    for i in range(1, 4):
        value = jnp.where(k == i, jnp.broadcast_to(members[i], (128, 128)), value)
    of_lane = 4 * lax.shift_right_logical(lane, 4) + lax.bitwise_and(lane, 3)
    return jnp.concatenate(
        [jnp.sum(jnp.where(slot == of_lane + 32 * t, value, 0.0), axis=0, keepdims=True) for t in range(4)], axis=1)


def near_cells(want, member_rows, cell_row, exchanged, cells_ref, groups_ref, rows_ref, ids_ref):
    hits = [jnp.where(row == want, 1.0, 0.0) for row in member_rows]
    slot = (hits[0] + hits[1]) + (hits[2] + hits[3])
    ids = jnp.concatenate([jnp.sum(slot * row, axis=1, keepdims=True) for row in member_rows], axis=0)
    cell = jnp.floor(ids / 4.0)
    cells = jnp.where(cell_row == cell, 1.0, 0.0)
    cells_ref[...] = cells.astype(BF16)
    for k in range(4):
        groups_ref[256 * k : 256 * k + 256, :] = jnp.where(exchanged == 4.0 * cell + float(k), 1.0, 0.0).astype(BF16)
    ids = jnp.concatenate([ids, want], axis=0)
    rows_ref[...] = jnp.where(exchanged == ids, 1.0, 0.0).astype(BF16)
    ids_ref[...] = jnp.broadcast_to(ids, (320, 128))
    return ids, cells


def start_kernel(place_ref, placement_hbm, members_hbm, factor_hbm, up_hbm, sum_a_ref, sum_b_ref, factor_ref, up_ref, own_ids_ref, onehot_ref,
                 cell_ref, cells_ref, groups_ref, rows_ref, ids_ref, placement_ref, members_ref, sems):
    pairs = ((placement_hbm, placement_ref), (members_hbm, members_ref), (factor_hbm, factor_ref), (up_hbm, up_ref))
    copies = [pltpu.make_async_copy(*pair, sems.at[i]) for i, pair in enumerate(pairs)]
    for copy in copies:
        copy.start()
    for copy in copies[:2]:
        copy.wait()
    cell_col, cell_row = local_cells(placement_ref[...].astype(F32), place_ref[0])
    member_rows = member_rows_of(members_ref)
    ids = own_ids(member_rows, place_ref[1])
    own_ids_ref[...] = jnp.broadcast_to(ids, (16, 128))
    cells = jnp.floor(ids / 4.0)
    onehot_ref[...] = jnp.where(cell_row == cells, 1.0, 0.0)
    cell_ref[...] = jnp.broadcast_to(cell_col, (128, 128))
    want = jnp.concatenate([4.0 * cells + float(k) for k in range(4)], axis=0)
    near_cells(want, member_rows, cell_row, exchange_ids(member_rows), cells_ref, groups_ref, rows_ref, ids_ref)
    for copy in copies[2:]:
        copy.wait()
    y = targets(0, W)
    sum_a_ref[...] = cell_sums(nearness(cell_centre(jnp.floor(ids / 4.0)), y), factor_ref, up_ref)
    sum_b_ref[...] = sums(nearness(basic_centre(ids), y), factor_ref, up_ref)


def first_kernel(place_ref, own_ref, other_ref, sum_a_ref, sum_b_ref, ids_ref, onehot_ref, cell_ref, cells_ref, near_ref,
                 factor_ref, up_ref, whole_hbm, send_ref, here_ref, level_ref, mass_a_ref, mass_b_ref, mass_one_ref, d_ref, part_ref, whole_ref, table_ref, sems):
    copy = pltpu.make_async_copy(whole_hbm, whole_ref, sems.at[0])
    copy.start()
    ids, onehot = ids_ref[:, :1], onehot_ref[...]
    mass = []
    for part in (16, 17):
        at = pl.ds(part, 64, stride=18)
        rows = jnp.concatenate([own_ref[at, :], other_ref[at, :]], axis=0)
        mass.append(pick(onehot, rows))
    mass = jnp.concatenate(mass, axis=1)
    mass_a = ordered(mass, factor_ref)
    k = ids - 4.0 * jnp.floor(ids / 4.0)
    mass_b = segment(quadrupled(mass), k)
    lane_k = lax.bitwise_and(lax.shift_right_logical(lax.broadcasted_iota(jnp.int32, (128, 128), 1), 3), 3).astype(F32)
    mass_one = jnp.where(lane_k == jnp.concatenate([k] * 8, axis=0), mass_a, 0.0)
    mass_one = mass_one + pltpu.roll(mass_one, 8, 1)
    mass_one = mass_one + pltpu.roll(mass_one, 16, 1)
    d = cell_back(balanced(mass_a, sum_a_ref[...]), factor_ref, up_ref)
    log_b = []
    for t in range(16):
        starts = [18 * (16 * x + t) for x in range(4)]
        rows = [ref[i : i + 16, :] for ref in (own_ref, other_ref) for i in starts]
        rows = jnp.concatenate(rows, axis=0)
        table_ref[:, 128 * t : 128 * t + 128] = rows
        log_b.append(pick(onehot, rows))
    here_ref[...] = table_ref[:, pl.ds(pl.multiple_of(place_ref[2] * 128, 128), 128)]
    log_b = jnp.concatenate(log_b, axis=1)
    at_basic = basic_centre(ids)
    top = 200.0 * (at_basic[0] * at_basic[0] + at_basic[1] * at_basic[1])
    part = column_part(tilt(at_basic, targets(0, W)), top, cols(mass_b / sum_b_ref[...], factor_ref, up_ref))
    mass_a_ref[...] = mass_a
    mass_b_ref[...] = mass_b
    mass_one_ref[...] = mass_one
    d_ref[...] = d
    part_ref[...] = part
    near, cell_col = near_ref[0:256, :1], cell_ref[:, :1]

    def level(block):
        at = slice(256 * block, 256 * block + 256)
        level_ref[:, at] = near_level(near, cells_ref[...], table_ref[:, at], cell_col, targets(256 * block, 256))

    solve_pair(log_b, mass_a, (mass_one, mass_b), ids, d, part, factor_ref, up_ref, send_ref, level)
    copy.wait()


def received(recv_ref):
    return [jnp.concatenate([recv_ref[g, 4 * k : 4 * k + 4, :] for g in range(32)], axis=0) for k in range(4)]


def high_top(x):
    return jnp.max(jnp.where(low_half(x.shape), -jnp.inf, x), axis=1, keepdims=True)


def unpack(f):
    top = -high_top(f)
    return doubled(f, False), jnp.exp(doubled(f, True) + top), top


def a_rows(member_rows, cell_col, k):
    want = 4.0 * cell_col + float(k)
    return jnp.concatenate([jnp.where(row == want, 1.0, 0.0) for row in member_rows], axis=1).astype(BF16)


def packed(f):
    high, low = split2(f)
    return jnp.where(low_half(f.shape), high.astype(F32), swap(low.astype(F32))).astype(BF16)


def cell_halves(by_k):
    mask = low_half(by_k[0].shape)
    high = [jnp.where(mask, by_k[i], swap(by_k[i + 1])) for i in (0, 2)]
    low = [jnp.where(mask, swap(by_k[i]), by_k[i + 1]) for i in (0, 2)]
    return jnp.concatenate([jnp.concatenate(high, axis=1), jnp.concatenate(low, axis=1)], axis=0).astype(BF16)


def mix(v, d):
    peak = jnp.maximum(jnp.maximum(v[0], v[1]), jnp.maximum(v[2], v[3]))
    z = [jnp.exp(a - peak) * b for a, b in zip(v, d)]
    return peak + jnp.log((z[0] + z[1]) + (z[2] + z[3]))


def near_level(ids, cells, log_b, cell_col, y):
    return pick(cells, log_b - tilt(cell_centre(cell_col), y)) + tilt(basic_centre(ids), y)


def gathered(recv_ref, groups_ref, rows_ref):
    f = recv_ref[...].reshape(512, 128)
    by_k = dot(groups_ref[...], packed(f))
    o = rows_ref[...]
    high, mid, low = split3(f)
    two = dot(o, jnp.concatenate([high, mid], axis=1))
    e0, e1, top = unpack((two[:, :128] + two[:, 128:]) + dot(o, low))
    by_k = [by_k[256 * k : 256 * k + 256] for k in range(4)]
    return cell_halves(by_k), wide(e0[:256]), wide(e1), top


def near_margins(gather, level, centre, y, whole):
    e_cell, e0, e1, top = gather
    parts = [slice(64 * k, 64 * k + 64) for k in range(4)]
    v = level - jnp.log(cell_cols(e_cell, whole))
    d0 = basic_cols(e0, whole)
    d1 = basic_cols(e1, whole)
    q = tilt(centre, y) - top
    log_b = mix([v[a] for a in parts], [d0[a] for a in parts])
    gamma = log_b - mix([q[a] for a in parts], [d1[a] for a in parts])
    return gamma + q[256:], d1[256:]


def second_kernel(place_ref, own_ids_ref, recv_ref, level_ref, groups_ref, rows_ref, ids_ref, mass_a_ref, mass_b_ref, mass_one_ref, d_ref,
                  part_ref, factor_ref, up_ref, whole_ref, send_ref, here_ref):
    here_ref[...] = whole_ref[:, pl.ds(pl.multiple_of(place_ref[2] * 128, 128), 128)]
    gather = gathered(recv_ref, groups_ref, rows_ref)
    centre = basic_centre(ids_ref[:, :1])
    log_b = []
    for block in range(8):
        at = slice(block * 256, block * 256 + 256)
        v, d = near_margins(gather, level_ref[:, at], centre, targets(256 * block, 256), whole_ref[:, at])
        log_b.append(mix([v[16 * k : 16 * k + 16] for k in range(4)], [d[16 * k : 16 * k + 16] for k in range(4)]))
    solve_pair(jnp.concatenate(log_b, axis=1), mass_a_ref[...], (mass_one_ref[...], mass_b_ref[...]), own_ids_ref[:, :1], d_ref[...], part_ref[...],
               factor_ref, up_ref, send_ref)


def middle_kernel(place_ref, placement_ref, members_ref, log_b_ref, recv_ref, whole_ref, level_ref, cells_ref, groups_ref,
                  rows_ref, ids_ref):
    cell_col, cell_row = local_cells(placement_ref[...].astype(F32), place_ref[0])
    member_rows = member_rows_of(members_ref)
    share = place_ref[2]
    y = targets(share * 128, 128)
    whole = whole_ref[...]
    b_ids = [to_col(row) for row in member_rows]
    b_cell = jnp.concatenate([jnp.where(cell_row == jnp.floor(i / 4.0), 1.0, 0.0) for i in b_ids], axis=0)
    b_tilt = [tilt(basic_centre(i), y) for i in b_ids]
    a_tilt = [tilt(basic_centre(4.0 * cell_col + float(k)), y) for k in range(4)]
    parts = [slice(128 * k, 128 * k + 128) for k in range(4)]
    every = jnp.concatenate(received(recv_ref), axis=0)
    hits = [a_rows(member_rows, cell_col, k) for k in range(4)]
    rows = packed(every)
    e_cell = cell_halves([dot(h, rows) for h in hits])
    by_k = jnp.concatenate([pick(h, every) for h in hits], axis=0)
    gamma = pick(b_cell, log_b_ref[...] - jnp.log(cell_cols(e_cell, whole)) - tilt(cell_centre(cell_col), y))
    e0, e1, top = unpack(every)
    _, ea, a_top = unpack(by_k)
    d0, d1, da = [basic_cols(wide(e), whole) for e in (e0, e1, ea)]
    log_b1 = mix([gamma[a] + t for a, t in zip(parts, b_tilt)], [d0[a] for a in parts])
    gamma1 = log_b1 - mix([t - top[a] for a, t in zip(parts, b_tilt)], [d1[a] for a in parts])
    log_b = []
    for k in range(4):
        hit = hits[k].astype(F32)
        slot = (hit[:, :128] + hit[:, 128:256]) + (hit[:, 256:384] + hit[:, 384:])
        log_b.append(pick(slot, gamma1) + a_tilt[k] - a_top[parts[k]])
    log_b = mix(log_b, [da[a] for a in parts])
    lane = lax.broadcasted_iota(jnp.int32, (16, 128), 1)
    first = place_ref[3] * 16 + lax.broadcasted_iota(jnp.int32, (16, 128), 0)
    own_cells = jnp.sum(jnp.where(lane == first, jnp.broadcast_to(cell_row, (16, 128)), 0.0), axis=1, keepdims=True)
    want = jnp.concatenate([4.0 * own_cells + float(k) for k in range(4)], axis=0)
    ids, cells = near_cells(want, member_rows, cell_row, exchange_ids(member_rows), cells_ref, groups_ref, rows_ref, ids_ref)
    level_ref[...] = near_level(ids[:256], cells, log_b, cell_col, y)


def last_kernel(place_ref, recv_ref, level_ref, groups_ref, rows_ref, ids_ref, whole_ref, out_ref):
    centre = basic_centre(ids_ref[:, :1])
    v, d = near_margins(gathered(recv_ref, groups_ref, rows_ref), level_ref[...], centre,
                        targets(place_ref[2] * 128, 128), whole_ref[...])
    out = jnp.exp(v + jnp.log(d))
    for k in range(4):
        out_ref[:, k, :] = out[16 * k : 16 * k + 16]


def call(body, inputs, outs, scratch=(), work=1, far=0):
    near = len(inputs) - far
    inputs = inputs[:near] + tuple(pltpu.with_memory_space_constraint(v, pltpu.HBM) for v in inputs[near:])

    def spec(value):
        return pl.BlockSpec(memory_space=pltpu.SMEM if value.shape == (4,) else pltpu.VMEM)

    return pl.pallas_call(
        body,
        out_shape=[jax.ShapeDtypeStruct(s[:-1], BF16) if s[-1] is BF16 else jax.ShapeDtypeStruct(s, F32) for s in outs],
        in_specs=[spec(value) for value in inputs[:near]] + [pl.BlockSpec(memory_space=pltpu.HBM)] * far,
        out_specs=[pl.BlockSpec(memory_space=pltpu.VMEM)] * len(outs),
        scratch_shapes=list(scratch),
        compiler_params=pltpu.CompilerParams(vmem_limit_bytes=24 * 2**20),
        cost_estimate=pl.CostEstimate(flops=work * 10**9, bytes_accessed=10**6, transcendentals=0),
    )(*inputs)


FACTORS = [(3840, 128, BF16), (1152, 128)]
NEAR = [(256, 128, BF16), (1024, 512, BF16), (320, 512, BF16), (320, 128)]


def on_device(placement_a, members_b, source_mass, init_log, factors, wholes, ups):
    x, c, z, y = (lax.axis_index(name) for name in ("x", "c", "z", "y"))
    share = z * 4 + y
    place = jnp.stack([c, x * 8 + c * 4 + y, share, x]).astype(jnp.int32)
    index = (place, placement_a.reshape(1, 128), members_b.T)
    v = [init_log[:, k, :] for k in range(4)]
    peak = jnp.maximum(jnp.maximum(v[0], v[1]), jnp.maximum(v[2], v[3]))
    e = [jnp.exp(a - peak) for a in v]
    log_b = peak + jnp.log((e[0] + e[1]) + (e[2] + e[3])) + float(np.log(64.0 / W))
    mass = lax.dynamic_slice_in_dim(source_mass, share, 1, 0).reshape(2, 128)
    block = jnp.concatenate([log_b, mass], axis=0).reshape(9, 2, 128)
    own = lax.all_to_all(jnp.broadcast_to(block[None], (64, 9, 2, 128)), ("x", "z", "y"), 0, 0, tiled=True)
    sum_a, sum_b, factors, ups, held, onehot, cell, cells, groups, rows, ids = call(
        start_kernel, index + (factors, ups), [(128, 128), (16, 128)] + FACTORS + [(16, 128), (16, 128), (128, 128)] + NEAR,
        [pltpu.VMEM((1, 128), jnp.int32), pltpu.VMEM((4, 128), jnp.int32), pltpu.SemaphoreType.DMA((4,))], far=4)
    other = lax.ppermute(own, "c", [(0, 1), (1, 0)]).reshape(1152, 128)
    own = own.reshape(1152, 128)

    def exchange(rows):
        return lax.all_to_all(rows, ("x", "c", "y"), 0, 0, tiled=True)

    send, here, level, *rest, wholes = call(
        first_kernel, (place, own, other, sum_a, sum_b, held, onehot, cell, cells, ids, factors, ups, wholes),
        [(32, 16, 128), (128, 128), (256, W), (128, 128), (16, 128), (128, 128), (16, W), (8, W), (768, W, BF16)],
        [pltpu.VMEM((128, W), F32), pltpu.SemaphoreType.DMA((1,))], far=1)
    first = exchange(send)
    send, whole = call(second_kernel, (place, held, first, level, groups, rows, ids, *rest, factors, ups, wholes),
                       [(32, 16, 128), (768, 128, BF16)])
    second = exchange(send)
    level, _, groups, rows, ids = call(middle_kernel, index + (here, first, whole), [(256, 128)] + NEAR)
    (out,) = call(last_kernel, (place, second, level, groups, rows, ids, whole), [(16, 4, 128)])
    return out


def solution(mesh):
    split = Mesh(mesh.devices.reshape(4, 2, 4, 4), ("x", "c", "z", "y"))
    tables = _tables()
    placed = (P(), P(), P(("x", "c"), None), P(("x", "c"), None, ("z", "y"))) + (P(),) * len(tables)
    body = jax.shard_map(
        on_device, mesh=split, in_specs=placed, out_specs=P(("x", "c"), None, ("z", "y")), check_vma=False
    )

    def run(placement_a, members_b, source_mass, init_log):
        return body(placement_a, members_b, source_mass, init_log, *(jnp.asarray(t) for t in tables))

    return run
```

```python
import numpy as np
import ml_dtypes

import jax
import jax.numpy as jnp
from jax import lax
from jax.experimental import pallas as pl
from jax.experimental.pallas import tpu as pltpu
from jax.sharding import Mesh, PartitionSpec as P

F32 = jnp.float32
BF16 = jnp.bfloat16
W = 2048
CENTRE = (slice(48, 64), slice(15, 16))


def _halves(matrix):
    high = matrix.astype(ml_dtypes.bfloat16)
    low = (matrix - high.astype(np.float64)).astype(ml_dtypes.bfloat16)
    return high, low


def _thrice(matrix):
    high, low = _halves(matrix)
    return np.concatenate([high, high, low], axis=0)


def _tables():
    yh = (np.arange(32) + 0.5) / 32 - 0.5
    ya = (np.arange(64) + 0.5) / 64 - 0.5
    dh = (np.arange(8) - 3.5) / 128
    da = (np.arange(8) - 3.5) / 256
    shifts = [(k - 1.5) / 32 for k in range(4)]

    def whole(shift):
        up = np.exp(400.0 * dh[:, None] * yh[None])
        along = np.exp(400.0 * (da + shift)[:, None] * ya[None])
        return (up[:, None, :, None] * along[None, :, None, :]).reshape(64, W)

    cell = np.concatenate([np.exp(400.0 * ya[:, None] * (da + s)[None]) for s in shifts], axis=1)
    high, low = _halves(np.concatenate([cell.T, cell.T], axis=1))
    one = np.exp(400.0 * ya[:, None] * da[None])
    turned = _halves(np.concatenate([one.T, one.T], axis=1))
    turned = (turned[0],) + turned + (np.zeros_like(turned[0]),)
    order = np.zeros((8, 4, 8, 8, 4, 4, 8), ml_dtypes.bfloat16)
    for i, k, r in np.ndindex(8, 4, 8):
        order[i, k, i, r, :, k, r] = 1
    factors = [
        _thrice(np.tile(cell, (2, 4))),
        np.concatenate([high, high, low, np.zeros_like(low)], axis=0),
        order.reshape(2048, 128),
        _thrice(np.tile(one, (2, 16))),
        np.concatenate([np.concatenate([m, np.zeros((24, 128), m.dtype)], axis=0) for m in turned], axis=0),
    ]
    high, low = _halves(whole(0.0))
    wholes = _halves(np.concatenate([whole(s) for s in shifts], axis=0)) + (high, high, low, np.zeros_like(low))
    up = np.exp(400.0 * yh.reshape(16, 2, 1) * dh[None, None])
    of_row = np.repeat(up.transpose(0, 2, 1).reshape(128, 1, 2), 64, axis=2)
    ups = np.repeat(of_row, 8, axis=1).reshape(1024, 128)
    return np.concatenate(factors, axis=0), np.concatenate(wholes, axis=0), ups.astype(np.float32)


CELL, BACK, ORDER, ONE, ONE_BACK = 0, 384, 512, 2560, 2944


def dot(a, b):
    return jnp.dot(a, b, preferred_element_type=F32)


def split2(x):
    high = x.astype(BF16)
    return high, (x - high.astype(F32)).astype(BF16)


def split3(x):
    high = x.astype(BF16)
    rest = x - high.astype(F32)
    mid = rest.astype(BF16)
    return high, mid, (rest - mid.astype(F32)).astype(BF16)


def pick(onehot, x):
    o = onehot.astype(BF16)
    return dot(jnp.concatenate([o, o, o], axis=1), jnp.concatenate(split3(x), axis=0))


def targets(first, count):
    j = first + lax.broadcasted_iota(jnp.int32, (1, count), 1)
    yh = (lax.shift_right_logical(j, 6).astype(F32) + 0.5) / 32.0 - 0.5
    ya = (lax.bitwise_and(j, 63).astype(F32) + 0.5) / 64.0 - 0.5
    return yh, ya


def basic_centre(ids):
    row = jnp.floor(ids / 32.0)
    return (row * 8.0 + 4.0) / 128.0 - 0.5, ((ids - row * 32.0) * 8.0 + 4.0) / 256.0 - 0.5


def cell_centre(cells):
    row = jnp.floor(cells / 8.0)
    return (row * 8.0 + 4.0) / 128.0 - 0.5, ((cells - row * 8.0) * 32.0 + 16.0) / 256.0 - 0.5


def tilt(centre, y):
    return (400.0 * centre[0]) * y[0] + (400.0 * centre[1]) * y[1]


def eye_mask():
    return lax.broadcasted_iota(jnp.int32, (128, 128), 0) == lax.broadcasted_iota(jnp.int32, (128, 128), 1)


def to_col(row):
    return jnp.sum(jnp.where(eye_mask(), jnp.broadcast_to(row, (128, 128)), 0.0), axis=1, keepdims=True)


def to_row(col):
    return jnp.sum(jnp.where(eye_mask(), jnp.broadcast_to(col, (128, 128)), 0.0), axis=0, keepdims=True)


def local_cells(placement_row, core):
    dst = lax.broadcasted_iota(jnp.int32, (128, 128), 0)
    src = lax.broadcasted_iota(jnp.int32, (128, 128), 1)
    side = lax.bitwise_xor(lax.shift_right_logical(dst, 6), core)
    slot = lax.bitwise_and(lax.shift_right_logical(dst, 4), 3) * 32 + side * 16 + lax.bitwise_and(dst, 15)
    col = jnp.sum(jnp.where(slot == src, jnp.broadcast_to(placement_row, (128, 128)), 0.0), axis=1, keepdims=True)
    return col, to_row(col)


def own_ids(member_rows, group):
    lane = lax.broadcasted_iota(jnp.int32, (16, 128), 1)
    sub = lax.broadcasted_iota(jnp.int32, (16, 128), 0)
    k = lax.shift_right_logical(sub, 2)
    rows = jnp.zeros((16, 128), F32)
    for i in range(4):
        rows = jnp.where(k == i, jnp.broadcast_to(member_rows[i], (16, 128)), rows)
    return jnp.sum(jnp.where(lane == 4 * group + lax.bitwise_and(sub, 3), rows, 0.0), axis=1, keepdims=True)


def low_half(shape):
    return lax.broadcasted_iota(jnp.int32, shape, 1) < 64


def swap(x):
    return pltpu.roll(x, 64, 1)


def doubled(x, upper):
    mask = low_half(x.shape)
    return jnp.where(mask, swap(x), x) if upper else jnp.where(mask, x, swap(x))


def thrice(x):
    high, low = split2(x)
    return jnp.concatenate([high, low, high], axis=1)


def up_of(up_ref, i):
    h = up_ref[8 * i : 8 * i + 8, :]
    return jnp.concatenate([h, h], axis=0)


def total(parts):
    while len(parts) > 1:
        parts = [parts[i] + parts[i + 1] for i in range(0, len(parts), 2)]
    return parts[0]


def cell_sums(u, factor_ref, up_ref, first=CELL):
    v = [None] * 8
    for t in range(16):
        part = u[:, 128 * t : 128 * t + 128]
        for i in range(8):
            term = part * up_of(up_ref, 8 * t + i)
            v[i] = term if t == 0 else v[i] + term
    return dot(thrice(jnp.concatenate(v, axis=0)), factor_ref[first : first + 384, :])


def cell_back(e, factor_ref, up_ref, first=BACK):
    high = e.astype(BF16).astype(F32)
    lane = lax.broadcasted_iota(jnp.int32, e.shape, 1)
    x = jnp.where(lax.shift_right_logical(lane, 5) == 1, e - high, high).astype(BF16)
    z = dot(x, factor_ref[first : first + 128, :])
    z = [z[16 * i : 16 * i + 16] for i in range(8)]
    return jnp.concatenate(
        [total([z[i] * up_of(up_ref, 8 * t + i) for i in range(8)]) for t in range(16)], axis=1)


def ordered(mass, factor_ref):
    x = jnp.concatenate(split3(mass), axis=0)
    out = []
    for i in range(8):
        p = dot(x, factor_ref[ORDER + 256 * i : ORDER + 256 * i + 256, :])
        out.append((p[:16] + p[16:32]) + p[32:])
    return jnp.concatenate(out, axis=0)


def spread(e):
    row = lax.bitwise_and(lax.shift_right_logical(lax.broadcasted_iota(jnp.int32, (16, 128), 1), 3), 7)
    out = e[:16]
    for i in range(1, 8):
        out = jnp.where(row == i, e[16 * i : 16 * i + 16], out)
    return out


def wide(e):
    high = e.astype(BF16).astype(F32)
    return jnp.concatenate([jnp.where(low_half(e.shape), high, e - high), high], axis=1).astype(BF16)


def cell_cols(e, whole):
    n = e.shape[0] // 2
    p = dot(e, whole[:256])
    return p[:n] + p[n:] + dot(e[:n], whole[256:512])


def basic_cols(e, whole):
    return dot(e, whole[512:])


def nearness(centre, y):
    return jnp.exp(-200.0 * ((centre[0] - y[0]) ** 2 + (centre[1] - y[1]) ** 2))


def balanced(mass, s):
    return mass * (jnp.concatenate([s[CENTRE]] * 8, axis=0) / s)


def sweep_a(log_b, mass, d, factor_ref, up_ref, beside):
    b = jnp.exp(log_b - jnp.max(log_b, axis=1, keepdims=True))
    for i in range(3):
        beside(i)
        u = b / d
        s = cell_sums(u, factor_ref, up_ref)
        d = cell_back(balanced(mass, s), factor_ref, up_ref)
    return u, s[CENTRE], d


def over_k(x, op):
    y = op(x[:8], x[8:])
    return op(y, pltpu.roll(y, 4, 0))


def twice(x):
    return jnp.concatenate([x, x], axis=0)


def column_part(r, top, d):
    q = r - top
    peak = over_k(q, jnp.maximum)
    return peak + jnp.log(over_k(jnp.exp(q - twice(peak)) * d, jnp.add))


def sweep_b(log_b, mass, r, part, factor_ref, up_ref, beside):
    for i in range(3):
        beside(5 + i)
        v = r + twice(log_b - part)
        top = jnp.max(v, axis=1, keepdims=True)
        e = mass / cell_sums(jnp.exp(v - top), factor_ref, up_ref, ONE)
        if i < 2:
            part = column_part(r, top, cell_back(e, factor_ref, up_ref, ONE_BACK))
    return e, top


def solve_pair(log_b_a, mass_a, mass_b, ids, d, part, factor_ref, up_ref, send_ref, beside=lambda i: None):
    y = targets(0, W)
    at_cell = cell_centre(jnp.floor(ids / 4.0))
    at_basic = basic_centre(ids)
    shift = (400.0 * (at_basic[1] - at_cell[1])) * y[1]
    u, centre, d_a = sweep_a(log_b_a, mass_a, d, factor_ref, up_ref, beside)
    s = cell_sums(u * jnp.exp(shift), factor_ref, up_ref, ONE)
    e_first = mass_b * (jnp.concatenate([centre] * 8, axis=0) / s)
    beside(3)
    d_first = cell_back(e_first, factor_ref, up_ref, ONE_BACK)
    v = log_b_a - jnp.log(d_a) + shift
    peak = over_k(v, jnp.maximum)
    beside(4)
    log_b_b = peak + jnp.log(over_k(jnp.exp(v - twice(peak)) * d_first, jnp.add))
    e_second, top = sweep_b(log_b_b, mass_b, tilt(at_basic, y), part, factor_ref, up_ref, beside)
    rows = jnp.where(low_half((16, 128)), spread(e_first), jnp.log(spread(e_second)) - top)
    for i in range(32):
        send_ref[i, :, :] = rows


def member_rows_of(members_ref):
    members = members_ref[...].astype(F32)
    return [members[k : k + 1, :] for k in range(4)]


def exchange_ids(member_rows):
    members = [to_col(row) for row in member_rows]
    slot = lax.broadcasted_iota(jnp.int32, (128, 128), 0)
    lane = lax.broadcasted_iota(jnp.int32, (128, 128), 1)
    k = lax.bitwise_and(lax.shift_right_logical(lane, 2), 3)
    value = jnp.broadcast_to(members[0], (128, 128))
    for i in range(1, 4):
        value = jnp.where(k == i, jnp.broadcast_to(members[i], (128, 128)), value)
    of_lane = 4 * lax.shift_right_logical(lane, 4) + lax.bitwise_and(lane, 3)
    return jnp.concatenate(
        [jnp.sum(jnp.where(slot == of_lane + 32 * t, value, 0.0), axis=0, keepdims=True) for t in range(4)], axis=1)


def near_cells(want, member_rows, cell_row, exchanged, cells_ref, groups_ref, rows_ref, ids_ref):
    hits = [jnp.where(row == want, 1.0, 0.0) for row in member_rows]
    slot = (hits[0] + hits[1]) + (hits[2] + hits[3])
    ids = jnp.concatenate([jnp.sum(slot * row, axis=1, keepdims=True) for row in member_rows], axis=0)
    cell = jnp.floor(ids / 4.0)
    cells = jnp.where(cell_row == cell, 1.0, 0.0)
    cells_ref[...] = cells.astype(BF16)
    for k in range(4):
        groups_ref[256 * k : 256 * k + 256, :] = jnp.where(exchanged == 4.0 * cell + float(k), 1.0, 0.0).astype(BF16)
    ids = jnp.concatenate([ids, want], axis=0)
    rows_ref[...] = jnp.where(exchanged == ids, 1.0, 0.0).astype(BF16)
    ids_ref[...] = jnp.broadcast_to(ids, (320, 128))
    return ids, cells


def start_kernel(place_ref, placement_hbm, members_hbm, factor_hbm, up_hbm, sum_a_ref, sum_b_ref, factor_ref, up_ref, own_ids_ref, onehot_ref,
                 cell_ref, cells_ref, groups_ref, rows_ref, ids_ref, placement_ref, members_ref, sems):
    pairs = [(placement_hbm, placement_ref), (members_hbm, members_ref), (up_hbm, up_ref)]
    pairs += [(factor_hbm.at[at, :], factor_ref.at[at, :]) for at in (pl.ds(0, ORDER), pl.ds(ONE, 512), pl.ds(ORDER, ONE - ORDER))]
    copies = [pltpu.make_async_copy(*pair, sems.at[i]) for i, pair in enumerate(pairs)]
    for copy in copies:
        copy.start()
    for copy in copies[:2]:
        copy.wait()
    cell_col, cell_row = local_cells(placement_ref[...].astype(F32), place_ref[0])
    member_rows = member_rows_of(members_ref)
    ids = own_ids(member_rows, place_ref[1])
    own_ids_ref[...] = jnp.broadcast_to(ids, (16, 128))
    cells = jnp.floor(ids / 4.0)
    onehot_ref[...] = jnp.where(cell_row == cells, 1.0, 0.0)
    cell_ref[...] = jnp.broadcast_to(cell_col, (128, 128))
    want = jnp.concatenate([4.0 * cells + float(k) for k in range(4)], axis=0)
    near_cells(want, member_rows, cell_row, exchange_ids(member_rows), cells_ref, groups_ref, rows_ref, ids_ref)
    for copy in copies[2:5]:
        copy.wait()
    y = targets(0, W)
    sum_a_ref[...] = cell_sums(nearness(cell_centre(jnp.floor(ids / 4.0)), y), factor_ref, up_ref)
    sum_b_ref[...] = cell_sums(nearness(basic_centre(ids), y), factor_ref, up_ref, ONE)
    copies[5].wait()


def first_kernel(place_ref, own_ref, other_ref, sum_a_ref, sum_b_ref, ids_ref, onehot_ref, cell_ref, cells_ref, near_ref,
                 factor_ref, up_ref, whole_hbm, send_ref, here_ref, level_ref, mass_a_ref, mass_b_ref, d_ref, part_ref, whole_ref, table_ref, sems):
    copy = pltpu.make_async_copy(whole_hbm, whole_ref, sems.at[0])
    copy.start()
    ids, onehot = ids_ref[:, :1], onehot_ref[...]
    mass = []
    for part in (16, 17):
        at = pl.ds(part, 64, stride=18)
        rows = jnp.concatenate([own_ref[at, :], other_ref[at, :]], axis=0)
        mass.append(pick(onehot, rows))
    mass = jnp.concatenate(mass, axis=1)
    mass_a = ordered(mass, factor_ref)
    k = ids - 4.0 * jnp.floor(ids / 4.0)
    lane_k = lax.bitwise_and(lax.shift_right_logical(lax.broadcasted_iota(jnp.int32, (128, 128), 1), 3), 3).astype(F32)
    mass_b = jnp.where(lane_k == jnp.concatenate([k] * 8, axis=0), mass_a, 0.0)
    mass_b = mass_b + pltpu.roll(mass_b, 8, 1)
    mass_b = mass_b + pltpu.roll(mass_b, 16, 1)
    d = cell_back(balanced(mass_a, sum_a_ref[...]), factor_ref, up_ref)
    log_b = []
    for t in range(16):
        starts = [18 * (16 * x + t) for x in range(4)]
        rows = [ref[i : i + 16, :] for ref in (own_ref, other_ref) for i in starts]
        rows = jnp.concatenate(rows, axis=0)
        table_ref[:, 128 * t : 128 * t + 128] = rows
        log_b.append(pick(onehot, rows))
    here_ref[...] = table_ref[:, pl.ds(pl.multiple_of(place_ref[2] * 128, 128), 128)]
    log_b = jnp.concatenate(log_b, axis=1)
    at_basic = basic_centre(ids)
    top = 200.0 * (at_basic[0] * at_basic[0] + at_basic[1] * at_basic[1])
    part = column_part(tilt(at_basic, targets(0, W)), top, cell_back(mass_b / sum_b_ref[...], factor_ref, up_ref, ONE_BACK))
    mass_a_ref[...] = mass_a
    mass_b_ref[...] = mass_b
    d_ref[...] = d
    part_ref[...] = part
    near, cell_col = near_ref[0:256, :1], cell_ref[:, :1]

    def level(block):
        at = slice(256 * block, 256 * block + 256)
        level_ref[:, at] = near_level(near, cells_ref[...], table_ref[:, at], cell_col, targets(256 * block, 256))

    solve_pair(log_b, mass_a, mass_b, ids, d, part, factor_ref, up_ref, send_ref, level)
    copy.wait()


def received(recv_ref):
    return [jnp.concatenate([recv_ref[g, 4 * k : 4 * k + 4, :] for g in range(32)], axis=0) for k in range(4)]


def high_top(x):
    return jnp.max(jnp.where(low_half(x.shape), -jnp.inf, x), axis=1, keepdims=True)


def unpack(f):
    top = -high_top(f)
    return doubled(f, False), jnp.exp(doubled(f, True) + top), top


def a_rows(member_rows, cell_col, k):
    want = 4.0 * cell_col + float(k)
    return jnp.concatenate([jnp.where(row == want, 1.0, 0.0) for row in member_rows], axis=1).astype(BF16)


def packed(f):
    high, low = split2(f)
    return jnp.where(low_half(f.shape), high.astype(F32), swap(low.astype(F32))).astype(BF16)


def cell_halves(by_k):
    mask = low_half(by_k[0].shape)
    high = [jnp.where(mask, by_k[i], swap(by_k[i + 1])) for i in (0, 2)]
    low = [jnp.where(mask, swap(by_k[i]), by_k[i + 1]) for i in (0, 2)]
    return jnp.concatenate([jnp.concatenate(high, axis=1), jnp.concatenate(low, axis=1)], axis=0).astype(BF16)


def mix(v, d):
    peak = jnp.maximum(jnp.maximum(v[0], v[1]), jnp.maximum(v[2], v[3]))
    z = [jnp.exp(a - peak) * b for a, b in zip(v, d)]
    return peak + jnp.log((z[0] + z[1]) + (z[2] + z[3]))


def near_level(ids, cells, log_b, cell_col, y):
    return pick(cells, log_b - tilt(cell_centre(cell_col), y)) + tilt(basic_centre(ids), y)


def gathered(recv_ref, groups_ref, rows_ref):
    f = recv_ref[...].reshape(512, 128)
    by_k = dot(groups_ref[...], packed(f))
    o = rows_ref[...]
    high, mid, low = split3(f)
    two = dot(o, jnp.concatenate([high, mid], axis=1))
    e0, e1, top = unpack((two[:, :128] + two[:, 128:]) + dot(o, low))
    by_k = [by_k[256 * k : 256 * k + 256] for k in range(4)]
    return cell_halves(by_k), wide(e0[:256]), wide(e1), top


def near_margins(gather, level, centre, y, whole):
    e_cell, e0, e1, top = gather
    parts = [slice(64 * k, 64 * k + 64) for k in range(4)]
    v = level - jnp.log(cell_cols(e_cell, whole))
    d0 = basic_cols(e0, whole)
    d1 = basic_cols(e1, whole)
    q = tilt(centre, y) - top
    log_b = mix([v[a] for a in parts], [d0[a] for a in parts])
    gamma = log_b - mix([q[a] for a in parts], [d1[a] for a in parts])
    return gamma + q[256:], d1[256:]


def second_kernel(place_ref, own_ids_ref, recv_ref, level_ref, groups_ref, rows_ref, ids_ref, mass_a_ref, mass_b_ref, d_ref,
                  part_ref, factor_ref, up_ref, whole_ref, send_ref, here_ref):
    here_ref[...] = whole_ref[:, pl.ds(pl.multiple_of(place_ref[2] * 128, 128), 128)]
    gather = gathered(recv_ref, groups_ref, rows_ref)
    centre = basic_centre(ids_ref[:, :1])
    log_b = []
    for block in range(8):
        at = slice(block * 256, block * 256 + 256)
        v, d = near_margins(gather, level_ref[:, at], centre, targets(256 * block, 256), whole_ref[:, at])
        log_b.append(mix([v[16 * k : 16 * k + 16] for k in range(4)], [d[16 * k : 16 * k + 16] for k in range(4)]))
    solve_pair(jnp.concatenate(log_b, axis=1), mass_a_ref[...], mass_b_ref[...], own_ids_ref[:, :1], d_ref[...], part_ref[...],
               factor_ref, up_ref, send_ref)


def middle_kernel(place_ref, placement_ref, members_ref, log_b_ref, recv_ref, whole_ref, level_ref, cells_ref, groups_ref,
                  rows_ref, ids_ref):
    cell_col, cell_row = local_cells(placement_ref[...].astype(F32), place_ref[0])
    member_rows = member_rows_of(members_ref)
    share = place_ref[2]
    y = targets(share * 128, 128)
    whole = whole_ref[...]
    b_ids = [to_col(row) for row in member_rows]
    b_cell = jnp.concatenate([jnp.where(cell_row == jnp.floor(i / 4.0), 1.0, 0.0) for i in b_ids], axis=0)
    b_tilt = [tilt(basic_centre(i), y) for i in b_ids]
    a_tilt = [tilt(basic_centre(4.0 * cell_col + float(k)), y) for k in range(4)]
    parts = [slice(128 * k, 128 * k + 128) for k in range(4)]
    every = jnp.concatenate(received(recv_ref), axis=0)
    hits = [a_rows(member_rows, cell_col, k) for k in range(4)]
    rows = packed(every)
    e_cell = cell_halves([dot(h, rows) for h in hits])
    by_k = jnp.concatenate([pick(h, every) for h in hits], axis=0)
    gamma = pick(b_cell, log_b_ref[...] - jnp.log(cell_cols(e_cell, whole)) - tilt(cell_centre(cell_col), y))
    e0, e1, top = unpack(every)
    _, ea, a_top = unpack(by_k)
    d0, d1, da = [basic_cols(wide(e), whole) for e in (e0, e1, ea)]
    log_b1 = mix([gamma[a] + t for a, t in zip(parts, b_tilt)], [d0[a] for a in parts])
    gamma1 = log_b1 - mix([t - top[a] for a, t in zip(parts, b_tilt)], [d1[a] for a in parts])
    log_b = []
    for k in range(4):
        hit = hits[k].astype(F32)
        slot = (hit[:, :128] + hit[:, 128:256]) + (hit[:, 256:384] + hit[:, 384:])
        log_b.append(pick(slot, gamma1) + a_tilt[k] - a_top[parts[k]])
    log_b = mix(log_b, [da[a] for a in parts])
    lane = lax.broadcasted_iota(jnp.int32, (16, 128), 1)
    first = place_ref[3] * 16 + lax.broadcasted_iota(jnp.int32, (16, 128), 0)
    own_cells = jnp.sum(jnp.where(lane == first, jnp.broadcast_to(cell_row, (16, 128)), 0.0), axis=1, keepdims=True)
    want = jnp.concatenate([4.0 * own_cells + float(k) for k in range(4)], axis=0)
    ids, cells = near_cells(want, member_rows, cell_row, exchange_ids(member_rows), cells_ref, groups_ref, rows_ref, ids_ref)
    level_ref[...] = near_level(ids[:256], cells, log_b, cell_col, y)


def last_kernel(place_ref, recv_ref, level_ref, groups_ref, rows_ref, ids_ref, whole_ref, out_ref):
    centre = basic_centre(ids_ref[:, :1])
    v, d = near_margins(gathered(recv_ref, groups_ref, rows_ref), level_ref[...], centre,
                        targets(place_ref[2] * 128, 128), whole_ref[...])
    out = jnp.exp(v + jnp.log(d))
    for k in range(4):
        out_ref[:, k, :] = out[16 * k : 16 * k + 16]


def call(body, inputs, outs, scratch=(), work=1, far=0):
    near = len(inputs) - far
    inputs = inputs[:near] + tuple(pltpu.with_memory_space_constraint(v, pltpu.HBM) for v in inputs[near:])

    def spec(value):
        return pl.BlockSpec(memory_space=pltpu.SMEM if value.shape == (4,) else pltpu.VMEM)

    return pl.pallas_call(
        body,
        out_shape=[jax.ShapeDtypeStruct(s[:-1], BF16) if s[-1] is BF16 else jax.ShapeDtypeStruct(s, F32) for s in outs],
        in_specs=[spec(value) for value in inputs[:near]] + [pl.BlockSpec(memory_space=pltpu.HBM)] * far,
        out_specs=[pl.BlockSpec(memory_space=pltpu.VMEM)] * len(outs),
        scratch_shapes=list(scratch),
        compiler_params=pltpu.CompilerParams(vmem_limit_bytes=24 * 2**20),
        cost_estimate=pl.CostEstimate(flops=work * 10**9, bytes_accessed=10**6, transcendentals=0),
    )(*inputs)


FACTORS = [(3072, 128, BF16), (1024, 128)]
NEAR = [(256, 128, BF16), (1024, 512, BF16), (320, 512, BF16), (320, 128)]


def on_device(placement_a, members_b, source_mass, init_log, factors, wholes, ups):
    x, c, z, y = (lax.axis_index(name) for name in ("x", "c", "z", "y"))
    share = z * 4 + y
    place = jnp.stack([c, x * 8 + c * 4 + y, share, x]).astype(jnp.int32)
    index = (place, placement_a.reshape(1, 128), members_b.T)
    v = [init_log[:, k, :] for k in range(4)]
    peak = jnp.maximum(jnp.maximum(v[0], v[1]), jnp.maximum(v[2], v[3]))
    e = [jnp.exp(a - peak) for a in v]
    log_b = peak + jnp.log((e[0] + e[1]) + (e[2] + e[3])) + float(np.log(64.0 / W))
    mass = lax.dynamic_slice_in_dim(source_mass, share, 1, 0).reshape(2, 128)
    block = jnp.concatenate([log_b, mass], axis=0).reshape(9, 2, 128)
    own = lax.all_to_all(jnp.broadcast_to(block[None], (64, 9, 2, 128)), ("x", "z", "y"), 0, 0, tiled=True)
    sum_a, sum_b, factors, ups, held, onehot, cell, cells, groups, rows, ids = call(
        start_kernel, index + (factors, ups), [(128, 128), (128, 128)] + FACTORS + [(16, 128), (16, 128), (128, 128)] + NEAR,
        [pltpu.VMEM((1, 128), jnp.int32), pltpu.VMEM((4, 128), jnp.int32), pltpu.SemaphoreType.DMA((6,))], far=4)
    other = lax.ppermute(own, "c", [(0, 1), (1, 0)]).reshape(1152, 128)
    own = own.reshape(1152, 128)

    def exchange(rows):
        return lax.all_to_all(rows, ("x", "c", "y"), 0, 0, tiled=True)

    send, here, level, *rest, wholes = call(
        first_kernel, (place, own, other, sum_a, sum_b, held, onehot, cell, cells, ids, factors, ups, wholes),
        [(32, 16, 128), (128, 128), (256, W), (128, 128), (128, 128), (16, W), (8, W), (768, W, BF16)],
        [pltpu.VMEM((128, W), F32), pltpu.SemaphoreType.DMA((1,))], far=1)
    first = exchange(send)
    send, whole = call(second_kernel, (place, held, first, level, groups, rows, ids, *rest, factors, ups, wholes),
                       [(32, 16, 128), (768, 128, BF16)])
    second = exchange(send)
    level, _, groups, rows, ids = call(middle_kernel, index + (here, first, whole), [(256, 128)] + NEAR)
    (out,) = call(last_kernel, (place, second, level, groups, rows, ids, whole), [(16, 4, 128)])
    return out


def solution(mesh):
    split = Mesh(mesh.devices.reshape(4, 2, 4, 4), ("x", "c", "z", "y"))
    tables = _tables()
    placed = (P(), P(), P(("x", "c"), None), P(("x", "c"), None, ("z", "y"))) + (P(),) * len(tables)
    body = jax.shard_map(
        on_device, mesh=split, in_specs=placed, out_specs=P(("x", "c"), None, ("z", "y")), check_vma=False
    )

    def run(placement_a, members_b, source_mass, init_log):
        return body(placement_a, members_b, source_mass, init_log, *(jnp.asarray(t) for t in tables))

    return run
```

```python
import numpy as np
import ml_dtypes

import jax
import jax.numpy as jnp
from jax import lax
from jax.experimental import pallas as pl
from jax.experimental.pallas import tpu as pltpu
from jax.sharding import Mesh, PartitionSpec as P

F32 = jnp.float32
BF16 = jnp.bfloat16
W = 2048
CENTRE = (slice(48, 64), slice(15, 16))


def _halves(matrix):
    high = matrix.astype(ml_dtypes.bfloat16)
    low = (matrix - high.astype(np.float64)).astype(ml_dtypes.bfloat16)
    return high, low


def _thrice(matrix):
    high, low = _halves(matrix)
    return np.concatenate([high, high, low], axis=0)


def _tables():
    yh = (np.arange(32) + 0.5) / 32 - 0.5
    ya = (np.arange(64) + 0.5) / 64 - 0.5
    dh = (np.arange(8) - 3.5) / 128
    da = (np.arange(8) - 3.5) / 256
    shifts = [(k - 1.5) / 32 for k in range(4)]

    def whole(shift):
        up = np.exp(400.0 * dh[:, None] * yh[None])
        along = np.exp(400.0 * (da + shift)[:, None] * ya[None])
        return (up[:, None, :, None] * along[None, :, None, :]).reshape(64, W)

    cell = np.concatenate([np.exp(400.0 * ya[:, None] * (da + s)[None]) for s in shifts], axis=1)
    high, low = _halves(np.concatenate([cell.T, cell.T], axis=1))
    one = np.exp(400.0 * ya[:, None] * da[None])
    turned = _halves(np.concatenate([one.T, one.T], axis=1))
    turned = (turned[0],) + turned + (np.zeros_like(turned[0]),)
    order = np.zeros((8, 4, 8, 8, 4, 4, 8), ml_dtypes.bfloat16)
    for i, k, r in np.ndindex(8, 4, 8):
        order[i, k, i, r, :, k, r] = 1
    factors = [
        _thrice(np.tile(cell, (2, 4))),
        np.concatenate([high, high, low, np.zeros_like(low)], axis=0),
        order.reshape(2048, 128),
        _thrice(np.tile(one, (2, 16))),
        np.concatenate([np.concatenate([m, np.zeros((24, 128), m.dtype)], axis=0) for m in turned], axis=0),
    ]
    high, low = _halves(whole(0.0))
    wholes = _halves(np.concatenate([whole(s) for s in shifts], axis=0)) + (high, high, low, np.zeros_like(low))
    up = np.exp(400.0 * yh.reshape(16, 2, 1) * dh[None, None])
    of_row = np.repeat(up.transpose(0, 2, 1).reshape(128, 1, 2), 64, axis=2)
    ups = np.repeat(of_row, 8, axis=1).reshape(1024, 128)
    return np.concatenate(factors, axis=0), np.concatenate(wholes, axis=0), ups.astype(np.float32)


CELL, BACK, ORDER, ONE, ONE_BACK = 0, 384, 512, 2560, 2944


def dot(a, b):
    return jnp.dot(a, b, preferred_element_type=F32)


def split2(x):
    high = x.astype(BF16)
    return high, (x - high.astype(F32)).astype(BF16)


def split3(x):
    high = x.astype(BF16)
    rest = x - high.astype(F32)
    mid = rest.astype(BF16)
    return high, mid, (rest - mid.astype(F32)).astype(BF16)


def pick(onehot, x):
    o = onehot.astype(BF16)
    return dot(jnp.concatenate([o, o, o], axis=1), jnp.concatenate(split3(x), axis=0))


def targets(first, count):
    j = first + lax.broadcasted_iota(jnp.int32, (1, count), 1)
    yh = (lax.shift_right_logical(j, 6).astype(F32) + 0.5) / 32.0 - 0.5
    ya = (lax.bitwise_and(j, 63).astype(F32) + 0.5) / 64.0 - 0.5
    return yh, ya


def basic_centre(ids):
    row = jnp.floor(ids / 32.0)
    return (row * 8.0 + 4.0) / 128.0 - 0.5, ((ids - row * 32.0) * 8.0 + 4.0) / 256.0 - 0.5


def cell_centre(cells):
    row = jnp.floor(cells / 8.0)
    return (row * 8.0 + 4.0) / 128.0 - 0.5, ((cells - row * 8.0) * 32.0 + 16.0) / 256.0 - 0.5


def tilt(centre, y):
    return (400.0 * centre[0]) * y[0] + (400.0 * centre[1]) * y[1]


def eye_mask():
    return lax.broadcasted_iota(jnp.int32, (128, 128), 0) == lax.broadcasted_iota(jnp.int32, (128, 128), 1)


def to_col(row):
    return jnp.sum(jnp.where(eye_mask(), jnp.broadcast_to(row, (128, 128)), 0.0), axis=1, keepdims=True)


def to_row(col):
    return jnp.sum(jnp.where(eye_mask(), jnp.broadcast_to(col, (128, 128)), 0.0), axis=0, keepdims=True)


def local_cells(placement_row, core):
    dst = lax.broadcasted_iota(jnp.int32, (128, 128), 0)
    src = lax.broadcasted_iota(jnp.int32, (128, 128), 1)
    side = lax.bitwise_xor(lax.shift_right_logical(dst, 6), core)
    slot = lax.bitwise_and(lax.shift_right_logical(dst, 4), 3) * 32 + side * 16 + lax.bitwise_and(dst, 15)
    col = jnp.sum(jnp.where(slot == src, jnp.broadcast_to(placement_row, (128, 128)), 0.0), axis=1, keepdims=True)
    return col, to_row(col)


def own_ids(member_rows, group):
    lane = lax.broadcasted_iota(jnp.int32, (16, 128), 1)
    sub = lax.broadcasted_iota(jnp.int32, (16, 128), 0)
    k = lax.shift_right_logical(sub, 2)
    rows = jnp.zeros((16, 128), F32)
    for i in range(4):
        rows = jnp.where(k == i, jnp.broadcast_to(member_rows[i], (16, 128)), rows)
    return jnp.sum(jnp.where(lane == 4 * group + lax.bitwise_and(sub, 3), rows, 0.0), axis=1, keepdims=True)


def low_half(shape):
    return lax.broadcasted_iota(jnp.int32, shape, 1) < 64


def swap(x):
    return pltpu.roll(x, 64, 1)


def doubled(x, upper):
    mask = low_half(x.shape)
    return jnp.where(mask, swap(x), x) if upper else jnp.where(mask, x, swap(x))


def thrice(x):
    high, low = split2(x)
    return jnp.concatenate([high, low, high], axis=1)


def up_of(up_ref, i):
    h = up_ref[8 * i : 8 * i + 8, :]
    return jnp.concatenate([h, h], axis=0)


def total(parts):
    while len(parts) > 1:
        parts = [parts[i] + parts[i + 1] for i in range(0, len(parts), 2)]
    return parts[0]


def cell_sums(u, factor_ref, up_ref, first=CELL):
    v = [None] * 8
    for t in range(16):
        part = u[:, 128 * t : 128 * t + 128]
        for i in range(8):
            term = part * up_of(up_ref, 8 * t + i)
            v[i] = term if t == 0 else v[i] + term
    return dot(thrice(jnp.concatenate(v, axis=0)), factor_ref[first : first + 384, :])


def cell_back(e, factor_ref, up_ref, first=BACK):
    high = e.astype(BF16).astype(F32)
    lane = lax.broadcasted_iota(jnp.int32, e.shape, 1)
    x = jnp.where(lax.shift_right_logical(lane, 5) == 1, e - high, high).astype(BF16)
    z = dot(x, factor_ref[first : first + 128, :])
    z = [z[16 * i : 16 * i + 16] for i in range(8)]
    return jnp.concatenate(
        [total([z[i] * up_of(up_ref, 8 * t + i) for i in range(8)]) for t in range(16)], axis=1)


def ordered(mass, factor_ref):
    x = jnp.concatenate(split3(mass), axis=0)
    out = []
    for i in range(8):
        p = dot(x, factor_ref[ORDER + 256 * i : ORDER + 256 * i + 256, :])
        out.append((p[:16] + p[16:32]) + p[32:])
    return jnp.concatenate(out, axis=0)


def spread(e):
    row = lax.bitwise_and(lax.shift_right_logical(lax.broadcasted_iota(jnp.int32, (16, 128), 1), 3), 7)
    out = e[:16]
    for i in range(1, 8):
        out = jnp.where(row == i, e[16 * i : 16 * i + 16], out)
    return out


def wide(e):
    high = e.astype(BF16).astype(F32)
    return jnp.concatenate([jnp.where(low_half(e.shape), high, e - high), high], axis=1).astype(BF16)


def cell_cols(e, whole):
    n = e.shape[0] // 2
    p = dot(e, whole[:256])
    return p[:n] + p[n:] + dot(e[:n], whole[256:512])


def basic_cols(e, whole):
    return dot(e, whole[512:])


def nearness(centre, y):
    return jnp.exp(-200.0 * ((centre[0] - y[0]) ** 2 + (centre[1] - y[1]) ** 2))


def balanced(mass, s):
    return mass * (jnp.concatenate([s[CENTRE]] * 8, axis=0) / s)


def sweep_a(log_b, mass, d, factor_ref, up_ref, beside):
    b = jnp.exp(log_b - jnp.max(log_b, axis=1, keepdims=True))
    for i in range(3):
        beside(i)
        u = b / d
        s = cell_sums(u, factor_ref, up_ref)
        d = cell_back(balanced(mass, s), factor_ref, up_ref)
    return u, s[CENTRE], d


def over_k(x, op):
    y = op(x[:8], x[8:])
    return op(y, pltpu.roll(y, 4, 0))


def twice(x):
    return jnp.concatenate([x, x], axis=0)


def column_part(r, top, d):
    q = r - top
    peak = over_k(q, jnp.maximum)
    return peak + jnp.log(over_k(jnp.exp(q - twice(peak)) * d, jnp.add))


def sweep_b(log_b, mass, r, part, factor_ref, up_ref, beside):
    for i in range(3):
        beside(5 + i)
        v = r + twice(log_b - part)
        top = jnp.max(v, axis=1, keepdims=True)
        e = mass / cell_sums(jnp.exp(v - top), factor_ref, up_ref, ONE)
        if i < 2:
            part = column_part(r, top, cell_back(e, factor_ref, up_ref, ONE_BACK))
    return e, top


def solve_pair(log_b_a, mass_a, mass_b, ids, d, part, factor_ref, up_ref, send_ref, beside=lambda i: None):
    y = targets(0, W)
    at_cell = cell_centre(jnp.floor(ids / 4.0))
    at_basic = basic_centre(ids)
    shift = (400.0 * (at_basic[1] - at_cell[1])) * y[1]
    u, centre, d_a = sweep_a(log_b_a, mass_a, d, factor_ref, up_ref, beside)
    s = cell_sums(u * jnp.exp(shift), factor_ref, up_ref, ONE)
    e_first = mass_b * (jnp.concatenate([centre] * 8, axis=0) / s)
    beside(3)
    d_first = cell_back(e_first, factor_ref, up_ref, ONE_BACK)
    v = log_b_a - jnp.log(d_a) + shift
    peak = over_k(v, jnp.maximum)
    beside(4)
    log_b_b = peak + jnp.log(over_k(jnp.exp(v - twice(peak)) * d_first, jnp.add))
    e_second, top = sweep_b(log_b_b, mass_b, tilt(at_basic, y), part, factor_ref, up_ref, beside)
    rows = jnp.where(low_half((16, 128)), spread(e_first), jnp.log(spread(e_second)) - top)
    for i in range(32):
        send_ref[i, :, :] = rows


def member_rows_of(members_ref):
    members = members_ref[...].astype(F32)
    return [members[k : k + 1, :] for k in range(4)]


def exchange_ids(member_rows):
    members = [to_col(row) for row in member_rows]
    slot = lax.broadcasted_iota(jnp.int32, (128, 128), 0)
    lane = lax.broadcasted_iota(jnp.int32, (128, 128), 1)
    k = lax.bitwise_and(lax.shift_right_logical(lane, 2), 3)
    value = jnp.broadcast_to(members[0], (128, 128))
    for i in range(1, 4):
        value = jnp.where(k == i, jnp.broadcast_to(members[i], (128, 128)), value)
    of_lane = 4 * lax.shift_right_logical(lane, 4) + lax.bitwise_and(lane, 3)
    return jnp.concatenate(
        [jnp.sum(jnp.where(slot == of_lane + 32 * t, value, 0.0), axis=0, keepdims=True) for t in range(4)], axis=1)


def near_cells(want, member_rows, cell_row, exchanged, cells_ref, groups_ref, rows_ref, ids_ref):
    hits = [jnp.where(row == want, 1.0, 0.0) for row in member_rows]
    slot = (hits[0] + hits[1]) + (hits[2] + hits[3])
    ids = jnp.concatenate([jnp.sum(slot * row, axis=1, keepdims=True) for row in member_rows], axis=0)
    cell = jnp.floor(ids / 4.0)
    cells = jnp.where(cell_row == cell, 1.0, 0.0)
    cells_ref[...] = cells.astype(BF16)
    for k in range(4):
        groups_ref[256 * k : 256 * k + 256, :] = jnp.where(exchanged == 4.0 * cell + float(k), 1.0, 0.0).astype(BF16)
    ids = jnp.concatenate([ids, want], axis=0)
    rows_ref[...] = jnp.where(exchanged == ids, 1.0, 0.0).astype(BF16)
    ids_ref[...] = jnp.broadcast_to(ids, (320, 128))
    return ids, cells


def start_kernel(place_ref, placement_hbm, members_hbm, factor_hbm, up_hbm, sum_a_ref, sum_b_ref, factor_ref, up_ref, own_ids_ref, onehot_ref,
                 cell_ref, cells_ref, groups_ref, rows_ref, ids_ref, placement_ref, members_ref, sems):
    pairs = [(placement_hbm, placement_ref), (members_hbm, members_ref), (up_hbm, up_ref)]
    pairs += [(factor_hbm.at[at, :], factor_ref.at[at, :]) for at in (pl.ds(0, ORDER), pl.ds(ONE, 512), pl.ds(ORDER, ONE - ORDER))]
    copies = [pltpu.make_async_copy(*pair, sems.at[i]) for i, pair in enumerate(pairs)]
    for copy in copies:
        copy.start()
    for copy in copies[:2]:
        copy.wait()
    cell_col, cell_row = local_cells(placement_ref[...].astype(F32), place_ref[0])
    member_rows = member_rows_of(members_ref)
    ids = own_ids(member_rows, place_ref[1])
    own_ids_ref[...] = jnp.broadcast_to(ids, (16, 128))
    cells = jnp.floor(ids / 4.0)
    onehot_ref[...] = jnp.where(cell_row == cells, 1.0, 0.0)
    cell_ref[...] = jnp.broadcast_to(cell_col, (128, 128))
    want = jnp.concatenate([4.0 * cells + float(k) for k in range(4)], axis=0)
    near_cells(want, member_rows, cell_row, exchange_ids(member_rows), cells_ref, groups_ref, rows_ref, ids_ref)
    for copy in copies[2:5]:
        copy.wait()
    y = targets(0, W)
    sum_a_ref[...] = cell_sums(nearness(cell_centre(jnp.floor(ids / 4.0)), y), factor_ref, up_ref)
    sum_b_ref[...] = cell_sums(nearness(basic_centre(ids), y), factor_ref, up_ref, ONE)
    copies[5].wait()


def first_kernel(place_ref, own_ref, other_ref, sum_a_ref, sum_b_ref, ids_ref, onehot_ref, cell_ref, cells_ref, near_ref,
                 factor_ref, up_ref, whole_hbm, send_ref, here_ref, level_ref, mass_a_ref, mass_b_ref, d_ref, part_ref, whole_ref, table_ref, sems):
    copy = pltpu.make_async_copy(whole_hbm, whole_ref, sems.at[0])
    copy.start()
    ids, onehot = ids_ref[:, :1], onehot_ref[...]
    mass = []
    for part in (16, 17):
        at = pl.ds(part, 64, stride=18)
        rows = jnp.concatenate([own_ref[at, :], other_ref[at, :]], axis=0)
        mass.append(pick(onehot, rows))
    mass = jnp.concatenate(mass, axis=1)
    mass_a = ordered(mass, factor_ref)
    k = ids - 4.0 * jnp.floor(ids / 4.0)
    lane_k = lax.bitwise_and(lax.shift_right_logical(lax.broadcasted_iota(jnp.int32, (128, 128), 1), 3), 3).astype(F32)
    mass_b = jnp.where(lane_k == jnp.concatenate([k] * 8, axis=0), mass_a, 0.0)
    mass_b = mass_b + pltpu.roll(mass_b, 8, 1)
    mass_b = mass_b + pltpu.roll(mass_b, 16, 1)
    d = cell_back(balanced(mass_a, sum_a_ref[...]), factor_ref, up_ref)
    log_b = []
    for t in range(16):
        starts = [18 * (16 * x + t) for x in range(4)]
        rows = [ref[i : i + 16, :] for ref in (own_ref, other_ref) for i in starts]
        rows = jnp.concatenate(rows, axis=0)
        table_ref[:, 128 * t : 128 * t + 128] = rows
        log_b.append(pick(onehot, rows))
    here_ref[...] = table_ref[:, pl.ds(pl.multiple_of(place_ref[2] * 128, 128), 128)]
    log_b = jnp.concatenate(log_b, axis=1)
    at_basic = basic_centre(ids)
    top = 200.0 * (at_basic[0] * at_basic[0] + at_basic[1] * at_basic[1])
    part = column_part(tilt(at_basic, targets(0, W)), top, cell_back(mass_b / sum_b_ref[...], factor_ref, up_ref, ONE_BACK))
    mass_a_ref[...] = mass_a
    mass_b_ref[...] = mass_b
    d_ref[...] = d
    part_ref[...] = part
    near, cell_col = near_ref[0:256, :1], cell_ref[:, :1]

    def level(block):
        at = slice(256 * block, 256 * block + 256)
        level_ref[:, at] = near_level(near, cells_ref[...], table_ref[:, at], cell_col, targets(256 * block, 256))

    solve_pair(log_b, mass_a, mass_b, ids, d, part, factor_ref, up_ref, send_ref, lambda i: [level(b) for b in LEVELS[i]])
    copy.wait()


def received(recv_ref):
    return [jnp.concatenate([recv_ref[g, 4 * k : 4 * k + 4, :] for g in range(32)], axis=0) for k in range(4)]


def high_top(x):
    return jnp.max(jnp.where(low_half(x.shape), -jnp.inf, x), axis=1, keepdims=True)


def unpack(f):
    top = -high_top(f)
    return doubled(f, False), jnp.exp(doubled(f, True) + top), top


def a_rows(member_rows, cell_col, k):
    want = 4.0 * cell_col + float(k)
    return jnp.concatenate([jnp.where(row == want, 1.0, 0.0) for row in member_rows], axis=1).astype(BF16)


def packed(f):
    high, low = split2(f)
    return jnp.where(low_half(f.shape), high.astype(F32), swap(low.astype(F32))).astype(BF16)


def cell_halves(by_k):
    mask = low_half(by_k[0].shape)
    high = [jnp.where(mask, by_k[i], swap(by_k[i + 1])) for i in (0, 2)]
    low = [jnp.where(mask, swap(by_k[i]), by_k[i + 1]) for i in (0, 2)]
    return jnp.concatenate([jnp.concatenate(high, axis=1), jnp.concatenate(low, axis=1)], axis=0).astype(BF16)


def mix(v, d):
    peak = jnp.maximum(jnp.maximum(v[0], v[1]), jnp.maximum(v[2], v[3]))
    z = [jnp.exp(a - peak) * b for a, b in zip(v, d)]
    return peak + jnp.log((z[0] + z[1]) + (z[2] + z[3]))


def near_level(ids, cells, log_b, cell_col, y):
    return pick(cells, log_b - tilt(cell_centre(cell_col), y)) + tilt(basic_centre(ids), y)


def gathered(recv_ref, groups_ref, rows_ref):
    f = recv_ref[...].reshape(512, 128)
    by_k = dot(groups_ref[...], packed(f))
    o = rows_ref[...]
    high, mid, low = split3(f)
    two = dot(o, jnp.concatenate([high, mid], axis=1))
    e0, e1, top = unpack((two[:, :128] + two[:, 128:]) + dot(o, low))
    by_k = [by_k[256 * k : 256 * k + 256] for k in range(4)]
    return cell_halves(by_k), wide(e0[:256]), wide(e1), top


def near_margins(gather, level, centre, y, whole):
    e_cell, e0, e1, top = gather
    parts = [slice(64 * k, 64 * k + 64) for k in range(4)]
    v = level - jnp.log(cell_cols(e_cell, whole))
    d0 = basic_cols(e0, whole)
    d1 = basic_cols(e1, whole)
    q = tilt(centre, y) - top
    log_b = mix([v[a] for a in parts], [d0[a] for a in parts])
    gamma = log_b - mix([q[a] for a in parts], [d1[a] for a in parts])
    return gamma + q[256:], d1[256:]


def second_kernel(place_ref, own_ids_ref, recv_ref, level_ref, groups_ref, rows_ref, ids_ref, mass_a_ref, mass_b_ref, d_ref,
                  part_ref, factor_ref, up_ref, whole_ref, send_ref, here_ref):
    here_ref[...] = whole_ref[:, pl.ds(pl.multiple_of(place_ref[2] * 128, 128), 128)]
    gather = gathered(recv_ref, groups_ref, rows_ref)
    centre = basic_centre(ids_ref[:, :1])
    log_b = []
    for block in range(8):
        at = slice(block * 256, block * 256 + 256)
        v, d = near_margins(gather, level_ref[:, at], centre, targets(256 * block, 256), whole_ref[:, at])
        log_b.append(mix([v[16 * k : 16 * k + 16] for k in range(4)], [d[16 * k : 16 * k + 16] for k in range(4)]))
    solve_pair(jnp.concatenate(log_b, axis=1), mass_a_ref[...], mass_b_ref[...], own_ids_ref[:, :1], d_ref[...], part_ref[...],
               factor_ref, up_ref, send_ref)


def middle_kernel(place_ref, placement_ref, members_ref, log_b_ref, recv_ref, whole_ref, level_ref, cells_ref, groups_ref,
                  rows_ref, ids_ref):
    cell_col, cell_row = local_cells(placement_ref[...].astype(F32), place_ref[0])
    member_rows = member_rows_of(members_ref)
    share = place_ref[2]
    y = targets(share * 128, 128)
    whole = whole_ref[...]
    b_ids = [to_col(row) for row in member_rows]
    b_cell = jnp.concatenate([jnp.where(cell_row == jnp.floor(i / 4.0), 1.0, 0.0) for i in b_ids], axis=0)
    b_tilt = [tilt(basic_centre(i), y) for i in b_ids]
    a_tilt = [tilt(basic_centre(4.0 * cell_col + float(k)), y) for k in range(4)]
    parts = [slice(128 * k, 128 * k + 128) for k in range(4)]
    every = jnp.concatenate(received(recv_ref), axis=0)
    hits = [a_rows(member_rows, cell_col, k) for k in range(4)]
    rows = packed(every)
    e_cell = cell_halves([dot(h, rows) for h in hits])
    by_k = jnp.concatenate([pick(h, every) for h in hits], axis=0)
    gamma = pick(b_cell, log_b_ref[...] - jnp.log(cell_cols(e_cell, whole)) - tilt(cell_centre(cell_col), y))
    e0, e1, top = unpack(every)
    _, ea, a_top = unpack(by_k)
    d0, d1, da = [basic_cols(wide(e), whole) for e in (e0, e1, ea)]
    log_b1 = mix([gamma[a] + t for a, t in zip(parts, b_tilt)], [d0[a] for a in parts])
    gamma1 = log_b1 - mix([t - top[a] for a, t in zip(parts, b_tilt)], [d1[a] for a in parts])
    log_b = []
    for k in range(4):
        hit = hits[k].astype(F32)
        slot = (hit[:, :128] + hit[:, 128:256]) + (hit[:, 256:384] + hit[:, 384:])
        log_b.append(pick(slot, gamma1) + a_tilt[k] - a_top[parts[k]])
    log_b = mix(log_b, [da[a] for a in parts])
    lane = lax.broadcasted_iota(jnp.int32, (16, 128), 1)
    first = place_ref[3] * 16 + lax.broadcasted_iota(jnp.int32, (16, 128), 0)
    own_cells = jnp.sum(jnp.where(lane == first, jnp.broadcast_to(cell_row, (16, 128)), 0.0), axis=1, keepdims=True)
    want = jnp.concatenate([4.0 * own_cells + float(k) for k in range(4)], axis=0)
    ids, cells = near_cells(want, member_rows, cell_row, exchange_ids(member_rows), cells_ref, groups_ref, rows_ref, ids_ref)
    level_ref[...] = near_level(ids[:256], cells, log_b, cell_col, y)


def last_kernel(place_ref, recv_ref, level_ref, groups_ref, rows_ref, ids_ref, whole_ref, out_ref):
    centre = basic_centre(ids_ref[:, :1])
    v, d = near_margins(gathered(recv_ref, groups_ref, rows_ref), level_ref[...], centre,
                        targets(place_ref[2] * 128, 128), whole_ref[...])
    out = jnp.exp(v + jnp.log(d))
    for k in range(4):
        out_ref[:, k, :] = out[16 * k : 16 * k + 16]


def call(body, inputs, outs, scratch=(), work=1, far=0):
    near = len(inputs) - far
    inputs = inputs[:near] + tuple(pltpu.with_memory_space_constraint(v, pltpu.HBM) for v in inputs[near:])

    def spec(value):
        return pl.BlockSpec(memory_space=pltpu.SMEM if value.shape == (4,) else pltpu.VMEM)

    return pl.pallas_call(
        body,
        out_shape=[jax.ShapeDtypeStruct(s[:-1], BF16) if s[-1] is BF16 else jax.ShapeDtypeStruct(s, F32) for s in outs],
        in_specs=[spec(value) for value in inputs[:near]] + [pl.BlockSpec(memory_space=pltpu.HBM)] * far,
        out_specs=[pl.BlockSpec(memory_space=pltpu.VMEM)] * len(outs),
        scratch_shapes=list(scratch),
        compiler_params=pltpu.CompilerParams(vmem_limit_bytes=24 * 2**20),
        cost_estimate=pl.CostEstimate(flops=work * 10**9, bytes_accessed=10**6, transcendentals=0),
    )(*inputs)


LEVELS = ((0, 1), (2, 3), (4, 5), (6,), (7,), (), (), ())
FACTORS = [(3072, 128, BF16), (1024, 128)]
NEAR = [(256, 128, BF16), (1024, 512, BF16), (320, 512, BF16), (320, 128)]


def on_device(placement_a, members_b, source_mass, init_log, factors, wholes, ups):
    x, c, z, y = (lax.axis_index(name) for name in ("x", "c", "z", "y"))
    share = z * 4 + y
    place = jnp.stack([c, x * 8 + c * 4 + y, share, x]).astype(jnp.int32)
    index = (place, placement_a.reshape(1, 128), members_b.T)
    v = [init_log[:, k, :] for k in range(4)]
    peak = jnp.maximum(jnp.maximum(v[0], v[1]), jnp.maximum(v[2], v[3]))
    e = [jnp.exp(a - peak) for a in v]
    log_b = peak + jnp.log((e[0] + e[1]) + (e[2] + e[3])) + float(np.log(64.0 / W))
    mass = lax.dynamic_slice_in_dim(source_mass, share, 1, 0).reshape(2, 128)
    block = jnp.concatenate([log_b, mass], axis=0).reshape(9, 2, 128)
    own = lax.all_to_all(jnp.broadcast_to(block[None], (64, 9, 2, 128)), ("x", "z", "y"), 0, 0, tiled=True)
    sum_a, sum_b, factors, ups, held, onehot, cell, cells, groups, rows, ids = call(
        start_kernel, index + (factors, ups), [(128, 128), (128, 128)] + FACTORS + [(16, 128), (16, 128), (128, 128)] + NEAR,
        [pltpu.VMEM((1, 128), jnp.int32), pltpu.VMEM((4, 128), jnp.int32), pltpu.SemaphoreType.DMA((6,))], far=4)
    other = lax.ppermute(own, "c", [(0, 1), (1, 0)]).reshape(1152, 128)
    own = own.reshape(1152, 128)

    def exchange(rows):
        return lax.all_to_all(rows, ("x", "c", "y"), 0, 0, tiled=True)

    send, here, level, *rest, wholes = call(
        first_kernel, (place, own, other, sum_a, sum_b, held, onehot, cell, cells, ids, factors, ups, wholes),
        [(32, 16, 128), (128, 128), (256, W), (128, 128), (128, 128), (16, W), (8, W), (768, W, BF16)],
        [pltpu.VMEM((128, W), F32), pltpu.SemaphoreType.DMA((1,))], far=1)
    first = exchange(send)
    send, whole = call(second_kernel, (place, held, first, level, groups, rows, ids, *rest, factors, ups, wholes),
                       [(32, 16, 128), (768, 128, BF16)])
    second = exchange(send)
    level, _, groups, rows, ids = call(middle_kernel, index + (here, first, whole), [(256, 128)] + NEAR)
    (out,) = call(last_kernel, (place, second, level, groups, rows, ids, whole), [(16, 4, 128)])
    return out


def solution(mesh):
    split = Mesh(mesh.devices.reshape(4, 2, 4, 4), ("x", "c", "z", "y"))
    tables = _tables()
    placed = (P(), P(), P(("x", "c"), None), P(("x", "c"), None, ("z", "y"))) + (P(),) * len(tables)
    body = jax.shard_map(
        on_device, mesh=split, in_specs=placed, out_specs=P(("x", "c"), None, ("z", "y")), check_vma=False
    )

    def run(placement_a, members_b, source_mass, init_log):
        return body(placement_a, members_b, source_mass, init_log, *(jnp.asarray(t) for t in tables))

    return run
```

```python
import numpy as np
import ml_dtypes

import jax
import jax.numpy as jnp
from jax import lax
from jax.experimental import pallas as pl
from jax.experimental.pallas import tpu as pltpu
from jax.sharding import Mesh, PartitionSpec as P

F32 = jnp.float32
BF16 = jnp.bfloat16
W = 2048
CENTRE = (slice(48, 64), slice(15, 16))


def _halves(matrix):
    high = matrix.astype(ml_dtypes.bfloat16)
    low = (matrix - high.astype(np.float64)).astype(ml_dtypes.bfloat16)
    return high, low


def _thrice(matrix):
    high, low = _halves(matrix)
    return np.concatenate([high, high, low], axis=0)


def _tables():
    yh = (np.arange(32) + 0.5) / 32 - 0.5
    ya = (np.arange(64) + 0.5) / 64 - 0.5
    dh = (np.arange(8) - 3.5) / 128
    da = (np.arange(8) - 3.5) / 256
    shifts = [(k - 1.5) / 32 for k in range(4)]

    def whole(shift):
        up = np.exp(400.0 * dh[:, None] * yh[None])
        along = np.exp(400.0 * (da + shift)[:, None] * ya[None])
        return (up[:, None, :, None] * along[None, :, None, :]).reshape(64, W)

    cell = np.concatenate([np.exp(400.0 * ya[:, None] * (da + s)[None]) for s in shifts], axis=1)
    high, low = _halves(np.concatenate([cell.T, cell.T], axis=1))
    one = np.exp(400.0 * ya[:, None] * da[None])
    turned = _halves(np.concatenate([one.T, one.T], axis=1))
    turned = (turned[0],) + turned + (np.zeros_like(turned[0]),)
    order = np.zeros((8, 4, 8, 8, 4, 4, 8), ml_dtypes.bfloat16)
    for i, k, r in np.ndindex(8, 4, 8):
        order[i, k, i, r, :, k, r] = 1
    factors = [
        _thrice(np.tile(cell, (2, 4))),
        np.concatenate([high, high, low, np.zeros_like(low)], axis=0),
        order.reshape(2048, 128),
        _thrice(np.tile(one, (2, 16))),
        np.concatenate([np.concatenate([m, np.zeros((24, 128), m.dtype)], axis=0) for m in turned], axis=0),
    ]
    high, low = _halves(whole(0.0))
    wholes = _halves(np.concatenate([whole(s) for s in shifts], axis=0)) + (high, high, low, np.zeros_like(low))
    up = np.exp(400.0 * yh.reshape(16, 2, 1) * dh[None, None])
    of_row = np.repeat(up.transpose(0, 2, 1).reshape(128, 1, 2), 64, axis=2)
    ups = np.repeat(of_row, 8, axis=1).reshape(1024, 128)
    return np.concatenate(factors, axis=0), np.concatenate(wholes, axis=0), ups.astype(np.float32)


CELL, BACK, ORDER, ONE, ONE_BACK = 0, 384, 512, 2560, 2944


def dot(a, b):
    return jnp.dot(a, b, preferred_element_type=F32)


def split2(x):
    high = x.astype(BF16)
    return high, (x - high.astype(F32)).astype(BF16)


def split3(x):
    high = x.astype(BF16)
    rest = x - high.astype(F32)
    mid = rest.astype(BF16)
    return high, mid, (rest - mid.astype(F32)).astype(BF16)


def pick(onehot, x):
    o = onehot.astype(BF16)
    return dot(jnp.concatenate([o, o, o], axis=1), jnp.concatenate(split3(x), axis=0))


def targets(first, count):
    j = first + lax.broadcasted_iota(jnp.int32, (1, count), 1)
    yh = (lax.shift_right_logical(j, 6).astype(F32) + 0.5) / 32.0 - 0.5
    ya = (lax.bitwise_and(j, 63).astype(F32) + 0.5) / 64.0 - 0.5
    return yh, ya


def basic_centre(ids):
    row = jnp.floor(ids / 32.0)
    return (row * 8.0 + 4.0) / 128.0 - 0.5, ((ids - row * 32.0) * 8.0 + 4.0) / 256.0 - 0.5


def cell_centre(cells):
    row = jnp.floor(cells / 8.0)
    return (row * 8.0 + 4.0) / 128.0 - 0.5, ((cells - row * 8.0) * 32.0 + 16.0) / 256.0 - 0.5


def tilt(centre, y):
    return (400.0 * centre[0]) * y[0] + (400.0 * centre[1]) * y[1]


def eye_mask():
    return lax.broadcasted_iota(jnp.int32, (128, 128), 0) == lax.broadcasted_iota(jnp.int32, (128, 128), 1)


def to_col(row):
    return jnp.sum(jnp.where(eye_mask(), jnp.broadcast_to(row, (128, 128)), 0.0), axis=1, keepdims=True)


def to_row(col):
    return jnp.sum(jnp.where(eye_mask(), jnp.broadcast_to(col, (128, 128)), 0.0), axis=0, keepdims=True)


def local_cells(placement_row, core):
    dst = lax.broadcasted_iota(jnp.int32, (128, 128), 0)
    src = lax.broadcasted_iota(jnp.int32, (128, 128), 1)
    side = lax.bitwise_xor(lax.shift_right_logical(dst, 6), core)
    slot = lax.bitwise_and(lax.shift_right_logical(dst, 4), 3) * 32 + side * 16 + lax.bitwise_and(dst, 15)
    col = jnp.sum(jnp.where(slot == src, jnp.broadcast_to(placement_row, (128, 128)), 0.0), axis=1, keepdims=True)
    return col, to_row(col)


def own_ids(member_rows, group):
    lane = lax.broadcasted_iota(jnp.int32, (16, 128), 1)
    sub = lax.broadcasted_iota(jnp.int32, (16, 128), 0)
    k = lax.shift_right_logical(sub, 2)
    rows = jnp.zeros((16, 128), F32)
    for i in range(4):
        rows = jnp.where(k == i, jnp.broadcast_to(member_rows[i], (16, 128)), rows)
    return jnp.sum(jnp.where(lane == 4 * group + lax.bitwise_and(sub, 3), rows, 0.0), axis=1, keepdims=True)


def low_half(shape):
    return lax.broadcasted_iota(jnp.int32, shape, 1) < 64


def swap(x):
    return pltpu.roll(x, 64, 1)


def doubled(x, upper):
    mask = low_half(x.shape)
    return jnp.where(mask, swap(x), x) if upper else jnp.where(mask, x, swap(x))


def thrice(x):
    high, low = split2(x)
    return jnp.concatenate([high, low, high], axis=1)


def up_of(up_ref, i):
    h = up_ref[8 * i : 8 * i + 8, :]
    return jnp.concatenate([h, h], axis=0)


def total(parts):
    while len(parts) > 1:
        parts = [parts[i] + parts[i + 1] for i in range(0, len(parts), 2)]
    return parts[0]


def cell_sums(u, factor_ref, up_ref, first=CELL):
    v = [None] * 8
    for t in range(16):
        part = u[:, 128 * t : 128 * t + 128]
        for i in range(8):
            term = part * up_of(up_ref, 8 * t + i)
            v[i] = term if t == 0 else v[i] + term
    return dot(thrice(jnp.concatenate(v, axis=0)), factor_ref[first : first + 384, :])


def cell_back(e, factor_ref, up_ref, first=BACK):
    high = e.astype(BF16).astype(F32)
    lane = lax.broadcasted_iota(jnp.int32, e.shape, 1)
    x = jnp.where(lax.shift_right_logical(lane, 5) == 1, e - high, high).astype(BF16)
    z = dot(x, factor_ref[first : first + 128, :])
    z = [z[16 * i : 16 * i + 16] for i in range(8)]
    return jnp.concatenate(
        [total([z[i] * up_of(up_ref, 8 * t + i) for i in range(8)]) for t in range(16)], axis=1)


def ordered(mass, factor_ref):
    x = jnp.concatenate(split3(mass), axis=0)
    out = []
    for i in range(8):
        p = dot(x, factor_ref[ORDER + 256 * i : ORDER + 256 * i + 256, :])
        out.append((p[:16] + p[16:32]) + p[32:])
    return jnp.concatenate(out, axis=0)


def spread(e):
    row = lax.bitwise_and(lax.shift_right_logical(lax.broadcasted_iota(jnp.int32, (16, 128), 1), 3), 7)
    out = e[:16]
    for i in range(1, 8):
        out = jnp.where(row == i, e[16 * i : 16 * i + 16], out)
    return out


def wide(e):
    high = e.astype(BF16).astype(F32)
    return jnp.concatenate([jnp.where(low_half(e.shape), high, e - high), high], axis=1).astype(BF16)


def cell_cols(e, whole):
    n = e.shape[0] // 2
    p = dot(e, whole[:256])
    return p[:n] + p[n:] + dot(e[:n], whole[256:512])


def basic_cols(e, whole):
    return dot(e, whole[512:])


def nearness(centre, y):
    return jnp.exp(-200.0 * ((centre[0] - y[0]) ** 2 + (centre[1] - y[1]) ** 2))


def balanced(mass, s):
    return mass * (jnp.concatenate([s[CENTRE]] * 8, axis=0) / s)


def sweep_a(log_b, mass, d, factor_ref, up_ref, beside):
    b = jnp.exp(log_b - jnp.max(log_b, axis=1, keepdims=True))
    for i in range(3):
        beside(i)
        u = b / d
        s = cell_sums(u, factor_ref, up_ref)
        d = cell_back(balanced(mass, s), factor_ref, up_ref)
    return u, s[CENTRE], d


def over_k(x, op):
    y = op(x[:8], x[8:])
    return op(y, pltpu.roll(y, 4, 0))


def twice(x):
    return jnp.concatenate([x, x], axis=0)


def column_part(r, top, d):
    q = r - top
    peak = over_k(q, jnp.maximum)
    return peak + jnp.log(over_k(jnp.exp(q - twice(peak)) * d, jnp.add))


def sweep_b(log_b, mass, r, part, factor_ref, up_ref, beside):
    for i in range(3):
        beside(5 + i)
        v = r + twice(log_b - part)
        top = jnp.max(v, axis=1, keepdims=True)
        e = mass / cell_sums(jnp.exp(v - top), factor_ref, up_ref, ONE)
        if i < 2:
            part = column_part(r, top, cell_back(e, factor_ref, up_ref, ONE_BACK))
    return e, top


def solve_pair(log_b_a, mass_a, mass_b, ids, d, part, factor_ref, up_ref, send_ref, beside=lambda i: None):
    y = targets(0, W)
    at_cell = cell_centre(jnp.floor(ids / 4.0))
    at_basic = basic_centre(ids)
    shift = (400.0 * (at_basic[1] - at_cell[1])) * y[1]
    u, centre, d_a = sweep_a(log_b_a, mass_a, d, factor_ref, up_ref, beside)
    s = cell_sums(u * jnp.exp(shift), factor_ref, up_ref, ONE)
    e_first = mass_b * (jnp.concatenate([centre] * 8, axis=0) / s)
    beside(3)
    d_first = cell_back(e_first, factor_ref, up_ref, ONE_BACK)
    v = log_b_a - jnp.log(d_a) + shift
    peak = over_k(v, jnp.maximum)
    beside(4)
    log_b_b = peak + jnp.log(over_k(jnp.exp(v - twice(peak)) * d_first, jnp.add))
    e_second, top = sweep_b(log_b_b, mass_b, tilt(at_basic, y), part, factor_ref, up_ref, beside)
    rows = jnp.where(low_half((16, 128)), spread(e_first), jnp.log(spread(e_second)) - top)
    for i in range(32):
        send_ref[i, :, :] = rows


def member_rows_of(members_ref):
    members = members_ref[...].astype(F32)
    return [members[k : k + 1, :] for k in range(4)]


def exchange_ids(member_rows):
    members = [to_col(row) for row in member_rows]
    slot = lax.broadcasted_iota(jnp.int32, (128, 128), 0)
    lane = lax.broadcasted_iota(jnp.int32, (128, 128), 1)
    k = lax.bitwise_and(lax.shift_right_logical(lane, 2), 3)
    value = jnp.broadcast_to(members[0], (128, 128))
    for i in range(1, 4):
        value = jnp.where(k == i, jnp.broadcast_to(members[i], (128, 128)), value)
    of_lane = 4 * lax.shift_right_logical(lane, 4) + lax.bitwise_and(lane, 3)
    return jnp.concatenate(
        [jnp.sum(jnp.where(slot == of_lane + 32 * t, value, 0.0), axis=0, keepdims=True) for t in range(4)], axis=1)


def near_cells(want, member_rows, cell_row, exchanged, cells_ref, groups_ref, rows_ref, ids_ref):
    hits = [jnp.where(row == want, 1.0, 0.0) for row in member_rows]
    slot = (hits[0] + hits[1]) + (hits[2] + hits[3])
    ids = jnp.concatenate([jnp.sum(slot * row, axis=1, keepdims=True) for row in member_rows], axis=0)
    cell = jnp.floor(ids / 4.0)
    cells = jnp.where(cell_row == cell, 1.0, 0.0)
    cells_ref[...] = cells.astype(BF16)
    for k in range(4):
        groups_ref[256 * k : 256 * k + 256, :] = jnp.where(exchanged == 4.0 * cell + float(k), 1.0, 0.0).astype(BF16)
    ids = jnp.concatenate([ids, want], axis=0)
    rows_ref[...] = jnp.where(exchanged == ids, 1.0, 0.0).astype(BF16)
    ids_ref[...] = jnp.broadcast_to(ids, (320, 128))
    return ids, cells


def start_kernel(place_ref, placement_hbm, members_hbm, factor_hbm, up_hbm, sum_a_ref, sum_b_ref, factor_ref, up_ref, own_ids_ref, onehot_ref,
                 cell_ref, cells_ref, groups_ref, rows_ref, ids_ref, placement_ref, members_ref, sems):
    pairs = [(placement_hbm, placement_ref), (members_hbm, members_ref), (up_hbm, up_ref)]
    pairs += [(factor_hbm.at[at, :], factor_ref.at[at, :]) for at in (pl.ds(0, ORDER), pl.ds(ONE, 512), pl.ds(ORDER, ONE - ORDER))]
    copies = [pltpu.make_async_copy(*pair, sems.at[i]) for i, pair in enumerate(pairs)]
    for copy in copies:
        copy.start()
    for copy in copies[:2]:
        copy.wait()
    cell_col, cell_row = local_cells(placement_ref[...].astype(F32), place_ref[0])
    member_rows = member_rows_of(members_ref)
    ids = own_ids(member_rows, place_ref[1])
    own_ids_ref[...] = jnp.broadcast_to(ids, (16, 128))
    cells = jnp.floor(ids / 4.0)
    onehot_ref[...] = jnp.where(cell_row == cells, 1.0, 0.0)
    cell_ref[...] = jnp.broadcast_to(cell_col, (128, 128))
    want = jnp.concatenate([4.0 * cells + float(k) for k in range(4)], axis=0)
    near_cells(want, member_rows, cell_row, exchange_ids(member_rows), cells_ref, groups_ref, rows_ref, ids_ref)
    for copy in copies[2:5]:
        copy.wait()
    y = targets(0, W)
    sum_a_ref[...] = cell_sums(nearness(cell_centre(jnp.floor(ids / 4.0)), y), factor_ref, up_ref)
    sum_b_ref[...] = cell_sums(nearness(basic_centre(ids), y), factor_ref, up_ref, ONE)
    copies[5].wait()


def first_kernel(place_ref, own_ref, other_ref, sum_a_ref, sum_b_ref, ids_ref, onehot_ref, cell_ref, cells_ref, near_ref,
                 factor_ref, up_ref, whole_hbm, send_ref, here_ref, level_ref, mass_a_ref, mass_b_ref, d_ref, part_ref, whole_ref, table_ref, sems):
    copy = pltpu.make_async_copy(whole_hbm, whole_ref, sems.at[0])
    copy.start()
    ids, onehot = ids_ref[:, :1], onehot_ref[...]
    mass = []
    for part in (16, 17):
        at = pl.ds(part, 64, stride=18)
        rows = jnp.concatenate([own_ref[at, :], other_ref[at, :]], axis=0)
        mass.append(pick(onehot, rows))
    mass = jnp.concatenate(mass, axis=1)
    mass_a = ordered(mass, factor_ref)
    k = ids - 4.0 * jnp.floor(ids / 4.0)
    lane_k = lax.bitwise_and(lax.shift_right_logical(lax.broadcasted_iota(jnp.int32, (128, 128), 1), 3), 3).astype(F32)
    mass_b = jnp.where(lane_k == jnp.concatenate([k] * 8, axis=0), mass_a, 0.0)
    mass_b = mass_b + pltpu.roll(mass_b, 8, 1)
    mass_b = mass_b + pltpu.roll(mass_b, 16, 1)
    d = cell_back(balanced(mass_a, sum_a_ref[...]), factor_ref, up_ref)
    log_b = []
    for t in range(16):
        starts = [18 * (16 * x + t) for x in range(4)]
        rows = [ref[i : i + 16, :] for ref in (own_ref, other_ref) for i in starts]
        rows = jnp.concatenate(rows, axis=0)
        table_ref[:, 128 * t : 128 * t + 128] = rows
        log_b.append(pick(onehot, rows))
    here_ref[...] = table_ref[:, pl.ds(pl.multiple_of(place_ref[2] * 128, 128), 128)]
    log_b = jnp.concatenate(log_b, axis=1)
    at_basic = basic_centre(ids)
    top = 200.0 * (at_basic[0] * at_basic[0] + at_basic[1] * at_basic[1])
    part = column_part(tilt(at_basic, targets(0, W)), top, cell_back(mass_b / sum_b_ref[...], factor_ref, up_ref, ONE_BACK))
    mass_a_ref[...] = mass_a
    mass_b_ref[...] = mass_b
    d_ref[...] = d
    part_ref[...] = part
    near, cell_col = near_ref[0:256, :1], cell_ref[:, :1]

    def level(block):
        at = slice(256 * block, 256 * block + 256)
        level_ref[:, at] = near_level(near, cells_ref[...], table_ref[:, at], cell_col, targets(256 * block, 256))

    solve_pair(log_b, mass_a, mass_b, ids, d, part, factor_ref, up_ref, send_ref, lambda i: [level(b) for b in LEVELS[i]])
    copy.wait()


def received(recv_ref):
    return [jnp.concatenate([recv_ref[g, 4 * k : 4 * k + 4, :] for g in range(32)], axis=0) for k in range(4)]


def high_top(x):
    return jnp.max(jnp.where(low_half(x.shape), -jnp.inf, x), axis=1, keepdims=True)


def unpack(f):
    top = -high_top(f)
    return doubled(f, False), jnp.exp(doubled(f, True) + top), top


def a_rows(member_rows, cell_col, k):
    want = 4.0 * cell_col + float(k)
    return jnp.concatenate([jnp.where(row == want, 1.0, 0.0) for row in member_rows], axis=1).astype(BF16)


def packed(f):
    high, low = split2(f)
    return jnp.where(low_half(f.shape), high.astype(F32), swap(low.astype(F32))).astype(BF16)


def cell_halves(by_k):
    mask = low_half(by_k[0].shape)
    high = [jnp.where(mask, by_k[i], swap(by_k[i + 1])) for i in (0, 2)]
    low = [jnp.where(mask, swap(by_k[i]), by_k[i + 1]) for i in (0, 2)]
    return jnp.concatenate([jnp.concatenate(high, axis=1), jnp.concatenate(low, axis=1)], axis=0).astype(BF16)


def mix(v, d):
    peak = jnp.maximum(jnp.maximum(v[0], v[1]), jnp.maximum(v[2], v[3]))
    z = [jnp.exp(a - peak) * b for a, b in zip(v, d)]
    return peak + jnp.log((z[0] + z[1]) + (z[2] + z[3]))


def near_level(ids, cells, log_b, cell_col, y):
    return pick(cells, log_b - tilt(cell_centre(cell_col), y)) + tilt(basic_centre(ids), y)


def gathered(recv_ref, groups_ref, rows_ref):
    f = recv_ref[...].reshape(512, 128)
    o = rows_ref[...]
    high, mid, low = split3(f)
    three = dot(o, jnp.concatenate([high, mid, low], axis=1))
    e0, e1, top = unpack((three[:, :128] + three[:, 128:256]) + three[:, 256:])
    by_k = dot(groups_ref[...], packed(f))
    by_k = [by_k[256 * k : 256 * k + 256] for k in range(4)]
    return cell_halves(by_k), wide(e0[:256]), wide(e1), top


def near_margins(gather, level, centre, y, whole):
    e_cell, e0, e1, top = gather
    parts = [slice(64 * k, 64 * k + 64) for k in range(4)]
    v = level - jnp.log(cell_cols(e_cell, whole))
    d0 = basic_cols(e0, whole)
    d1 = basic_cols(e1, whole)
    q = tilt(centre, y) - top
    log_b = mix([v[a] for a in parts], [d0[a] for a in parts])
    gamma = log_b - mix([q[a] for a in parts], [d1[a] for a in parts])
    return gamma + q[256:], d1[256:]


def second_kernel(place_ref, own_ids_ref, recv_ref, level_ref, groups_ref, rows_ref, ids_ref, mass_a_ref, mass_b_ref, d_ref,
                  part_ref, factor_ref, up_ref, whole_ref, send_ref, here_ref):
    here_ref[...] = whole_ref[:, pl.ds(pl.multiple_of(place_ref[2] * 128, 128), 128)]
    gather = gathered(recv_ref, groups_ref, rows_ref)
    centre = basic_centre(ids_ref[:, :1])
    log_b = []
    for block in range(8):
        at = slice(block * 256, block * 256 + 256)
        v, d = near_margins(gather, level_ref[:, at], centre, targets(256 * block, 256), whole_ref[:, at])
        log_b.append(mix([v[16 * k : 16 * k + 16] for k in range(4)], [d[16 * k : 16 * k + 16] for k in range(4)]))
    solve_pair(jnp.concatenate(log_b, axis=1), mass_a_ref[...], mass_b_ref[...], own_ids_ref[:, :1], d_ref[...], part_ref[...],
               factor_ref, up_ref, send_ref)


def middle_kernel(place_ref, placement_ref, members_ref, log_b_ref, recv_ref, whole_ref, level_ref, cells_ref, groups_ref,
                  rows_ref, ids_ref):
    cell_col, cell_row = local_cells(placement_ref[...].astype(F32), place_ref[0])
    member_rows = member_rows_of(members_ref)
    share = place_ref[2]
    y = targets(share * 128, 128)
    whole = whole_ref[...]
    b_ids = [to_col(row) for row in member_rows]
    b_cell = jnp.concatenate([jnp.where(cell_row == jnp.floor(i / 4.0), 1.0, 0.0) for i in b_ids], axis=0)
    b_tilt = [tilt(basic_centre(i), y) for i in b_ids]
    a_tilt = [tilt(basic_centre(4.0 * cell_col + float(k)), y) for k in range(4)]
    parts = [slice(128 * k, 128 * k + 128) for k in range(4)]
    every = jnp.concatenate(received(recv_ref), axis=0)
    hits = [a_rows(member_rows, cell_col, k) for k in range(4)]
    rows = packed(every)
    e_cell = cell_halves([dot(h, rows) for h in hits])
    by_k = jnp.concatenate([pick(h, every) for h in hits], axis=0)
    gamma = pick(b_cell, log_b_ref[...] - jnp.log(cell_cols(e_cell, whole)) - tilt(cell_centre(cell_col), y))
    e0, e1, top = unpack(every)
    _, ea, a_top = unpack(by_k)
    d0, d1, da = [basic_cols(wide(e), whole) for e in (e0, e1, ea)]
    log_b1 = mix([gamma[a] + t for a, t in zip(parts, b_tilt)], [d0[a] for a in parts])
    gamma1 = log_b1 - mix([t - top[a] for a, t in zip(parts, b_tilt)], [d1[a] for a in parts])
    log_b = []
    for k in range(4):
        hit = hits[k].astype(F32)
        slot = (hit[:, :128] + hit[:, 128:256]) + (hit[:, 256:384] + hit[:, 384:])
        log_b.append(pick(slot, gamma1) + a_tilt[k] - a_top[parts[k]])
    log_b = mix(log_b, [da[a] for a in parts])
    lane = lax.broadcasted_iota(jnp.int32, (16, 128), 1)
    first = place_ref[3] * 16 + lax.broadcasted_iota(jnp.int32, (16, 128), 0)
    own_cells = jnp.sum(jnp.where(lane == first, jnp.broadcast_to(cell_row, (16, 128)), 0.0), axis=1, keepdims=True)
    want = jnp.concatenate([4.0 * own_cells + float(k) for k in range(4)], axis=0)
    ids, cells = near_cells(want, member_rows, cell_row, exchange_ids(member_rows), cells_ref, groups_ref, rows_ref, ids_ref)
    level_ref[...] = near_level(ids[:256], cells, log_b, cell_col, y)


def last_kernel(place_ref, recv_ref, level_ref, groups_ref, rows_ref, ids_ref, whole_ref, out_ref):
    centre = basic_centre(ids_ref[:, :1])
    v, d = near_margins(gathered(recv_ref, groups_ref, rows_ref), level_ref[...], centre,
                        targets(place_ref[2] * 128, 128), whole_ref[...])
    out = jnp.exp(v + jnp.log(d))
    for k in range(4):
        out_ref[:, k, :] = out[16 * k : 16 * k + 16]


def call(body, inputs, outs, scratch=(), work=1, far=0):
    near = len(inputs) - far
    inputs = inputs[:near] + tuple(pltpu.with_memory_space_constraint(v, pltpu.HBM) for v in inputs[near:])

    def spec(value):
        return pl.BlockSpec(memory_space=pltpu.SMEM if value.shape == (4,) else pltpu.VMEM)

    return pl.pallas_call(
        body,
        out_shape=[jax.ShapeDtypeStruct(s[:-1], BF16) if s[-1] is BF16 else jax.ShapeDtypeStruct(s, F32) for s in outs],
        in_specs=[spec(value) for value in inputs[:near]] + [pl.BlockSpec(memory_space=pltpu.HBM)] * far,
        out_specs=[pl.BlockSpec(memory_space=pltpu.VMEM)] * len(outs),
        scratch_shapes=list(scratch),
        compiler_params=pltpu.CompilerParams(vmem_limit_bytes=24 * 2**20),
        cost_estimate=pl.CostEstimate(flops=work * 10**9, bytes_accessed=10**6, transcendentals=0),
    )(*inputs)


LEVELS = ((0, 1), (2, 3), (4, 5), (6,), (7,), (), (), ())
FACTORS = [(3072, 128, BF16), (1024, 128)]
NEAR = [(256, 128, BF16), (1024, 512, BF16), (320, 512, BF16), (320, 128)]


def on_device(placement_a, members_b, source_mass, init_log, factors, wholes, ups):
    x, c, z, y = (lax.axis_index(name) for name in ("x", "c", "z", "y"))
    share = z * 4 + y
    place = jnp.stack([c, x * 8 + c * 4 + y, share, x]).astype(jnp.int32)
    index = (place, placement_a.reshape(1, 128), members_b.T)
    v = [init_log[:, k, :] for k in range(4)]
    peak = jnp.maximum(jnp.maximum(v[0], v[1]), jnp.maximum(v[2], v[3]))
    e = [jnp.exp(a - peak) for a in v]
    log_b = peak + jnp.log((e[0] + e[1]) + (e[2] + e[3])) + float(np.log(64.0 / W))
    mass = lax.dynamic_slice_in_dim(source_mass, share, 1, 0).reshape(2, 128)
    block = jnp.concatenate([log_b, mass], axis=0).reshape(9, 2, 128)
    own = lax.all_to_all(jnp.broadcast_to(block[None], (64, 9, 2, 128)), ("x", "z", "y"), 0, 0, tiled=True)
    sum_a, sum_b, factors, ups, held, onehot, cell, cells, groups, rows, ids = call(
        start_kernel, index + (factors, ups), [(128, 128), (128, 128)] + FACTORS + [(16, 128), (16, 128), (128, 128)] + NEAR,
        [pltpu.VMEM((1, 128), jnp.int32), pltpu.VMEM((4, 128), jnp.int32), pltpu.SemaphoreType.DMA((6,))], far=4)
    other = lax.ppermute(own, "c", [(0, 1), (1, 0)]).reshape(1152, 128)
    own = own.reshape(1152, 128)

    def exchange(rows):
        return lax.all_to_all(rows, ("x", "c", "y"), 0, 0, tiled=True)

    send, here, level, *rest, wholes = call(
        first_kernel, (place, own, other, sum_a, sum_b, held, onehot, cell, cells, ids, factors, ups, wholes),
        [(32, 16, 128), (128, 128), (256, W), (128, 128), (128, 128), (16, W), (8, W), (768, W, BF16)],
        [pltpu.VMEM((128, W), F32), pltpu.SemaphoreType.DMA((1,))], far=1)
    first = exchange(send)
    send, whole = call(second_kernel, (place, held, first, level, groups, rows, ids, *rest, factors, ups, wholes),
                       [(32, 16, 128), (768, 128, BF16)])
    second = exchange(send)
    level, _, groups, rows, ids = call(middle_kernel, index + (here, first, whole), [(256, 128)] + NEAR)
    (out,) = call(last_kernel, (place, second, level, groups, rows, ids, whole), [(16, 4, 128)])
    return out


def solution(mesh):
    split = Mesh(mesh.devices.reshape(4, 2, 4, 4), ("x", "c", "z", "y"))
    tables = _tables()
    placed = (P(), P(), P(("x", "c"), None), P(("x", "c"), None, ("z", "y"))) + (P(),) * len(tables)
    body = jax.shard_map(
        on_device, mesh=split, in_specs=placed, out_specs=P(("x", "c"), None, ("z", "y")), check_vma=False
    )

    def run(placement_a, members_b, source_mass, init_log):
        return body(placement_a, members_b, source_mass, init_log, *(jnp.asarray(t) for t in tables))

    return run
```

```python
import numpy as np
import ml_dtypes

import jax
import jax.numpy as jnp
from jax import lax
from jax.experimental import pallas as pl
from jax.experimental.pallas import tpu as pltpu
from jax.sharding import Mesh, PartitionSpec as P

F32 = jnp.float32
BF16 = jnp.bfloat16
W = 2048
CENTRE = (slice(48, 64), slice(15, 16))


def _halves(matrix):
    high = matrix.astype(ml_dtypes.bfloat16)
    low = (matrix - high.astype(np.float64)).astype(ml_dtypes.bfloat16)
    return high, low


def _thrice(matrix):
    high, low = _halves(matrix)
    return np.concatenate([high, high, low], axis=0)


def _tables():
    yh = (np.arange(32) + 0.5) / 32 - 0.5
    ya = (np.arange(64) + 0.5) / 64 - 0.5
    dh = (np.arange(8) - 3.5) / 128
    da = (np.arange(8) - 3.5) / 256
    shifts = [(k - 1.5) / 32 for k in range(4)]

    def whole(shift):
        up = np.exp(400.0 * dh[:, None] * yh[None])
        along = np.exp(400.0 * (da + shift)[:, None] * ya[None])
        return (up[:, None, :, None] * along[None, :, None, :]).reshape(64, W)

    cell = np.concatenate([np.exp(400.0 * ya[:, None] * (da + s)[None]) for s in shifts], axis=1)
    high, low = _halves(np.concatenate([cell.T, cell.T], axis=1))
    one = np.exp(400.0 * ya[:, None] * da[None])
    turned = _halves(np.concatenate([one.T, one.T], axis=1))
    turned = (turned[0],) + turned + (np.zeros_like(turned[0]),)
    order = np.zeros((8, 4, 8, 8, 4, 4, 8), ml_dtypes.bfloat16)
    for i, k, r in np.ndindex(8, 4, 8):
        order[i, k, i, r, :, k, r] = 1
    factors = [
        _thrice(np.tile(cell, (2, 4))),
        np.concatenate([high, high, low, np.zeros_like(low)], axis=0),
        order.reshape(2048, 128),
        _thrice(np.tile(one, (2, 16))),
        np.concatenate([np.concatenate([m, np.zeros((24, 128), m.dtype)], axis=0) for m in turned], axis=0),
    ]
    high, low = _halves(whole(0.0))
    wholes = _halves(np.concatenate([whole(s) for s in shifts], axis=0)) + (high, high, low, np.zeros_like(low))
    up = np.exp(400.0 * yh.reshape(16, 2, 1) * dh[None, None])
    of_row = np.repeat(up.transpose(0, 2, 1).reshape(128, 1, 2), 64, axis=2)
    ups = np.repeat(of_row, 8, axis=1).reshape(1024, 128)
    return np.concatenate(factors, axis=0), np.concatenate(wholes, axis=0), ups.astype(np.float32)


CELL, BACK, ORDER, ONE, ONE_BACK = 0, 384, 512, 2560, 2944


def dot(a, b):
    return jnp.dot(a, b, preferred_element_type=F32)


def split2(x):
    high = x.astype(BF16)
    return high, (x - high.astype(F32)).astype(BF16)


def split3(x):
    high = x.astype(BF16)
    rest = x - high.astype(F32)
    mid = rest.astype(BF16)
    return high, mid, (rest - mid.astype(F32)).astype(BF16)


def pick(onehot, x):
    o = onehot.astype(BF16)
    return dot(jnp.concatenate([o, o, o], axis=1), jnp.concatenate(split3(x), axis=0))


def targets(first, count):
    j = first + lax.broadcasted_iota(jnp.int32, (1, count), 1)
    yh = (lax.shift_right_logical(j, 6).astype(F32) + 0.5) / 32.0 - 0.5
    ya = (lax.bitwise_and(j, 63).astype(F32) + 0.5) / 64.0 - 0.5
    return yh, ya


def basic_centre(ids):
    row = jnp.floor(ids / 32.0)
    return (row * 8.0 + 4.0) / 128.0 - 0.5, ((ids - row * 32.0) * 8.0 + 4.0) / 256.0 - 0.5


def cell_centre(cells):
    row = jnp.floor(cells / 8.0)
    return (row * 8.0 + 4.0) / 128.0 - 0.5, ((cells - row * 8.0) * 32.0 + 16.0) / 256.0 - 0.5


def tilt(centre, y):
    return (400.0 * centre[0]) * y[0] + (400.0 * centre[1]) * y[1]


def eye_mask():
    return lax.broadcasted_iota(jnp.int32, (128, 128), 0) == lax.broadcasted_iota(jnp.int32, (128, 128), 1)


def to_col(row):
    return jnp.sum(jnp.where(eye_mask(), jnp.broadcast_to(row, (128, 128)), 0.0), axis=1, keepdims=True)


def to_row(col):
    return jnp.sum(jnp.where(eye_mask(), jnp.broadcast_to(col, (128, 128)), 0.0), axis=0, keepdims=True)


def local_cells(placement_row, core):
    dst = lax.broadcasted_iota(jnp.int32, (128, 128), 0)
    src = lax.broadcasted_iota(jnp.int32, (128, 128), 1)
    side = lax.bitwise_xor(lax.shift_right_logical(dst, 6), core)
    slot = lax.bitwise_and(lax.shift_right_logical(dst, 4), 3) * 32 + side * 16 + lax.bitwise_and(dst, 15)
    col = jnp.sum(jnp.where(slot == src, jnp.broadcast_to(placement_row, (128, 128)), 0.0), axis=1, keepdims=True)
    return col, to_row(col)


def own_ids(member_rows, group):
    lane = lax.broadcasted_iota(jnp.int32, (16, 128), 1)
    sub = lax.broadcasted_iota(jnp.int32, (16, 128), 0)
    k = lax.shift_right_logical(sub, 2)
    rows = jnp.zeros((16, 128), F32)
    for i in range(4):
        rows = jnp.where(k == i, jnp.broadcast_to(member_rows[i], (16, 128)), rows)
    return jnp.sum(jnp.where(lane == 4 * group + lax.bitwise_and(sub, 3), rows, 0.0), axis=1, keepdims=True)


def low_half(shape):
    return lax.broadcasted_iota(jnp.int32, shape, 1) < 64


def swap(x):
    return pltpu.roll(x, 64, 1)


def doubled(x, upper):
    mask = low_half(x.shape)
    return jnp.where(mask, swap(x), x) if upper else jnp.where(mask, x, swap(x))


def thrice(x):
    high, low = split2(x)
    return jnp.concatenate([high, low, high], axis=1)


def up_of(up_ref, i):
    h = up_ref[8 * i : 8 * i + 8, :]
    return jnp.concatenate([h, h], axis=0)


def total(parts):
    while len(parts) > 1:
        parts = [parts[i] + parts[i + 1] for i in range(0, len(parts), 2)]
    return parts[0]


def cell_sums(u, factor_ref, up_ref, first=CELL):
    v = [None] * 8
    for t in range(16):
        part = u[:, 128 * t : 128 * t + 128]
        for i in range(8):
            term = part * up_of(up_ref, 8 * t + i)
            v[i] = term if t == 0 else v[i] + term
    return dot(thrice(jnp.concatenate(v, axis=0)), factor_ref[first : first + 384, :])


def cell_back(e, factor_ref, up_ref, first=BACK):
    high = e.astype(BF16).astype(F32)
    lane = lax.broadcasted_iota(jnp.int32, e.shape, 1)
    x = jnp.where(lax.shift_right_logical(lane, 5) == 1, e - high, high).astype(BF16)
    z = dot(x, factor_ref[first : first + 128, :])
    z = [z[16 * i : 16 * i + 16] for i in range(8)]
    return jnp.concatenate(
        [total([z[i] * up_of(up_ref, 8 * t + i) for i in range(8)]) for t in range(16)], axis=1)


def ordered(mass, factor_ref):
    x = jnp.concatenate(split3(mass), axis=0)
    out = []
    for i in range(8):
        p = dot(x, factor_ref[ORDER + 256 * i : ORDER + 256 * i + 256, :])
        out.append((p[:16] + p[16:32]) + p[32:])
    return jnp.concatenate(out, axis=0)


def spread(e):
    row = lax.bitwise_and(lax.shift_right_logical(lax.broadcasted_iota(jnp.int32, (16, 128), 1), 3), 7)
    out = e[:16]
    for i in range(1, 8):
        out = jnp.where(row == i, e[16 * i : 16 * i + 16], out)
    return out


def wide(e):
    high = e.astype(BF16).astype(F32)
    return jnp.concatenate([jnp.where(low_half(e.shape), high, e - high), high], axis=1).astype(BF16)


def cell_cols(e, whole):
    n = e.shape[0] // 2
    p = dot(e, whole[:256])
    return p[:n] + p[n:] + dot(e[:n], whole[256:512])


def basic_cols(e, whole):
    return dot(e, whole[512:])


def nearness(centre, y):
    return jnp.exp(-200.0 * ((centre[0] - y[0]) ** 2 + (centre[1] - y[1]) ** 2))


def balanced(mass, s):
    return mass * (jnp.concatenate([s[CENTRE]] * 8, axis=0) / s)


def sweep_a(log_b, mass, d, factor_ref, up_ref, beside):
    b = jnp.exp(log_b - jnp.max(log_b, axis=1, keepdims=True))
    for i in range(3):
        beside(i)
        u = b / d
        s = cell_sums(u, factor_ref, up_ref)
        d = cell_back(balanced(mass, s), factor_ref, up_ref)
    return u, s[CENTRE], d


def over_k(x, op):
    y = op(x[:8], x[8:])
    return op(y, pltpu.roll(y, 4, 0))


def twice(x):
    return jnp.concatenate([x, x], axis=0)


def column_part(r, top, d):
    q = r - top
    peak = over_k(q, jnp.maximum)
    return peak + jnp.log(over_k(jnp.exp(q - twice(peak)) * d, jnp.add))


def sweep_b(log_b, mass, r, part, factor_ref, up_ref, beside):
    for i in range(3):
        beside(5 + i)
        v = r + twice(log_b - part)
        top = jnp.max(v, axis=1, keepdims=True)
        e = mass / cell_sums(jnp.exp(v - top), factor_ref, up_ref, ONE)
        if i < 2:
            part = column_part(r, top, cell_back(e, factor_ref, up_ref, ONE_BACK))
    return e, top


def solve_pair(log_b_a, mass_a, mass_b, ids, d, part, factor_ref, up_ref, send_ref, beside=lambda i: None):
    y = targets(0, W)
    at_cell = cell_centre(jnp.floor(ids / 4.0))
    at_basic = basic_centre(ids)
    shift = (400.0 * (at_basic[1] - at_cell[1])) * y[1]
    u, centre, d_a = sweep_a(log_b_a, mass_a, d, factor_ref, up_ref, beside)
    s = cell_sums(u * jnp.exp(shift), factor_ref, up_ref, ONE)
    e_first = mass_b * (jnp.concatenate([centre] * 8, axis=0) / s)
    beside(3)
    d_first = cell_back(e_first, factor_ref, up_ref, ONE_BACK)
    v = log_b_a - jnp.log(d_a) + shift
    peak = over_k(v, jnp.maximum)
    beside(4)
    log_b_b = peak + jnp.log(over_k(jnp.exp(v - twice(peak)) * d_first, jnp.add))
    e_second, top = sweep_b(log_b_b, mass_b, tilt(at_basic, y), part, factor_ref, up_ref, beside)
    rows = jnp.where(low_half((16, 128)), spread(e_first), jnp.log(spread(e_second)) - top)
    for i in range(32):
        send_ref[i, :, :] = rows


def member_rows_of(members_ref):
    members = members_ref[...].astype(F32)
    return [members[k : k + 1, :] for k in range(4)]


def exchange_ids(member_rows):
    members = [to_col(row) for row in member_rows]
    slot = lax.broadcasted_iota(jnp.int32, (128, 128), 0)
    lane = lax.broadcasted_iota(jnp.int32, (128, 128), 1)
    k = lax.bitwise_and(lax.shift_right_logical(lane, 2), 3)
    value = jnp.broadcast_to(members[0], (128, 128))
    for i in range(1, 4):
        value = jnp.where(k == i, jnp.broadcast_to(members[i], (128, 128)), value)
    of_lane = 4 * lax.shift_right_logical(lane, 4) + lax.bitwise_and(lane, 3)
    return jnp.concatenate(
        [jnp.sum(jnp.where(slot == of_lane + 32 * t, value, 0.0), axis=0, keepdims=True) for t in range(4)], axis=1)


def near_cells(want, member_rows, cell_row, exchanged, cells_ref, groups_ref, rows_ref, ids_ref):
    hits = [jnp.where(row == want, 1.0, 0.0) for row in member_rows]
    slot = (hits[0] + hits[1]) + (hits[2] + hits[3])
    ids = jnp.concatenate([jnp.sum(slot * row, axis=1, keepdims=True) for row in member_rows], axis=0)
    cell = jnp.floor(ids / 4.0)
    cells = jnp.where(cell_row == cell, 1.0, 0.0)
    cells_ref[...] = cells.astype(BF16)
    for k in range(4):
        groups_ref[256 * k : 256 * k + 256, :] = jnp.where(exchanged == 4.0 * cell + float(k), 1.0, 0.0).astype(BF16)
    ids = jnp.concatenate([ids, want], axis=0)
    rows_ref[...] = jnp.where(exchanged == ids, 1.0, 0.0).astype(BF16)
    ids_ref[...] = jnp.broadcast_to(ids, (320, 128))
    return ids, cells


def start_kernel(place_ref, placement_hbm, members_hbm, factor_hbm, up_hbm, sum_a_ref, sum_b_ref, factor_ref, up_ref, own_ids_ref, onehot_ref,
                 cell_ref, cells_ref, groups_ref, rows_ref, ids_ref, placement_ref, members_ref, sems):
    pairs = [(placement_hbm, placement_ref), (members_hbm, members_ref), (up_hbm, up_ref)]
    pairs += [(factor_hbm.at[at, :], factor_ref.at[at, :]) for at in (pl.ds(0, ORDER), pl.ds(ONE, 512), pl.ds(ORDER, ONE - ORDER))]
    copies = [pltpu.make_async_copy(*pair, sems.at[i]) for i, pair in enumerate(pairs)]
    for copy in copies:
        copy.start()
    for copy in copies[:2]:
        copy.wait()
    cell_col, cell_row = local_cells(placement_ref[...].astype(F32), place_ref[0])
    member_rows = member_rows_of(members_ref)
    ids = own_ids(member_rows, place_ref[1])
    own_ids_ref[...] = jnp.broadcast_to(ids, (16, 128))
    cells = jnp.floor(ids / 4.0)
    onehot_ref[...] = jnp.where(cell_row == cells, 1.0, 0.0)
    cell_ref[...] = jnp.broadcast_to(cell_col, (128, 128))
    want = jnp.concatenate([4.0 * cells + float(k) for k in range(4)], axis=0)
    near_cells(want, member_rows, cell_row, exchange_ids(member_rows), cells_ref, groups_ref, rows_ref, ids_ref)
    for copy in copies[2:5]:
        copy.wait()
    y = targets(0, W)
    sum_a_ref[...] = cell_sums(nearness(cell_centre(jnp.floor(ids / 4.0)), y), factor_ref, up_ref)
    sum_b_ref[...] = cell_sums(nearness(basic_centre(ids), y), factor_ref, up_ref, ONE)
    copies[5].wait()


def first_kernel(place_ref, own_ref, other_ref, sum_a_ref, sum_b_ref, ids_ref, onehot_ref, cell_ref, cells_ref, near_ref,
                 factor_ref, up_ref, whole_hbm, send_ref, here_ref, level_ref, mass_a_ref, mass_b_ref, d_ref, part_ref, whole_ref, table_ref, sems):
    copy = pltpu.make_async_copy(whole_hbm, whole_ref, sems.at[0])
    copy.start()
    ids, onehot = ids_ref[:, :1], onehot_ref[...]
    mass = []
    for part in (16, 17):
        at = pl.ds(part, 64, stride=18)
        rows = jnp.concatenate([own_ref[at, :], other_ref[at, :]], axis=0)
        mass.append(pick(onehot, rows))
    mass = jnp.concatenate(mass, axis=1)
    mass_a = ordered(mass, factor_ref)
    k = ids - 4.0 * jnp.floor(ids / 4.0)
    lane_k = lax.bitwise_and(lax.shift_right_logical(lax.broadcasted_iota(jnp.int32, (128, 128), 1), 3), 3).astype(F32)
    mass_b = jnp.where(lane_k == jnp.concatenate([k] * 8, axis=0), mass_a, 0.0)
    mass_b = mass_b + pltpu.roll(mass_b, 8, 1)
    mass_b = mass_b + pltpu.roll(mass_b, 16, 1)
    d = cell_back(balanced(mass_a, sum_a_ref[...]), factor_ref, up_ref)
    log_b = []
    for t in range(16):
        starts = [18 * (16 * x + t) for x in range(4)]
        rows = [ref[i : i + 16, :] for ref in (own_ref, other_ref) for i in starts]
        rows = jnp.concatenate(rows, axis=0)
        table_ref[:, 128 * t : 128 * t + 128] = rows
        log_b.append(pick(onehot, rows))
    here_ref[...] = table_ref[:, pl.ds(pl.multiple_of(place_ref[2] * 128, 128), 128)]
    log_b = jnp.concatenate(log_b, axis=1)
    at_basic = basic_centre(ids)
    top = 200.0 * (at_basic[0] * at_basic[0] + at_basic[1] * at_basic[1])
    part = column_part(tilt(at_basic, targets(0, W)), top, cell_back(mass_b / sum_b_ref[...], factor_ref, up_ref, ONE_BACK))
    mass_a_ref[...] = mass_a
    mass_b_ref[...] = mass_b
    d_ref[...] = d
    part_ref[...] = part
    near, cell_col = near_ref[0:256, :1], cell_ref[:, :1]

    def level(block):
        at = slice(256 * block, 256 * block + 256)
        level_ref[:, at] = near_level(near, cells_ref[...], table_ref[:, at], cell_col, targets(256 * block, 256))

    solve_pair(log_b, mass_a, mass_b, ids, d, part, factor_ref, up_ref, send_ref, lambda i: [level(b) for b in LEVELS[i]])
    copy.wait()


def received(recv_ref):
    return [jnp.concatenate([recv_ref[g, 4 * k : 4 * k + 4, :] for g in range(32)], axis=0) for k in range(4)]


def high_top(x):
    return jnp.max(jnp.where(low_half(x.shape), -jnp.inf, x), axis=1, keepdims=True)


def unpack(f):
    top = -high_top(f)
    return doubled(f, False), jnp.exp(doubled(f, True) + top), top


def a_rows(member_rows, cell_col, k):
    want = 4.0 * cell_col + float(k)
    return jnp.concatenate([jnp.where(row == want, 1.0, 0.0) for row in member_rows], axis=1).astype(BF16)


def packed(f):
    high, low = split2(f)
    return jnp.where(low_half(f.shape), high.astype(F32), swap(low.astype(F32))).astype(BF16)


def cell_halves(by_k):
    mask = low_half(by_k[0].shape)
    high = [jnp.where(mask, by_k[i], swap(by_k[i + 1])) for i in (0, 2)]
    low = [jnp.where(mask, swap(by_k[i]), by_k[i + 1]) for i in (0, 2)]
    return jnp.concatenate([jnp.concatenate(high, axis=1), jnp.concatenate(low, axis=1)], axis=0).astype(BF16)


def mix(v, d):
    peak = jnp.maximum(jnp.maximum(v[0], v[1]), jnp.maximum(v[2], v[3]))
    z = [jnp.exp(a - peak) * b for a, b in zip(v, d)]
    return peak + jnp.log((z[0] + z[1]) + (z[2] + z[3]))


def near_level(ids, cells, log_b, cell_col, y):
    return pick(cells, log_b - tilt(cell_centre(cell_col), y)) + tilt(basic_centre(ids), y)


def gathered(recv_ref, groups_ref, rows_ref):
    f = recv_ref[...].reshape(512, 128)
    o = rows_ref[...]
    high, mid, low = split3(f)
    three = dot(o, jnp.concatenate([high, mid, low], axis=1))
    e0, e1, top = unpack((three[:, :128] + three[:, 128:256]) + three[:, 256:])
    by_k = dot(groups_ref[...], packed(f))
    by_k = [by_k[256 * k : 256 * k + 256] for k in range(4)]
    return cell_halves(by_k), wide(e0[:256]), wide(e1), top


def near_margins(gather, level, centre, y, whole):
    e_cell, e0, e1, top = gather
    parts = [slice(64 * k, 64 * k + 64) for k in range(4)]
    v = level - jnp.log(cell_cols(e_cell, whole))
    d0 = basic_cols(e0, whole)
    d1 = basic_cols(e1, whole)
    q = tilt(centre, y) - top
    log_b = mix([v[a] for a in parts], [d0[a] for a in parts])
    gamma = log_b - mix([q[a] for a in parts], [d1[a] for a in parts])
    return gamma + q[256:], d1[256:]


def second_kernel(place_ref, own_ids_ref, recv_ref, level_ref, groups_ref, rows_ref, ids_ref, mass_a_ref, mass_b_ref, d_ref,
                  part_ref, factor_ref, up_ref, whole_ref, send_ref, here_ref):
    here_ref[...] = whole_ref[:, pl.ds(pl.multiple_of(place_ref[2] * 128, 128), 128)]
    gather = gathered(recv_ref, groups_ref, rows_ref)
    centre = basic_centre(ids_ref[:, :1])
    log_b = []
    for block in range(8):
        at = slice(block * 256, block * 256 + 256)
        v, d = near_margins(gather, level_ref[:, at], centre, targets(256 * block, 256), whole_ref[:, at])
        log_b.append(mix([v[16 * k : 16 * k + 16] for k in range(4)], [d[16 * k : 16 * k + 16] for k in range(4)]))
    solve_pair(jnp.concatenate(log_b, axis=1), mass_a_ref[...], mass_b_ref[...], own_ids_ref[:, :1], d_ref[...], part_ref[...],
               factor_ref, up_ref, send_ref)


def middle_kernel(place_ref, placement_ref, members_ref, log_b_ref, recv_ref, whole_ref, level_ref, cells_ref, groups_ref,
                  rows_ref, ids_ref):
    cell_col, cell_row = local_cells(placement_ref[...].astype(F32), place_ref[0])
    member_rows = member_rows_of(members_ref)
    share = place_ref[2]
    y = targets(share * 128, 128)
    whole = whole_ref[...]
    b_ids = [to_col(row) for row in member_rows]
    b_cell = jnp.concatenate([jnp.where(cell_row == jnp.floor(i / 4.0), 1.0, 0.0) for i in b_ids], axis=0)
    b_tilt = [tilt(basic_centre(i), y) for i in b_ids]
    a_tilt = [tilt(basic_centre(4.0 * cell_col + float(k)), y) for k in range(4)]
    parts = [slice(128 * k, 128 * k + 128) for k in range(4)]
    every = jnp.concatenate(received(recv_ref), axis=0)
    hits = [a_rows(member_rows, cell_col, k) for k in range(4)]
    rows = packed(every)
    e_cell = cell_halves([dot(h, rows) for h in hits])
    by_k = jnp.concatenate([pick(h, every) for h in hits], axis=0)
    gamma = pick(b_cell, log_b_ref[...] - jnp.log(cell_cols(e_cell, whole)) - tilt(cell_centre(cell_col), y))
    e0, e1, top = unpack(every)
    _, ea, a_top = unpack(by_k)
    d0, d1, da = [basic_cols(wide(e), whole) for e in (e0, e1, ea)]
    log_b1 = mix([gamma[a] + t for a, t in zip(parts, b_tilt)], [d0[a] for a in parts])
    gamma1 = log_b1 - mix([t - top[a] for a, t in zip(parts, b_tilt)], [d1[a] for a in parts])
    log_b = []
    for k in range(4):
        hit = hits[k].astype(F32)
        slot = (hit[:, :128] + hit[:, 128:256]) + (hit[:, 256:384] + hit[:, 384:])
        log_b.append(pick(slot, gamma1) + a_tilt[k] - a_top[parts[k]])
    log_b = mix(log_b, [da[a] for a in parts])
    lane = lax.broadcasted_iota(jnp.int32, (16, 128), 1)
    first = place_ref[3] * 16 + lax.broadcasted_iota(jnp.int32, (16, 128), 0)
    own_cells = jnp.sum(jnp.where(lane == first, jnp.broadcast_to(cell_row, (16, 128)), 0.0), axis=1, keepdims=True)
    want = jnp.concatenate([4.0 * own_cells + float(k) for k in range(4)], axis=0)
    ids, cells = near_cells(want, member_rows, cell_row, exchange_ids(member_rows), cells_ref, groups_ref, rows_ref, ids_ref)
    level_ref[...] = near_level(ids[:256], cells, log_b, cell_col, y)


def last_kernel(place_ref, recv_ref, level_ref, groups_ref, rows_ref, ids_ref, whole_ref, out_ref):
    centre = basic_centre(ids_ref[:, :1])
    v, d = near_margins(gathered(recv_ref, groups_ref, rows_ref), level_ref[...], centre,
                        targets(place_ref[2] * 128, 128), whole_ref[...])
    out = jnp.exp(v) * d
    for k in range(4):
        out_ref[:, k, :] = out[16 * k : 16 * k + 16]


def call(body, inputs, outs, scratch=(), work=1, far=0):
    near = len(inputs) - far
    inputs = inputs[:near] + tuple(pltpu.with_memory_space_constraint(v, pltpu.HBM) for v in inputs[near:])

    def spec(value):
        return pl.BlockSpec(memory_space=pltpu.SMEM if value.shape == (4,) else pltpu.VMEM)

    return pl.pallas_call(
        body,
        out_shape=[jax.ShapeDtypeStruct(s[:-1], BF16) if s[-1] is BF16 else jax.ShapeDtypeStruct(s, F32) for s in outs],
        in_specs=[spec(value) for value in inputs[:near]] + [pl.BlockSpec(memory_space=pltpu.HBM)] * far,
        out_specs=[pl.BlockSpec(memory_space=pltpu.VMEM)] * len(outs),
        scratch_shapes=list(scratch),
        compiler_params=pltpu.CompilerParams(vmem_limit_bytes=24 * 2**20),
        cost_estimate=pl.CostEstimate(flops=work * 10**9, bytes_accessed=10**6, transcendentals=0),
    )(*inputs)


LEVELS = ((0, 1), (2, 3), (4, 5), (6,), (7,), (), (), ())
FACTORS = [(3072, 128, BF16), (1024, 128)]
NEAR = [(256, 128, BF16), (1024, 512, BF16), (320, 512, BF16), (320, 128)]


def on_device(placement_a, members_b, source_mass, init_log, factors, wholes, ups):
    x, c, z, y = (lax.axis_index(name) for name in ("x", "c", "z", "y"))
    share = z * 4 + y
    place = jnp.stack([c, x * 8 + c * 4 + y, share, x]).astype(jnp.int32)
    index = (place, placement_a.reshape(1, 128), members_b.T)
    v = [init_log[:, k, :] for k in range(4)]
    peak = jnp.maximum(jnp.maximum(v[0], v[1]), jnp.maximum(v[2], v[3]))
    e = [jnp.exp(a - peak) for a in v]
    log_b = peak + jnp.log((e[0] + e[1]) + (e[2] + e[3])) + float(np.log(64.0 / W))
    mass = lax.dynamic_slice_in_dim(source_mass, share, 1, 0).reshape(2, 128)
    block = jnp.concatenate([log_b, mass], axis=0).reshape(9, 2, 128)
    own = lax.all_to_all(jnp.broadcast_to(block[None], (64, 9, 2, 128)), ("x", "z", "y"), 0, 0, tiled=True)
    sum_a, sum_b, factors, ups, held, onehot, cell, cells, groups, rows, ids = call(
        start_kernel, index + (factors, ups), [(128, 128), (128, 128)] + FACTORS + [(16, 128), (16, 128), (128, 128)] + NEAR,
        [pltpu.VMEM((1, 128), jnp.int32), pltpu.VMEM((4, 128), jnp.int32), pltpu.SemaphoreType.DMA((6,))], far=4)
    other = lax.ppermute(own, "c", [(0, 1), (1, 0)]).reshape(1152, 128)
    own = own.reshape(1152, 128)

    def exchange(rows):
        return lax.all_to_all(rows, ("x", "c", "y"), 0, 0, tiled=True)

    send, here, level, *rest, wholes = call(
        first_kernel, (place, own, other, sum_a, sum_b, held, onehot, cell, cells, ids, factors, ups, wholes),
        [(32, 16, 128), (128, 128), (256, W), (128, 128), (128, 128), (16, W), (8, W), (768, W, BF16)],
        [pltpu.VMEM((128, W), F32), pltpu.SemaphoreType.DMA((1,))], far=1)
    first = exchange(send)
    send, whole = call(second_kernel, (place, held, first, level, groups, rows, ids, *rest, factors, ups, wholes),
                       [(32, 16, 128), (768, 128, BF16)])
    second = exchange(send)
    level, _, groups, rows, ids = call(middle_kernel, index + (here, first, whole), [(256, 128)] + NEAR)
    (out,) = call(last_kernel, (place, second, level, groups, rows, ids, whole), [(16, 4, 128)])
    return out


def solution(mesh):
    split = Mesh(mesh.devices.reshape(4, 2, 4, 4), ("x", "c", "z", "y"))
    tables = _tables()
    placed = (P(), P(), P(("x", "c"), None), P(("x", "c"), None, ("z", "y"))) + (P(),) * len(tables)
    body = jax.shard_map(
        on_device, mesh=split, in_specs=placed, out_specs=P(("x", "c"), None, ("z", "y")), check_vma=False
    )

    def run(placement_a, members_b, source_mass, init_log):
        return body(placement_a, members_b, source_mass, init_log, *(jnp.asarray(t) for t in tables))

    return run
```
